32 devices in a mesh: dp: 8 (over z, y), state: 4 (over x, core).
Axes of the slice: x: 2, y: 2, z: 4, core: 2. Of those that a mesh axis runs over, the one named last changes fastest.
Arguments:
- tokens: bfloat16 [2048, 2048], P('dp'), may hold values from -6 to 6
- norm_gain: float32 [2048], replicated, may hold values from 0.5 to 1.5
- w_x: bfloat16 [2048, 4096], P(None, 'state'), may hold values from -0.125 to 0.125
- w_z: bfloat16 [2048, 4096], P(None, 'state'), may hold values from -0.125 to 0.125
- conv_weight: float32 [4, 4096], P(None, 'state'), may hold values from -3 to 3
- conv_bias: float32 [4096], P('state'), may hold values from -3 to 3
- w_down: bfloat16 [4096, 128], P('state'), may hold values from -0.09375 to 0.09375
- w_up: bfloat16 [128, 4096], P(None, 'state'), may hold values from -0.5 to 0.5
- beta_bias: float32 [4096], P('state'), may hold values from -6 to 0
- w_keyq: bfloat16 [4096, 32], P('state'), may hold values from -0.09375 to 0.09375
- skip_gain: float32 [4096], P('state'), may hold values from 0.1 to 1.9
- w_out: bfloat16 [4096, 2048], P('state'), may hold values from -0.25 to 0.25
- cotangent: bfloat16 [2048, 2048], P('dp'), may hold values from -6 to 6
- group_ids: int32 [8], P('dp'), may hold values from 0 to 7
- group_weights: float32 [8], replicated, may hold values from 0.5 to 2
Outputs:
- block_out: bfloat16 [2048, 2048], P('dp', 'state')
- grad_tokens: float32 [2048, 2048], P('dp', 'state')
- grad_gain: float32 [2048], P('state')
- grad_wx: float32 [2048, 4096], P('dp', 'state')
- grad_wz: float32 [2048, 4096], P('dp', 'state')
- grad_conv_weight: float32 [4, 4096], P(None, 'state')
- grad_conv_bias: float32 [4096], P('state')
- grad_down: float32 [4096, 128], P('state')
- grad_up: float32 [128, 4096], P(None, 'state')
- grad_beta_bias: float32 [4096], P('state')
- grad_keyq: float32 [4096, 32], P('state')
- grad_skip: float32 [4096], P('state')
- grad_out: float32 [4096, 2048], P('state', 'dp')
- beta_max: float32 [], replicated
The draws below stay inside these ranges and needn't reach their ends.
All inputs are finite; a program needn't handle non-finite values.
Results may differ from the reference program's by a relative error of at most 0.011.
Values may be sent and summed in bfloat16 or wider, within the bound.
No kernel may reach another device: no remote copies, remote signals or barrier semaphores. Data moves between devices by JAX's collectives and lax.ppermute only.
A program may use at most 256 MiB of HBM per device.

```python
import math
import jax
import jax.numpy as jnp
from jax import lax

D = 2048
INNER = 4096
NSTATE = 16
CONV = 4
RANK = 128
SPAN = 128
GROUPS = 8
SEQ_LEN = 256
SEQUENCES = 8
TOKENS = 2048


def plant(array, stream_key, low, high):
    longest = array.shape.index(max(array.shape))
    spots = []
    for shift in (0, 1):
        where = [jax.random.randint(jax.random.fold_in(stream_key, axis), (), 0, length) for axis, length in enumerate(array.shape)]
        where[longest] = (where[longest] + shift) % array.shape[longest]
        spots.append(tuple(where))
    return array.at[spots[0]].set(low).at[spots[1]].set(high)


def steps_of(stream_key, extent, cuts, low, high):
    factor_of = 1.0
    for position, shards_of in cuts:
        steps = jax.random.uniform(jax.random.fold_in(jax.random.fold_in(stream_key, 6), position), (shards_of,), jnp.float32, low / len(cuts), high / len(cuts))
        factor_of = factor_of * jnp.repeat(jnp.exp(steps), extent[position] // shards_of).reshape((-1,) + (1,) * (len(extent) - 1 - position))
    return factor_of


def noise(rng, dims, deviation, reach, split=(), dtype=jnp.bfloat16):
    drawn = deviation * jax.random.normal(rng, dims, jnp.float32)
    if split:
        drawn = drawn * steps_of(rng, dims, split, -0.22, 0.18)
    return jnp.clip(drawn, -reach, reach).astype(dtype)


def setup_inputs(seed: int = 0) -> dict:
    key_of = jax.random.split(jax.random.key(seed), 16)
    return {
        "tokens": noise(key_of[0], (TOKENS, D), 1.0, 6.0, ((0, 8),)),
        "norm_gain": jnp.clip(1.0 + 0.1 * jax.random.normal(key_of[1], (D,), jnp.float32), 0.5, 1.5),
        "w_x": noise(key_of[2], (D, INNER), D ** -0.5, 0.125, ((1, 4),)),
        "w_z": noise(key_of[3], (D, INNER), D ** -0.5, 0.125, ((1, 4),)),
        "conv_weight": noise(key_of[4], (CONV, INNER), CONV ** -0.5, 3.0, ((1, 4),), jnp.float32),
        "conv_bias": noise(key_of[5], (INNER,), 0.5, 3.0, ((0, 4),), jnp.float32),
        "w_down": noise(key_of[6], (INNER, RANK), INNER ** -0.5, 0.09375, ((0, 4),)),
        "w_up": noise(key_of[7], (RANK, INNER), RANK ** -0.5, 0.5, ((1, 4),)),
        "beta_bias": jnp.clip(-6.0 + 6.0 * jax.random.uniform(key_of[8], (INNER,), jnp.float32) ** steps_of(key_of[8], (INNER,), ((0, 4),), -0.2, 0.2), -6.0, 0.0),
        "w_keyq": noise(key_of[9], (INNER, 2 * NSTATE), INNER ** -0.5, 0.09375, ((0, 4),)),
        "skip_gain": jnp.clip(1.0 + 0.18 * jax.random.normal(key_of[10], (INNER,), jnp.float32), 0.1, 1.9),
        "w_out": noise(key_of[11], (INNER, D), (INNER // 8) ** -0.5, 0.25, ((0, 4),)),
        "cotangent": noise(key_of[12], (TOKENS, D), 1.0, 6.0, ((0, 8),)),
        "group_ids": plant(jax.random.randint(key_of[13], (SEQUENCES,), 0, GROUPS), jax.random.fold_in(key_of[13], 1), 0, GROUPS - 1).astype(jnp.int32),
        "group_weights": jnp.clip(jnp.exp(jax.random.uniform(key_of[14], (GROUPS,), jnp.float32, math.log(0.5), math.log(2.0))), 0.5, 2.0),
    }


@jax.custom_vjp
def low(v):
    return lax.optimization_barrier(v.astype(jnp.bfloat16)).astype(jnp.float32)

@jax.custom_vjp
def low_back(v):
    return v

def low_keep(v):
    return (low(v), None)

def low_pass(kept, grad):
    return (grad,)

def back_keep(v):
    return (v, None)

def back_low(kept, grad):
    return (low(grad),)
low.defvjp(low_keep, low_pass)
low_back.defvjp(back_keep, back_low)
EPS = 1e-05

def exact_dot(left, right):
    return jnp.dot(left, right, precision=lax.Precision.HIGHEST, preferred_element_type=jnp.float32)

def combine(first, second):
    return (first[0] * second[0], second[0] * first[1] + second[1])

def span_step(carried, pieces):
    step_size, drive_in, key_part, query_part = pieces
    decay_rate = 1.0 - (key_part * key_part)[:, :, None] * step_size[:, None, :]
    source = key_part[:, :, None] * drive_in[:, None, :]
    decay_prod, offsets = lax.associative_scan(combine, (decay_rate, source), axis=0)
    states = decay_prod * carried[None] + offsets
    readout = lax.optimization_barrier(jnp.sum(states * query_part[:, :, None], axis=1))
    return (states[-1], readout)

def recurrence(step_size, drive_in, key_part, query_part):
    blocks = SEQ_LEN // SPAN

    def blocked(member):
        return member.reshape((blocks, SPAN) + member.shape[1:])
    initial = jnp.zeros((key_part.shape[1], step_size.shape[1]), jnp.float32)
    last_state, readout = lax.scan(jax.checkpoint(span_step), initial, (blocked(step_size), blocked(drive_in), blocked(key_part), blocked(query_part)))
    return readout.reshape(step_size.shape)

def block_forward(seq_x, norm_gain, w_x, w_z, conv_weight, conv_bias, w_down, w_up, beta_bias, w_keyq, skip_gain, w_out):
    inv_rms = lax.rsqrt(lax.optimization_barrier(jnp.mean(seq_x * seq_x, axis=1, keepdims=True)) + EPS)
    normed = low(seq_x * inv_rms * norm_gain)
    pre_x = low_back(exact_dot(normed, w_x))
    pre_z = low_back(exact_dot(normed, w_z))
    padded = jnp.concatenate([jnp.zeros((CONV - 1, INNER), jnp.float32), pre_x], axis=0)
    convolved = conv_bias + sum((conv_weight[tap_index] * padded[tap_index:tap_index + SEQ_LEN] for tap_index in range(CONV)))
    mixed_act = low(jax.nn.silu(convolved))
    rank_in = low(low_back(exact_dot(mixed_act, w_down)))
    beta_raw = jax.nn.sigmoid(low_back(exact_dot(rank_in, w_up)) + beta_bias)
    beta_val = low(beta_raw)
    key_query = low_back(exact_dot(mixed_act, w_keyq))
    key_all = key_query[:, :NSTATE]
    query_all = key_query[:, NSTATE:]
    key_norm = lax.optimization_barrier(jnp.sum(key_all * key_all, axis=1, keepdims=True))
    step_size = beta_val / (1.0 + beta_val * key_norm)
    state_out = low_back(recurrence(step_size, step_size * mixed_act, key_all, query_all))
    gated_out = low((state_out + skip_gain * mixed_act) * jax.nn.silu(pre_z))
    branch = low_back(exact_dot(gated_out, w_out))
    return (seq_x + branch, beta_raw)

def reference(tokens, norm_gain, w_x, w_z, conv_weight, conv_bias, w_down, w_up, beta_bias, w_keyq, skip_gain, w_out, cotangent, group_ids, group_weights):
    params = tuple((weight_arg.astype(jnp.float32) for weight_arg in (norm_gain, w_x, w_z, conv_weight, conv_bias, w_down, w_up, beta_bias, w_keyq, skip_gain, w_out)))
    seq_inputs = tokens.astype(jnp.float32).reshape(-1, SEQ_LEN, D)
    seq_cots = cotangent.astype(jnp.float32).reshape(-1, SEQ_LEN, D)
    seq_weights = group_weights[group_ids].astype(jnp.float32)

    def per_sequence(carried, pieces):
        grads_sum, beta_peak = carried
        seq_x, seq_cot, seq_weight = pieces
        result, pullback, beta_raw = jax.vjp(block_forward, seq_x, *params, has_aux=True)
        grad_list = pullback(seq_cot * seq_weight)
        grads_sum = tuple((running + grad_part for running, grad_part in zip(grads_sum, grad_list[1:])))
        carried = (grads_sum, jnp.maximum(beta_peak, jnp.max(beta_raw)))
        return (carried, (result.astype(jnp.bfloat16), grad_list[0]))
    initial = (tuple((jnp.zeros_like(weight_arg) for weight_arg in params)), jnp.zeros((), jnp.float32))
    (grads_sum, beta_peak), (outputs, grad_inputs) = lax.scan(per_sequence, initial, (seq_inputs, seq_cots, seq_weights))
    grad_gain, grad_wx, grad_wz, grad_taps, grad_conv_bias, grad_down, grad_up, grad_beta_bias, grad_keyq, grad_skip, grad_out = grads_sum
    return (outputs.reshape(-1, D), grad_inputs.reshape(-1, D), grad_gain, grad_wx, grad_wz, grad_taps, grad_conv_bias, grad_down, grad_up, grad_beta_bias, grad_keyq, grad_skip, grad_out, beta_peak)
```

```python
import functools

import jax
import jax.numpy as jnp
from jax import lax
from jax.experimental import pallas as pl
from jax.experimental.pallas import tpu as pltpu
from jax.sharding import PartitionSpec as P

EPS = 1e-05
LANES = 128
SUB = 8
F32 = jnp.float32
BF16 = jnp.bfloat16
MIB = 2**20
WHOLE = pl.BlockSpec(memory_space=pltpu.VMEM)


def mm(left, right):
    return jnp.dot(left, right, preferred_element_type=F32)


def mm_nt(left, right):
    return lax.dot_general(left, right, (((1,), (1,)), ((), ())), preferred_element_type=F32)


def mm_tn(left, right):
    return lax.dot_general(left, right, (((0,), (0,)), ((), ())), preferred_element_type=F32)


def swap(value, axis, bit):
    size = lax.axis_size(axis)
    return lax.ppermute(value, axis, [(i, i ^ bit) for i in range(size)])


def bits_of(axis):
    size = lax.axis_size(axis)
    bits, bit = [], 1
    while bit < size:
        bits.append(bit)
        bit *= 2
    return bits


def all_sum(value, axis):
    for bit in bits_of(axis):
        value = value + swap(value, axis, bit)
    return value


def all_max(value, axis):
    for bit in bits_of(axis):
        value = jnp.maximum(value, swap(value, axis, bit))
    return value


def halves(value, dim, bit_set):
    kept = lax.dynamic_index_in_dim(value, bit_set, dim, keepdims=False)
    sent = lax.dynamic_index_in_dim(value, 1 - bit_set, dim, keepdims=False)
    return kept, sent


def all_but_last(value, axis):
    bits = bits_of(axis)
    for bit in bits[:-1]:
        value = value + swap(value, axis, bit)
    return value, swap(value, axis, bits[-1])


def shifted(value, by, rows):
    if by == 0:
        return value
    count = value.shape[0]
    moved = pltpu.roll(value, by % count, 0)
    keep = rows >= by if by > 0 else rows < count + by
    return jnp.where(keep, moved, 0.0)


def front_kernel(
    blocked, place, ids, weights, tok, cot, gain, wx, cw, cb, wd, wk,
    normed, up, prex, mixed, dsilu, part, *rest,
):
    step = pl.program_id(0)
    rows, width = tok.shape
    acc = rest[-1]

    @pl.when(step == 0)
    def _():
        value = tok[...].astype(F32)
        inv = lax.rsqrt(jnp.mean(value * value, axis=1, keepdims=True) + EPS)
        normed[...] = (value * inv * gain[...]).astype(BF16)
        part[...] = jnp.zeros_like(part)
        acc[...] = jnp.zeros_like(acc)

    pre = mm(normed[...], wx[...])
    prex[...] = pre
    row = lax.broadcasted_iota(jnp.int32, pre.shape, 0)
    taps = cw.shape[0]
    conv = cb[...] + sum(cw[j : j + 1, :] * shifted(pre, taps - 1 - j, row) for j in range(taps))
    sig = jax.nn.sigmoid(conv)
    mix = (conv * sig).astype(BF16)
    mixed[...] = mix
    dsilu[...] = sig * (1.0 + conv * (1.0 - sig))
    part[:rows, :] += mm(mix, wd[...])
    acc[...] += mm(mix, wk[...])

    @pl.when(step == pl.num_programs(0) - 1)
    def _():
        flat = jnp.transpose(acc[...])
        wide = flat.shape[0]
        for c in range(rows // LANES):
            part[rows + c * wide : rows + (c + 1) * wide, :] = flat[:, c * LANES : (c + 1) * LANES]
        up[...] = (cot[...].astype(F32) * weights[ids[0]]).astype(BF16)
        if blocked:
            far, near, own = rest[:3]
            own_rows = width // blocked
            for p in range(blocked):
                from_cols = pl.ds(pl.multiple_of((place[0] ^ p) * own_rows, own_rows), own_rows)
                dest = far.at[p & 1] if p & 2 else (near if p & 1 else own)
                for side, source in enumerate((normed, up)):
                    first = (side * (blocked // 4) + p // 4) * own_rows
                    dest[:, first : first + own_rows] = source[:, from_cols]


def front(
    place, group_ids, group_weights, tokens, cotangent, norm_gain, w_x,
    conv_weight, conv_bias, w_down, w_keyq, blocked,
):
    rows, width = tokens.shape
    inner = w_x.shape[1]
    rank, kq = w_down.shape[1], w_keyq.shape[1]
    blk = min(inner, 256)
    whole = lambda shape: pl.BlockSpec(shape, lambda i: (0,) * len(shape))
    cols = lambda height: pl.BlockSpec((height, blk), lambda i: (0, i))
    down = lambda wide: pl.BlockSpec((blk, wide), lambda i: (i, 0))
    smem = pl.BlockSpec(memory_space=pltpu.SMEM)
    part_rows = rows + kq * rows // LANES
    both = 2 * width // 4
    shapes = [(2, rows, both), (rows, both), (rows, both)] if blocked else []
    return pl.pallas_call(
        functools.partial(front_kernel, blocked),
        grid=(inner // blk,),
        in_specs=[
            smem,
            smem,
            smem,
            whole((rows, width)),
            whole((rows, width)),
            whole((1, width)),
            cols(width),
            cols(conv_weight.shape[0]),
            cols(1),
            down(rank),
            down(kq),
        ],
        out_specs=[
            whole((rows, width)),
            whole((rows, width)),
            cols(rows),
            cols(rows),
            cols(rows),
            whole((part_rows, LANES)),
        ]
        + [whole(shape) for shape in shapes],
        out_shape=[
            jax.ShapeDtypeStruct((rows, width), BF16),
            jax.ShapeDtypeStruct((rows, width), BF16),
            jax.ShapeDtypeStruct((rows, inner), F32),
            jax.ShapeDtypeStruct((rows, inner), BF16),
            jax.ShapeDtypeStruct((rows, inner), F32),
            jax.ShapeDtypeStruct((part_rows, LANES), F32),
        ]
        + [jax.ShapeDtypeStruct(shape, BF16) for shape in shapes],
        scratch_shapes=[pltpu.VMEM((rows, kq), F32)],
        compiler_params=pltpu.CompilerParams(vmem_limit_bytes=26 * MIB),
        name="front",
    )(
        place, group_ids, group_weights, tokens, cotangent, norm_gain[None], w_x,
        conv_weight, conv_bias[None], w_down, w_keyq,
    )


def gate_kernel(normed, up, wz, wo, silu, dgate, gy):
    pre = mm(normed[...], wz[...])
    back = mm_nt(up[...], wo[...])
    sig = jax.nn.sigmoid(pre)
    act = pre * sig
    silu[...] = act
    gy[...] = back * act
    dgate[...] = back * sig * (1.0 + pre * (1.0 - sig))


def gate(normed, upstream_b, w_z, w_out):
    rows, width = normed.shape
    inner = w_z.shape[1]
    blk = min(inner, 256)
    whole = lambda shape: pl.BlockSpec(shape, lambda i: (0, 0))
    cols = lambda height: pl.BlockSpec((height, blk), lambda i: (0, i))
    return pl.pallas_call(
        gate_kernel,
        grid=(inner // blk,),
        in_specs=[
            whole((rows, width)),
            whole((rows, width)),
            cols(width),
            pl.BlockSpec((blk, width), lambda i: (i, 0)),
        ],
        out_specs=[cols(rows)] * 3,
        out_shape=[jax.ShapeDtypeStruct((rows, inner), F32)] * 3,
        compiler_params=pltpu.CompilerParams(vmem_limit_bytes=24 * MIB),
        cost_estimate=pl.CostEstimate(
            flops=4 * rows * width * inner, bytes_accessed=14 * MIB, transcendentals=rows * inner
        ),
        name="gate",
    )(normed, upstream_b, w_z, w_out)


def key_query_of(one, two, rows, count):
    parts = []
    for c in range(rows // LANES):
        at = slice(rows + c * count, rows + (c + 1) * count)
        parts.append(one[at, :] + two[at, :])
    return jnp.transpose(jnp.concatenate(parts, axis=1))


def lay_tiles(dest, value, base=0):
    for j in range(SUB):
        dest[pl.ds(base * SUB + j, value.shape[0], stride=SUB), :] = value[
            :, j * LANES : (j + 1) * LANES
        ]


def lay_rows(source, count, j):
    return source[pl.ds(j, count, stride=SUB), :]


def spread(dest, key_query):
    rows, count = key_query.shape
    for n in range(count):
        dest[n * rows : (n + 1) * rows, :] = jnp.broadcast_to(
            key_query[:, n : n + 1], (rows, LANES)
        )


def pick(source, rows, n, t):
    return source[pl.ds(n * rows + t, SUB, stride=0), :]


def scan_kernel(
    unroll, one, two, mixed, wup, bias, silu, dgate, skip,
    gated, prez, step_out, raw_out, peak, hist, last, step_t, mix_t, out_t, kb,
):
    rows, inner = mixed.shape
    states = kb.shape[0] // rows // 2
    kq = key_query_of(one, two, rows, 2 * states)
    keys = kq[:, :states]
    norm = jnp.sum(keys * keys, axis=1, keepdims=True)
    spread(kb, kq)
    rank_b = (one[:rows, :] + two[:rows, :]).astype(BF16)
    raw = jax.nn.sigmoid(mm(rank_b, wup[...]) + bias[...])
    raw_out[...] = raw
    highest = jnp.max(jnp.max(raw, axis=0, keepdims=True), axis=1, keepdims=True)
    peak[...] = jnp.broadcast_to(highest, peak.shape)
    beta = raw.astype(BF16).astype(F32)
    size = beta / (1.0 + beta * norm)
    step_out[...] = size
    lay_tiles(step_t, size)
    lay_tiles(mix_t, mixed[...].astype(F32))

    def token(t, carried):
        at = pl.ds(pl.multiple_of(t * SUB, SUB), SUB)
        size = step_t[at, :]
        mix = mix_t[at, :]
        sums = [None] * 4
        following = []
        for n in range(states):
            key = pick(kb, rows, n, t)
            query = pick(kb, rows, states + n, t)
            state = carried[n]
            hist[t, n] = state
            state = state + (size * key) * (mix - key * state)
            term = query * state
            sums[n % 4] = term if sums[n % 4] is None else sums[n % 4] + term
            following.append(state)
        out_t[at, :] = (sums[0] + sums[1]) + (sums[2] + sums[3])
        return tuple(following)

    zero = jnp.zeros((SUB, LANES), F32)
    final = lax.fori_loop(0, rows, token, (zero,) * states, unroll=unroll)
    for n in range(states):
        last[n] = final[n]
    for j in range(SUB):
        at = slice(j * LANES, (j + 1) * LANES)
        y = lay_rows(out_t, rows, j) + skip[:, at] * mixed[:, at].astype(F32)
        gated[:, at] = (y * silu[:, at]).astype(BF16)
        prez[:, at] = (y * dgate[:, at]).astype(BF16)


def scan_forward(summed, mixed, w_up, beta_bias, silu, dgate, skip_gain, states):
    rows, inner = mixed.shape
    full = lambda dtype: jax.ShapeDtypeStruct((rows, inner), dtype)
    return pl.pallas_call(
        functools.partial(scan_kernel, 4),
        in_specs=[WHOLE] * 8,
        out_specs=[WHOLE] * 7,
        out_shape=[
            full(BF16),
            full(BF16),
            full(F32),
            full(F32),
            jax.ShapeDtypeStruct((SUB, LANES), F32),
            pltpu.VMEM((rows, states, SUB, LANES), F32),
            jax.ShapeDtypeStruct((states, SUB, LANES), F32),
        ],
        scratch_shapes=[pltpu.VMEM((rows * SUB, LANES), F32)] * 3
        + [pltpu.VMEM((2 * states * rows, LANES), F32)],
        compiler_params=pltpu.CompilerParams(vmem_limit_bytes=22 * MIB),
        cost_estimate=pl.CostEstimate(
            flops=60 * rows * inner * states, bytes_accessed=16 * MIB, transcendentals=0
        ),
        name="scan",
    )(*summed, mixed, w_up, beta_bias[None], silu, dgate, skip_gain[None])


def back_kernel(
    unroll, place, one, two, mixed, wup, step_in, raw_in, gy, hist, last, peak,
    gmix, pay, ups, preb, step_t, mix_t, gs_t, kb, sum_d, sum_s, prods, zk, zq,
):
    rows, inner = mixed.shape
    states = last.shape[0]
    rank = wup.shape[0]
    span = zk.shape[0] // states
    kq = key_query_of(one, two, rows, 2 * states)
    keys = kq[:, :states]
    norm = jnp.sum(keys * keys, axis=1, keepdims=True)
    spread(kb, kq)
    lay_tiles(step_t, step_in[...])
    lay_tiles(mix_t, mixed[...].astype(F32) * 0.5)
    gs_t[0:SUB, :] = jnp.zeros((SUB, LANES), F32)
    lay_tiles(gs_t, gy[...].astype(BF16).astype(F32), 1)

    def reduce_to(dest, row, terms, slot):
        base = slot * states * SUB
        for n in range(states):
            prods[pl.ds(base + n * SUB, SUB), :] = terms[n]
        for g in range(states // SUB):
            total = None
            for s in range(SUB):
                part = prods[pl.ds(base + g * SUB * SUB + s, SUB, stride=SUB), :]
                total = part if total is None else total + part
            dest[pl.ds(row + g * SUB * span, SUB, stride=span), :] = total

    tail = gs_t[pl.ds(rows * SUB, SUB), :]
    reduce_to(zq, rows, [last[n] * tail for n in range(states)], 0)

    def token(t, u, carried):
        at = pl.ds(pl.multiple_of(t * SUB, SUB), SUB)
        size = step_t[at, :]
        half = mix_t[at, :]
        before = gs_t[at, :]
        grad = gs_t[pl.ds(pl.multiple_of(t * SUB + SUB, SUB), SUB), :]
        drive = size * half
        total_d, total_s = [None] * 2, [None] * 2
        following, for_key, for_query = [], [], []
        for n in range(states):
            key = pick(kb, rows, n, t)
            query = pick(kb, rows, states + n, t)
            state = hist[t, n]
            full = query * grad + carried[n]
            by_key = full * key
            by_state = by_key * state
            term = key * by_state
            following.append(full - key * (size * by_key))
            for_key.append(full * drive - size * by_state)
            for_query.append(state * before)
            i = n % 2
            total_d[i] = by_key if total_d[i] is None else total_d[i] + by_key
            total_s[i] = term if total_s[i] is None else total_s[i] + term
        sum_d[at, :] = total_d[0] + total_d[1]
        sum_s[at, :] = total_s[0] + total_s[1]
        reduce_to(zk, t, for_key, 2 * u)
        reduce_to(zq, t, for_query, 2 * u + 1)
        return tuple(following)

    def some(i, carried):
        for u in range(unroll):
            carried = token(rows - 1 - (i * unroll + u), u, carried)
        return carried

    zero = jnp.zeros((SUB, LANES), F32)
    lax.fori_loop(0, rows // unroll, some, (zero,) * states)

    total_norm = jnp.zeros((rows, 1), F32)
    for j in range(SUB):
        at = slice(j * LANES, (j + 1) * LANES)
        drive_grad = lay_rows(sum_d, rows, j)
        size = step_in[:, at]
        grad_step = drive_grad * mixed[:, at].astype(F32) - lay_rows(sum_s, rows, j)
        gmix[:, at] = drive_grad * size
        total_norm = total_norm - jnp.sum(grad_step * size * size, axis=1, keepdims=True)
        raw = raw_in[:, at]
        plus = 1.0 + raw.astype(BF16).astype(F32) * norm
        pre = grad_step / (plus * plus) * raw * (1.0 - raw)
        ups[rank : rank + SUB, at] = jnp.broadcast_to(
            jnp.sum(pre, axis=0, keepdims=True), (SUB, LANES)
        )
        preb[:, at] = pre.astype(BF16)
    pay[:rows, :] = mm_nt(preb[...], wup[...])
    rank_b = (one[:rows, :] + two[:rows, :]).astype(BF16)
    ups[:rank, :] = mm_tn(rank_b, preb[...])

    source = lax.broadcasted_iota(jnp.int32, (LANES, LANES), 1)
    lane = lax.broadcasted_iota(jnp.int32, (rows, LANES), 1)
    row = lax.broadcasted_iota(jnp.int32, (rows, LANES), 0)
    table = jnp.where(lane == 2 * states, jnp.broadcast_to(total_norm, (rows, LANES)), 0.0)
    mark = (lane == 2 * states + 1) & (row == place[1])
    table = jnp.where(mark, jnp.broadcast_to(peak[0:1, :], (rows, LANES)), table)
    for n in range(states):
        table = table + mm(
            zk[pl.ds(n * span, rows), :], jnp.where(source == n, 2.0, 0.0)
        )
        table = table + mm(
            zq[pl.ds(n * span + 1, rows), :], jnp.where(source == states + n, 1.0, 0.0)
        )
    flat = jnp.transpose(table)
    high = (pay.shape[0] - rows) * LANES // rows
    for c in range(rows // LANES):
        pay[rows + c * high : rows + (c + 1) * high, :] = flat[:high, c * LANES : (c + 1) * LANES]


def scan_backward(place, summed, mixed, w_up, step_in, raw, gy, hist, last, peak):
    rows, inner = mixed.shape
    states = last.shape[0]
    unroll = 2
    span = rows + SUB
    high = 2 * states + SUB
    pay_rows = rows + high * rows // LANES
    return pl.pallas_call(
        functools.partial(back_kernel, unroll),
        in_specs=[pl.BlockSpec(memory_space=pltpu.SMEM)] + [WHOLE] * 10,
        out_specs=[WHOLE] * 3,
        out_shape=[
            jax.ShapeDtypeStruct((rows, inner), F32),
            jax.ShapeDtypeStruct((pay_rows, LANES), F32),
            jax.ShapeDtypeStruct((w_up.shape[0] + SUB, inner), F32),
        ],
        scratch_shapes=[
            pltpu.VMEM((rows, inner), BF16),
            pltpu.VMEM((rows * SUB, LANES), F32),
            pltpu.VMEM((rows * SUB, LANES), F32),
            pltpu.VMEM((rows * SUB + SUB, LANES), F32),
            pltpu.VMEM((2 * states * rows, LANES), F32),
            pltpu.VMEM((rows * SUB, LANES), F32),
            pltpu.VMEM((rows * SUB, LANES), F32),
            pltpu.VMEM((unroll * 2 * states * SUB, LANES), F32),
            pltpu.VMEM((states * span, LANES), F32),
            pltpu.VMEM((states * span, LANES), F32),
        ],
        compiler_params=pltpu.CompilerParams(vmem_limit_bytes=28 * MIB),
        cost_estimate=pl.CostEstimate(
            flops=60 * rows * inner * states, bytes_accessed=16 * MIB, transcendentals=0
        ),
        name="back",
    )(
        place, *summed, mixed, w_up, step_in, raw, gy,
        pltpu.with_memory_space_constraint(hist, pltpu.VMEM), last, peak,
    )


def conv_kernel(
    place, one, two, grad_one, grad_two, mixed, gy, gmix, dsilu, prex, cw, skip, wd, wk,
    prex_b, down, rest,
):
    rows, inner = mixed.shape
    count = wk.shape[1]
    states = count // 2
    high = (grad_one.shape[0] - rows) * LANES // rows
    kq = key_query_of(one, two, rows, count)
    gkq = key_query_of(grad_one, grad_two, rows, high)
    norm_grad = gkq[:, count : count + 1]
    peak = jnp.max(gkq[:, count + 1 : count + 2], axis=0, keepdims=True)
    lane = lax.broadcasted_iota(jnp.int32, (rows, count), 1)
    kq_b = (gkq[:, :count] + jnp.where(lane < states, 2.0 * kq * norm_grad, 0.0)).astype(BF16)
    rank_b = (grad_one[:rows, :] + grad_two[:rows, :]).astype(BF16)
    taps = cw.shape[0]
    blk = 256
    for c in range(inner // blk):
        at = slice(c * blk, (c + 1) * blk)
        mix = mixed[:, at].astype(F32)
        grad_y = gy[:, at]
        total = grad_y * skip[:, at] + gmix[:, at]
        total = total + mm_nt(kq_b, wk[at, :]) + mm_nt(rank_b, wd[at, :])
        grad = total * dsilu[:, at]
        pre = prex[:, at]
        row = lax.broadcasted_iota(jnp.int32, grad.shape, 0)
        out = None
        sums = []
        for j in range(taps):
            by = taps - 1 - j
            sums.append(jnp.sum(grad * shifted(pre, by, row), axis=0, keepdims=True))
            term = cw[j : j + 1, at] * shifted(grad, -by, row)
            out = term if out is None else out + term
        sums.append(jnp.sum(grad, axis=0, keepdims=True))
        sums.append(jnp.sum(grad_y * mix, axis=0, keepdims=True))
        channel = lax.broadcasted_iota(jnp.int32, (1, blk), 1) + c * blk
        sums.append(jnp.where(channel == place[0], jnp.broadcast_to(peak, (1, blk)), 0.0))
        for i, line in enumerate(sums):
            rest[count + i : count + i + 1, at] = line
        prex_b[:, at] = out.astype(BF16)
    for i in range(len(sums), SUB):
        rest[count + i : count + i + 1, :] = jnp.zeros((1, inner), F32)
    down[...] = mm_tn(mixed[...], rank_b)
    rest[:count, :] = mm_tn(kq_b, mixed[...])


def conv_back(
    place, summed, grads, mixed, gy, gmix, dsilu, prex, conv_weight, skip_gain, w_down, w_keyq
):
    rows, inner = mixed.shape
    return pl.pallas_call(
        conv_kernel,
        in_specs=[pl.BlockSpec(memory_space=pltpu.SMEM)] + [WHOLE] * 13,
        out_specs=[WHOLE] * 3,
        out_shape=[
            jax.ShapeDtypeStruct((rows, inner), BF16),
            jax.ShapeDtypeStruct((inner, w_down.shape[1]), F32),
            jax.ShapeDtypeStruct((w_keyq.shape[1] + SUB, inner), F32),
        ],
        compiler_params=pltpu.CompilerParams(vmem_limit_bytes=24 * MIB),
        name="conv",
    )(
        place, *summed, *grads, mixed, gy, gmix, dsilu, prex, conv_weight, skip_gain[None],
        w_down, w_keyq,
    )


def branch_kernel(place, gated, wo, tok, send, keep):
    i = pl.program_id(0)
    value = mm(gated[...], wo[...])

    @pl.when(i == 0)
    def _():
        keep[0] = value + tok[...].astype(F32)

    @pl.when(i == 2)
    def _():
        keep[0] = value

    @pl.when(i % 2 == 1)
    def _():
        send[0] = value.astype(BF16)


def branch(place, gated, w_out, tokens, parts):
    rows, inner = gated.shape
    width = w_out.shape[1]
    own = width // parts
    return pl.pallas_call(
        branch_kernel,
        grid_spec=pltpu.PrefetchScalarGridSpec(
            num_scalar_prefetch=1,
            grid=(parts,),
            in_specs=[
                pl.BlockSpec((rows, inner), lambda i, place: (0, 0)),
                pl.BlockSpec((inner, own), lambda i, place: (0, place[1] ^ i)),
                pl.BlockSpec((rows, own), lambda i, place: (0, place[1])),
            ],
            out_specs=[pl.BlockSpec((1, rows, own), lambda i, place: (i // 2, 0, 0))] * 2,
        ),
        out_shape=[
            jax.ShapeDtypeStruct((parts // 2, rows, own), BF16),
            jax.ShapeDtypeStruct((parts // 2, rows, own), F32),
        ],
        compiler_params=pltpu.CompilerParams(vmem_limit_bytes=16 * MIB),
        cost_estimate=pl.CostEstimate(
            flops=2 * rows * inner * width, bytes_accessed=8 * MIB, transcendentals=0
        ),
        name="branch",
    )(place, gated, w_out, tokens)


def input_kernel(
    place, ids, weights, prex, prez, wx, wz, tok, tok_own, cot, gain,
    send, keep, stats, slope, shift, base, inv, dots,
):
    i = pl.program_id(0)
    rows, width = tok.shape

    @pl.when(i == 0)
    def _():
        value = tok[...].astype(F32)
        inv[...] = jnp.broadcast_to(
            lax.rsqrt(jnp.mean(value * value, axis=1, keepdims=True) + EPS), inv.shape
        )
        dots[...] = jnp.zeros_like(dots)

    value = mm_nt(prex[...], wx[...]) + mm_nt(prez[...], wz[...])
    rms = inv[:, 0:1]
    unit = tok_own[...].astype(F32) * rms
    by_unit = value * unit
    dots[...] += jnp.sum(by_unit * gain[...], axis=1, keepdims=True)
    line = jnp.sum(by_unit, axis=0, keepdims=True)
    own = line.shape[1] // LANES
    first = rows // LANES + (place[1] ^ i) * own
    for j in range(own):
        stats[pl.ds(first + j, 1), :] = line[:, j * LANES : (j + 1) * LANES]

    @pl.when(i == 0)
    def _():
        slope[...] = rms * gain[...]
        shift[...] = unit * rms * (1.0 / width)
        base[...] = cot[...].astype(F32) * weights[ids[0]]

    @pl.when(i % 2 == 0)
    def _():
        keep[0] = value

    @pl.when(i % 2 == 1)
    def _():
        send[0] = value.astype(BF16)

    @pl.when(i == pl.num_programs(0) - 1)
    def _():
        flat = jnp.transpose(dots[...])
        for c in range(rows // LANES):
            stats[c : c + 1, :] = flat[0:1, c * LANES : (c + 1) * LANES]


def input_grad(
    place, group_ids, group_weights, prex, prez, w_x, w_z, tokens, cotangent, norm_gain, parts
):
    rows, inner = prex.shape
    width = tokens.shape[1]
    own = width // parts
    whole = lambda shape: pl.BlockSpec(shape, lambda i, place: (0, 0))
    part = pl.BlockSpec((own, inner), lambda i, place: (place[1] ^ i, 0))
    mine = pl.BlockSpec((rows, own), lambda i, place: (0, 0))
    smem = pl.BlockSpec(memory_space=pltpu.SMEM)
    stat_rows = rows // LANES + width // LANES
    return pl.pallas_call(
        input_kernel,
        grid_spec=pltpu.PrefetchScalarGridSpec(
            num_scalar_prefetch=1,
            grid=(parts,),
            in_specs=[
                smem,
                smem,
                whole((rows, inner)),
                whole((rows, inner)),
                part,
                part,
                whole((rows, width)),
                pl.BlockSpec((rows, own), lambda i, place: (0, place[1] ^ i)),
                pl.BlockSpec((rows, own), lambda i, place: (0, place[1])),
                pl.BlockSpec((1, own), lambda i, place: (0, place[1] ^ i)),
            ],
            out_specs=[pl.BlockSpec((1, rows, own), lambda i, place: (i // 2, 0, 0))] * 2
            + [whole((stat_rows, LANES)), mine, mine, mine],
            scratch_shapes=[pltpu.VMEM((rows, LANES), F32)] * 2,
        ),
        out_shape=[
            jax.ShapeDtypeStruct((parts // 2, rows, own), BF16),
            jax.ShapeDtypeStruct((parts // 2, rows, own), F32),
            jax.ShapeDtypeStruct((stat_rows, LANES), F32),
        ]
        + [jax.ShapeDtypeStruct((rows, own), F32)] * 3,
        compiler_params=pltpu.CompilerParams(vmem_limit_bytes=24 * MIB),
        cost_estimate=pl.CostEstimate(
            flops=4 * rows * inner * width, bytes_accessed=12 * MIB, transcendentals=0
        ),
        name="inputs",
    )(
        place, group_ids, group_weights, prex, prez, w_x, w_z, tokens, tokens, cotangent,
        norm_gain[None],
    )


def out_weight_kernel(l0, l1, l2, l3, r0, r1, r2, r3, keep, send):
    own = keep.shape[1]
    total = None
    for left, right in ((l0, r0[:, 2 * own :]), (l1, r1[0, :, 2 * own :]), (l2, r2[:, 2 * own :]), (l3, r3[:, 2 * own :])):
        term = mm_tn(left[...], right)
        total = term if total is None else total + term
    keep[...] = total[:, :own]
    send[...] = total[:, own:].astype(BF16)


def out_weight(lefts, rights):
    rows, inner = lefts[0].shape
    own = rights[0].shape[1] // 4
    blk = 256
    whole = lambda value: pl.BlockSpec(value.shape, lambda i: (0,) * value.ndim)
    return pl.pallas_call(
        out_weight_kernel,
        grid=(inner // blk,),
        in_specs=[pl.BlockSpec((rows, blk), lambda i: (0, i))] * 4 + [whole(r) for r in rights],
        out_specs=[pl.BlockSpec((blk, own), lambda i: (i, 0))] * 2,
        out_shape=[
            jax.ShapeDtypeStruct((inner, own), F32),
            jax.ShapeDtypeStruct((inner, own), BF16),
        ],
        compiler_params=pltpu.CompilerParams(vmem_limit_bytes=20 * MIB),
        cost_estimate=pl.CostEstimate(
            flops=16 * rows * inner * own, bytes_accessed=6 * MIB, transcendentals=0
        ),
        name="outw",
    )(*lefts, *rights)


def in_weight_kernel(l0, l1, l2, l3, r0, r1, r2, r3, keep, send):
    i = pl.program_id(0)
    total = None
    for left, right in ((l0[...], r0), (l1[0], r1), (l2[...], r2), (l3[...], r3)):
        term = mm_tn(left, right[...])
        total = term if total is None else total + term

    @pl.when(i == 0)
    def _():
        send[...] = total.astype(BF16)

    @pl.when(i == 1)
    def _():
        keep[...] = total


def in_weight(lefts, rights):
    rows, inner = rights[0].shape
    own = lefts[0].shape[1] // 4
    whole = lambda value: pl.BlockSpec(value.shape, lambda i: (0,) * value.ndim)
    side = pl.BlockSpec((rows, own), lambda i: (0, 1 - i))
    return pl.pallas_call(
        in_weight_kernel,
        grid=(2,),
        in_specs=[side, pl.BlockSpec((1, rows, own), lambda i: (0, 0, 1 - i)), side, side]
        + [whole(r) for r in rights],
        out_specs=[pl.BlockSpec((own, inner), lambda i: (0, 0))] * 2,
        out_shape=[
            jax.ShapeDtypeStruct((own, inner), F32),
            jax.ShapeDtypeStruct((own, inner), BF16),
        ],
        compiler_params=pltpu.CompilerParams(vmem_limit_bytes=20 * MIB),
        cost_estimate=pl.CostEstimate(
            flops=16 * rows * inner * own, bytes_accessed=6 * MIB, transcendentals=0
        ),
        name="inw",
    )(*lefts, *rights)


def split_bits(axis):
    bits = bits_of(axis)
    return [bit for bit in (2, 1) if bit in bits], [bit for bit in reversed(bits) if bit > 2]


def gather_tokens(value, axis):
    pieces = [value]
    for bit in split_bits(axis)[0]:
        pieces = pieces + [swap(piece, axis, bit) for piece in pieces]
    return pieces


def exchange_cols(value, axis):
    size = lax.axis_size(axis)
    me = lax.axis_index(axis)
    gather, scatter = split_bits(axis)
    rows, cols = value.shape
    outer = 2 ** len(scatter)
    pieces = [value.reshape((rows, outer) + (2,) * len(gather) + (cols // size,))]
    for bit in gather:
        kept, sent = zip(*(halves(piece, 2, (me // bit) % 2) for piece in pieces))
        pieces = list(kept) + [swap(piece, axis, bit) for piece in sent]
    return [piece.reshape(rows, -1) for piece in pieces]


def scatter_sum(value, axis, dim):
    me = lax.axis_index(axis)
    scatter = split_bits(axis)[1]
    for bit in scatter:
        shape = value.shape
        split = shape[:dim] + (2, shape[dim] // 2) + shape[dim + 1 :]
        kept, sent = halves(value.reshape(split), dim, (me // bit) % 2)
        value = kept + swap(sent.astype(BF16), axis, bit).astype(F32)
    return value


def per_device(
    tokens,
    norm_gain,
    w_x,
    w_z,
    conv_weight,
    conv_bias,
    w_down,
    w_up,
    beta_bias,
    w_keyq,
    skip_gain,
    w_out,
    cotangent,
    group_ids,
    group_weights,
):
    rows, width = tokens.shape
    states = w_keyq.shape[1] // 2
    taps = conv_weight.shape[0]
    assert group_ids.shape[0] == 1
    parts = lax.axis_size("state")
    assert parts == 4
    dp_size = lax.axis_size("dp")
    own_width = width // parts
    state_index = lax.axis_index("state")
    place = jnp.stack([lax.axis_index("dp"), state_index]).astype(jnp.int32)
    blocked = dp_size if dp_size == 8 and width % (8 * LANES) == 0 else 0

    normed, upstream_b, pre_x, mixed_b, dsilu, part, *blocks = front(
        place, group_ids, group_weights, tokens, cotangent, norm_gain, w_x,
        conv_weight, conv_bias, w_down, w_keyq, blocked,
    )
    summed = all_but_last(part, "state")
    if blocked:
        far, near, own = blocks
        far = swap(far, "dp", 2)
        sides = (own, far, swap(near, "dp", 1), swap(far[1], "dp", 1))
    else:
        norm_parts = exchange_cols(normed, "dp")
        up_parts = exchange_cols(upstream_b, "dp")
    silu_z, dgate, grad_y = gate(normed, upstream_b, w_z, w_out)

    gated_b, prez_b, step_size, raw, peak, hist, last = scan_forward(
        summed, mixed_b, w_up, beta_bias, silu_z, dgate, skip_gain, states
    )

    def weight_grad(value, left):
        if blocked:
            far = swap(value, "dp", 2)
            pieces = (value, far, swap(value, "dp", 1), swap(far, "dp", 1))
            keep, send = out_weight(pieces, sides) if left else in_weight(sides, pieces)
            return keep + swap(send, "dp", 4).astype(F32)
        pieces = gather_tokens(value, "dp")
        pairs = zip(pieces, up_parts) if left else zip(norm_parts, pieces)
        return scatter_sum(sum(mm_tn(a, b) for a, b in pairs), "dp", 1 if left else 0)

    grad_wout = weight_grad(gated_b, True)
    grad_wz = weight_grad(prez_b, False)

    gmix, pay, ups = scan_backward(
        place, summed, mixed_b, w_up, step_size, raw, grad_y, hist, last, peak
    )
    grads = all_but_last(pay, "state")
    ups = lax.psum(ups, "dp")

    def over_state(send, keep):
        come = swap(send, "state", 1)
        last_come = swap((keep[1] + come[1].astype(F32)).astype(BF16), "state", 2)
        return keep[0] + come[0].astype(F32) + last_come.astype(F32)

    block_out = over_state(*branch(place, gated_b, w_out, tokens, parts)).astype(BF16)

    prex_b, down, rest = conv_back(
        place, summed, grads, mixed_b, grad_y, gmix, dsilu, pre_x, conv_weight, skip_gain,
        w_down, w_keyq,
    )
    down, rest = lax.psum((down, rest), "dp")
    grad_wx = weight_grad(prex_b, False)

    send, keep, stats, slope, shift, base = input_grad(
        place, group_ids, group_weights, prex_b, prez_b, w_x, w_z, tokens, cotangent, norm_gain,
        parts,
    )
    norm_grad = over_state(send, keep)
    stats = all_sum(stats, "state")
    row_stat = stats[: rows // LANES].reshape(rows, 1)
    grad_in = norm_grad * slope - shift * row_stat + base
    gain_rows = own_width // LANES
    own_gain = lax.dynamic_slice_in_dim(
        stats, rows // LANES + state_index * gain_rows, gain_rows, 0
    )
    grad_gain = all_sum(own_gain, "dp").reshape(-1)

    count = 2 * states
    rank = w_up.shape[0]
    return (
        block_out,
        grad_in,
        grad_gain,
        grad_wx,
        grad_wz,
        rest[count : count + taps],
        rest[count + taps],
        down,
        ups[:rank],
        ups[rank],
        rest[:count].T,
        rest[count + taps + 1],
        grad_wout,
        jnp.max(rest[count + taps + 2]),
    )


def solution(mesh):
    placed = (
        P("dp", None),
        P(),
        P(None, "state"),
        P(None, "state"),
        P(None, "state"),
        P("state"),
        P("state", None),
        P(None, "state"),
        P("state"),
        P("state", None),
        P("state"),
        P("state", None),
        P("dp", None),
        P("dp"),
        P(),
    )
    return jax.shard_map(
        per_device,
        mesh=mesh,
        in_specs=placed,
        out_specs=(
            P("dp", "state"),
            P("dp", "state"),
            P("state"),
            P("dp", "state"),
            P("dp", "state"),
            P(None, "state"),
            P("state"),
            P("state", None),
            P(None, "state"),
            P("state"),
            P("state", None),
            P("state"),
            P("state", "dp"),
            P(),
        ),
        check_vma=False,
    )
```

```python
import functools

import jax
import jax.numpy as jnp
from jax import lax
from jax.experimental import pallas as pl
from jax.experimental.pallas import tpu as pltpu
from jax.sharding import PartitionSpec as P

EPS = 1e-05
LANES = 128
SUB = 8
F32 = jnp.float32
BF16 = jnp.bfloat16
MIB = 2**20
WHOLE = pl.BlockSpec(memory_space=pltpu.VMEM)
ANY = pl.BlockSpec(memory_space=pl.ANY)
SMALL = 40


def mm(left, right):
    return jnp.dot(left, right, preferred_element_type=F32)


def mm_nt(left, right):
    return lax.dot_general(left, right, (((1,), (1,)), ((), ())), preferred_element_type=F32)


def mm_tn(left, right):
    return lax.dot_general(left, right, (((0,), (0,)), ((), ())), preferred_element_type=F32)


def swap(value, axis, bit):
    size = lax.axis_size(axis)
    return lax.ppermute(value, axis, [(i, i ^ bit) for i in range(size)])


def bits_of(axis):
    size = lax.axis_size(axis)
    bits, bit = [], 1
    while bit < size:
        bits.append(bit)
        bit *= 2
    return bits


def all_sum(value, axis):
    for bit in bits_of(axis):
        value = value + swap(value, axis, bit)
    return value


def all_max(value, axis):
    for bit in bits_of(axis):
        value = jnp.maximum(value, swap(value, axis, bit))
    return value


def halves(value, dim, bit_set):
    kept = lax.dynamic_index_in_dim(value, bit_set, dim, keepdims=False)
    sent = lax.dynamic_index_in_dim(value, 1 - bit_set, dim, keepdims=False)
    return kept, sent


def all_but_last(value, axis):
    bits = bits_of(axis)
    for bit in bits[:-1]:
        value = value + swap(value, axis, bit)
    return value, swap(value, axis, bits[-1])


def in_hbm(value):
    return pltpu.with_memory_space_constraint(value, pltpu.HBM)


def shifted(value, by, rows):
    if by == 0:
        return value
    count = value.shape[0]
    moved = pltpu.roll(value, by % count, 0)
    keep = rows >= by if by > 0 else rows < count + by
    return jnp.where(keep, moved, 0.0)


def front_kernel(
    blocked, place, ids, weights, tok, cot, gain, wx, cw, cb, wd, wk,
    normed, up, prex, mixed, dsilu, part, *rest,
):
    step = pl.program_id(0)
    rows, width = tok.shape
    acc = rest[-1]

    @pl.when(step == 0)
    def _():
        value = tok[...].astype(F32)
        inv = lax.rsqrt(jnp.mean(value * value, axis=1, keepdims=True) + EPS)
        normed[...] = (value * inv * gain[...]).astype(BF16)
        part[...] = jnp.zeros_like(part)
        acc[...] = jnp.zeros_like(acc)

    pre = mm(normed[...], wx[...])
    prex[...] = pre
    row = lax.broadcasted_iota(jnp.int32, pre.shape, 0)
    taps = cw.shape[0]
    conv = cb[...] + sum(cw[j : j + 1, :] * shifted(pre, taps - 1 - j, row) for j in range(taps))
    sig = jax.nn.sigmoid(conv)
    mix = (conv * sig).astype(BF16)
    mixed[...] = mix
    dsilu[...] = sig * (1.0 + conv * (1.0 - sig))
    part[:rows, :] += mm(mix, wd[...])
    acc[...] += mm_nt(wk[...], mix)

    @pl.when(step == pl.num_programs(0) - 1)
    def _():
        wide = acc.shape[0]
        for c in range(rows // LANES):
            part[rows + c * wide : rows + (c + 1) * wide, :] = acc[:, c * LANES : (c + 1) * LANES]
        up[...] = (cot[...].astype(F32) * weights[ids[0]]).astype(BF16)
        if blocked:
            far, near, own, up_far, up_own = rest[:5]
            size = width // blocked
            for p in range(blocked):
                cols = pl.ds(pl.multiple_of((place[0] ^ p) * size, size), size)
                dest = far.at[p & 1] if p & 2 else (near if p & 1 else own)
                dest[:, (p // 4) * size : (p // 4 + 1) * size] = normed[:, cols]
                at = (p & 1) * 2 + (p >> 1 & 1)
                (up_far if p & 4 else up_own)[:, at * size : (at + 1) * size] = up[:, cols]


def front(
    place, group_ids, group_weights, tokens, cotangent, norm_gain, w_x,
    conv_weight, conv_bias, w_down, w_keyq, blocked,
):
    rows, width = tokens.shape
    inner = w_x.shape[1]
    rank, kq = w_down.shape[1], w_keyq.shape[0]
    blk = min(inner, 256)
    whole = lambda shape: pl.BlockSpec(shape, lambda i: (0,) * len(shape))
    cols = lambda height: pl.BlockSpec((height, blk), lambda i: (0, i))
    smem = pl.BlockSpec(memory_space=pltpu.SMEM)
    part_rows = rows + kq * rows // LANES
    shapes = []
    if blocked:
        quarter, half = width // 4, width // 2
        shapes = [(2, rows, quarter), (rows, quarter), (rows, quarter), (rows, half), (rows, half)]
    return pl.pallas_call(
        functools.partial(front_kernel, blocked),
        grid=(inner // blk,),
        in_specs=[
            smem,
            smem,
            smem,
            whole((rows, width)),
            whole((rows, width)),
            whole((1, width)),
            cols(width),
            cols(conv_weight.shape[0]),
            cols(1),
            pl.BlockSpec((blk, rank), lambda i: (i, 0)),
            cols(kq),
        ],
        out_specs=[
            whole((rows, width)),
            whole((rows, width)),
            cols(rows),
            cols(rows),
            cols(rows),
            whole((part_rows, LANES)),
        ]
        + [whole(shape) for shape in shapes],
        out_shape=[
            pltpu.HBM((rows, width), BF16),
            pltpu.HBM((rows, width), BF16),
            pltpu.HBM((rows, inner), F32),
            pltpu.HBM((rows, inner), BF16),
            pltpu.HBM((rows, inner), F32),
            jax.ShapeDtypeStruct((part_rows, LANES), F32),
        ]
        + [pltpu.HBM(shape, BF16) for shape in shapes],
        scratch_shapes=[pltpu.VMEM((kq, rows), F32)],
        compiler_params=pltpu.CompilerParams(vmem_limit_bytes=26 * MIB),
        name="front",
    )(
        place, group_ids, group_weights, in_hbm(tokens), in_hbm(cotangent),
        in_hbm(norm_gain[None]), in_hbm(w_x), in_hbm(conv_weight), in_hbm(conv_bias[None]),
        in_hbm(w_down), in_hbm(w_keyq),
    )


def gate_kernel(normed, up, wz, wo, silu, dgate, gy):
    pre = mm(normed[...], wz[...])
    back = mm_nt(up[...], wo[...])
    sig = jax.nn.sigmoid(pre)
    act = pre * sig
    silu[...] = act
    gy[...] = back * act
    dgate[...] = back * sig * (1.0 + pre * (1.0 - sig))


def gate(normed, upstream_b, w_z, w_out):
    rows, width = normed.shape
    inner = w_z.shape[1]
    blk = min(inner, 256)
    whole = lambda shape: pl.BlockSpec(shape, lambda i: (0, 0))
    cols = lambda height: pl.BlockSpec((height, blk), lambda i: (0, i))
    return pl.pallas_call(
        gate_kernel,
        grid=(inner // blk,),
        in_specs=[
            whole((rows, width)),
            whole((rows, width)),
            cols(width),
            pl.BlockSpec((blk, width), lambda i: (i, 0)),
        ],
        out_specs=[cols(rows)] * 3,
        out_shape=[jax.ShapeDtypeStruct((rows, inner), F32)] * 3,
        compiler_params=pltpu.CompilerParams(vmem_limit_bytes=24 * MIB),
        name="gate",
    )(in_hbm(normed), in_hbm(upstream_b), in_hbm(w_z), in_hbm(w_out))


def key_query_of(one, two, rows, count):
    parts = []
    for c in range(rows // LANES):
        at = slice(rows + c * count, rows + (c + 1) * count)
        parts.append(one[at, :] + two[at, :])
    return jnp.transpose(jnp.concatenate(parts, axis=1))


def lay_tiles(dest, value, base=0):
    for j in range(SUB):
        dest[pl.ds(base * SUB + j, value.shape[0], stride=SUB), :] = value[
            :, j * LANES : (j + 1) * LANES
        ]


def lay_rows(source, count, j):
    return source[pl.ds(j, count, stride=SUB), :]


def spread(dest, key_query):
    rows, count = key_query.shape
    for n in range(count):
        dest[n * rows : (n + 1) * rows, :] = jnp.broadcast_to(
            key_query[:, n : n + 1], (rows, LANES)
        )


def pick(source, rows, n, t):
    return source[pl.ds(n * rows + t, SUB, stride=0), :]


def scan_kernel(
    unroll, one, two, mixed, wup, bias, silu, dgate, skip,
    gated, prez, step_out, raw_out, peak, hist, last, step_t, mix_t, out_t, kb, slots, sems,
):
    rows, inner = mixed.shape
    span = slots.shape[1]
    states = kb.shape[0] // rows // 2
    kq = key_query_of(one, two, rows, 2 * states)
    keys = kq[:, :states]
    norm = jnp.sum(keys * keys, axis=1, keepdims=True)
    spread(kb, kq)
    rank_b = (one[:rows, :] + two[:rows, :]).astype(BF16)
    raw = jax.nn.sigmoid(mm(rank_b, wup[...]) + bias[...])
    raw_out[...] = raw
    highest = jnp.max(jnp.max(raw, axis=0, keepdims=True), axis=1, keepdims=True)
    peak[...] = jnp.broadcast_to(highest, peak.shape)
    beta = raw.astype(BF16).astype(F32)
    size = beta / (1.0 + beta * norm)
    step_out[...] = size
    lay_tiles(step_t, size)
    lay_tiles(mix_t, mixed[...].astype(F32))

    def token(block, i, carried):
        t = block * span + i
        at = pl.ds(pl.multiple_of(t * SUB, SUB), SUB)
        size = step_t[at, :]
        mix = mix_t[at, :]
        sums = [None] * 4
        following = []
        for n in range(states):
            key = pick(kb, rows, n, t)
            query = pick(kb, rows, states + n, t)
            state = carried[n]
            slots[block % 2, i, n] = state
            state = state + (size * key) * (mix - key * state)
            term = query * state
            sums[n % 4] = term if sums[n % 4] is None else sums[n % 4] + term
            following.append(state)
        out_t[at, :] = (sums[0] + sums[1]) + (sums[2] + sums[3])
        return tuple(following)

    zero = jnp.zeros((SUB, LANES), F32)
    final = (zero,) * states
    copies = []
    for block in range(rows // span):
        if block >= 2:
            copies[block - 2].wait()
        final = lax.fori_loop(0, span, functools.partial(token, block), final, unroll=unroll)
        copies.append(
            pltpu.make_async_copy(
                slots.at[block % 2], hist.at[pl.ds(block * span, span)], sems.at[block % 2]
            )
        )
        copies[-1].start()
    for n in range(states):
        last[n] = final[n]
    for j in range(SUB):
        at = slice(j * LANES, (j + 1) * LANES)
        y = lay_rows(out_t, rows, j) + skip[:, at] * mixed[:, at].astype(F32)
        gated[:, at] = (y * silu[:, at]).astype(BF16)
        prez[:, at] = (y * dgate[:, at]).astype(BF16)
    for copy in copies[-2:]:
        copy.wait()


def scan_forward(summed, mixed, w_up, beta_bias, silu, dgate, skip_gain, states):
    rows, inner = mixed.shape
    full = lambda dtype: jax.ShapeDtypeStruct((rows, inner), dtype)
    return pl.pallas_call(
        functools.partial(scan_kernel, 4),
        in_specs=[WHOLE] * 8,
        out_specs=[WHOLE] * 5 + [pl.BlockSpec(memory_space=pl.ANY), WHOLE],
        out_shape=[
            pltpu.HBM((rows, inner), BF16),
            pltpu.HBM((rows, inner), BF16),
            full(F32),
            full(F32),
            jax.ShapeDtypeStruct((SUB, LANES), F32),
            pltpu.HBM((rows, states, SUB, LANES), F32),
            jax.ShapeDtypeStruct((states, SUB, LANES), F32),
        ],
        scratch_shapes=[pltpu.VMEM((rows * SUB, LANES), F32)] * 3
        + [
            pltpu.VMEM((2 * states * rows, LANES), F32),
            pltpu.VMEM((2, rows // 8, states, SUB, LANES), F32),
            pltpu.SemaphoreType.DMA((2,)),
        ],
        compiler_params=pltpu.CompilerParams(vmem_limit_bytes=22 * MIB),
        name="scan",
    )(*summed, mixed, in_hbm(w_up), in_hbm(beta_bias[None]), silu, dgate, in_hbm(skip_gain[None]))


def back_kernel(
    unroll, pins, place, one, two, mixed, wup, step_in, raw_in, gy, hist, last, peak, *rest, ):
    gmix, pay, ups, preb, step_t, mix_t, gs_t, kb, sum_d, sum_s, prods, zk, zq, slots, sems = rest[
        pins:
    ]
    rows, inner = mixed.shape
    states = last.shape[0]
    rank = wup.shape[0]
    span = zk.shape[0] // states
    chunk = slots.shape[1]
    chunks = rows // chunk

    def fetch(block):
        return pltpu.make_async_copy(
            hist.at[pl.ds(block * chunk, chunk)], slots.at[block % 2], sems.at[block % 2]
        )

    fetch(chunks - 1).start()
    fetch(chunks - 2).start()
    kq = key_query_of(one, two, rows, 2 * states)
    keys = kq[:, :states]
    norm = jnp.sum(keys * keys, axis=1, keepdims=True)
    spread(kb, kq)
    lay_tiles(step_t, step_in[...])
    lay_tiles(mix_t, mixed[...].astype(F32) * 0.5)
    gs_t[0:SUB, :] = jnp.zeros((SUB, LANES), F32)
    lay_tiles(gs_t, gy[...].astype(BF16).astype(F32), 1)

    def reduce_to(dest, row, terms, slot):
        base = slot * states * SUB
        for n in range(states):
            prods[pl.ds(base + n * SUB, SUB), :] = terms[n]
        for g in range(states // SUB):
            total = None
            for s in range(SUB):
                part = prods[pl.ds(base + g * SUB * SUB + s, SUB, stride=SUB), :]
                total = part if total is None else total + part
            dest[pl.ds(row + g * SUB * span, SUB, stride=span), :] = total

    tail = gs_t[pl.ds(rows * SUB, SUB), :]
    reduce_to(zq, rows, [last[n] * tail for n in range(states)], 0)

    def token(block, i, u, carried):
        t = block * chunk + i
        at = pl.ds(pl.multiple_of(t * SUB, SUB), SUB)
        size = step_t[at, :]
        half = mix_t[at, :]
        before = gs_t[at, :]
        grad = gs_t[pl.ds(pl.multiple_of(t * SUB + SUB, SUB), SUB), :]
        drive = size * half
        total_d, total_s = [None] * 2, [None] * 2
        following, for_key, for_query = [], [], []
        for n in range(states):
            key = pick(kb, rows, n, t)
            query = pick(kb, rows, states + n, t)
            state = slots[block % 2, i, n]
            full = query * grad + carried[n]
            by_key = full * key
            by_state = by_key * state
            term = key * by_state
            following.append(full - key * (size * by_key))
            for_key.append(full * drive - size * by_state)
            for_query.append(state * before)
            h = n % 2
            total_d[h] = by_key if total_d[h] is None else total_d[h] + by_key
            total_s[h] = term if total_s[h] is None else total_s[h] + term
        sum_d[at, :] = total_d[0] + total_d[1]
        sum_s[at, :] = total_s[0] + total_s[1]
        reduce_to(zk, t, for_key, 2 * u)
        reduce_to(zq, t, for_query, 2 * u + 1)
        return tuple(following)

    def some(block, i, carried):
        for u in range(unroll):
            carried = token(block, chunk - 1 - (i * unroll + u), u, carried)
        return carried

    zero = jnp.zeros((SUB, LANES), F32)
    carried = (zero,) * states
    for block in reversed(range(chunks)):
        fetch(block).wait()
        carried = lax.fori_loop(0, chunk // unroll, functools.partial(some, block), carried)
        if block >= 2:
            fetch(block - 2).start()

    total_norm = jnp.zeros((rows, 1), F32)
    for j in range(SUB):
        at = slice(j * LANES, (j + 1) * LANES)
        drive_grad = lay_rows(sum_d, rows, j)
        size = step_in[:, at]
        grad_step = drive_grad * mixed[:, at].astype(F32) - lay_rows(sum_s, rows, j)
        gmix[:, at] = drive_grad * size
        total_norm = total_norm - jnp.sum(grad_step * size * size, axis=1, keepdims=True)
        raw = raw_in[:, at]
        plus = 1.0 + raw.astype(BF16).astype(F32) * norm
        pre = grad_step / (plus * plus) * raw * (1.0 - raw)
        ups[rank : rank + SUB, at] = jnp.broadcast_to(
            jnp.sum(pre, axis=0, keepdims=True), (SUB, LANES)
        )
        preb[:, at] = pre.astype(BF16)
    pay[:rows, :] = mm_nt(preb[...], wup[...])
    rank_b = (one[:rows, :] + two[:rows, :]).astype(BF16)
    ups[:rank, :] = mm_tn(rank_b, preb[...])

    source = lax.broadcasted_iota(jnp.int32, (LANES, LANES), 1)
    lane = lax.broadcasted_iota(jnp.int32, (rows, LANES), 1)
    row = lax.broadcasted_iota(jnp.int32, (rows, LANES), 0)
    table = jnp.where(lane == 2 * states, jnp.broadcast_to(total_norm, (rows, LANES)), 0.0)
    mark = (lane == 2 * states + 1) & (row == place[1])
    table = jnp.where(mark, jnp.broadcast_to(peak[0:1, :], (rows, LANES)), table)
    for n in range(states):
        table = table + mm(
            zk[pl.ds(n * span, rows), :], jnp.where(source == n, 2.0, 0.0)
        )
        table = table + mm(
            zq[pl.ds(n * span + 1, rows), :], jnp.where(source == states + n, 1.0, 0.0)
        )
    flat = jnp.transpose(table)
    high = (pay.shape[0] - rows) * LANES // rows
    for c in range(rows // LANES):
        pay[rows + c * high : rows + (c + 1) * high, :] = flat[:high, c * LANES : (c + 1) * LANES]


def scan_backward(place, summed, mixed, w_up, step_in, raw, gy, hist, last, peak, pins):
    rows, inner = mixed.shape
    states = last.shape[0]
    unroll = 2
    span = rows + SUB
    high = 2 * states + SUB
    pay_rows = rows + high * rows // LANES
    return pl.pallas_call(
        functools.partial(back_kernel, unroll, len(pins)),
        in_specs=[pl.BlockSpec(memory_space=pltpu.SMEM)]
        + [WHOLE] * 7
        + [ANY]
        + [WHOLE] * 2
        + [ANY] * len(pins),
        out_specs=[WHOLE] * 3,
        out_shape=[
            pltpu.HBM((rows, inner), F32),
            jax.ShapeDtypeStruct((pay_rows, LANES), F32),
            pltpu.HBM((w_up.shape[0] + SUB, inner), F32),
        ],
        scratch_shapes=[
            pltpu.VMEM((rows, inner), BF16),
            pltpu.VMEM((rows * SUB, LANES), F32),
            pltpu.VMEM((rows * SUB, LANES), F32),
            pltpu.VMEM((rows * SUB + SUB, LANES), F32),
            pltpu.VMEM((2 * states * rows, LANES), F32),
            pltpu.VMEM((rows * SUB, LANES), F32),
            pltpu.VMEM((rows * SUB, LANES), F32),
            pltpu.VMEM((unroll * 2 * states * SUB, LANES), F32),
            pltpu.VMEM((states * span, LANES), F32),
            pltpu.VMEM((states * span, LANES), F32),
            pltpu.VMEM((2, rows // 8, states, SUB, LANES), F32),
            pltpu.SemaphoreType.DMA((2,)),
        ],
        compiler_params=pltpu.CompilerParams(vmem_limit_bytes=28 * MIB),
        name="back",
    )(
        place, *summed, mixed, in_hbm(w_up), step_in, raw, gy,
        in_hbm(hist), last, peak, *pins,
    )


def conv_kernel(
    pins, parts, place, one, two, grad_one, grad_two, mixed, gy, gmix, dsilu, prex, ups, cw, skip,
    wd, wk, *rest,
):
    prex_b, keep, send, table = rest[pins:]
    rows, inner = mixed.shape
    rank = wd.shape[1]
    count = wk.shape[0]
    states = count // 2
    high = (grad_one.shape[0] - rows) * LANES // rows
    kq = key_query_of(one, two, rows, count)
    gkq = key_query_of(grad_one, grad_two, rows, high)
    norm_grad = gkq[:, count : count + 1]
    peak = jnp.max(gkq[:, count + 1 : count + 2], axis=0, keepdims=True)
    peak_high = peak.astype(BF16).astype(F32)
    lane = lax.broadcasted_iota(jnp.int32, (rows, count), 1)
    kq_b = (gkq[:, :count] + jnp.where(lane < states, 2.0 * kq * norm_grad, 0.0)).astype(BF16)
    rank_b = (grad_one[:rows, :] + grad_two[:rows, :]).astype(BF16)
    taps = cw.shape[0]
    blk = 256
    first = 2 * rank + count
    table[:rank, :] = ups[:rank, :]
    table[rank : 2 * rank, :] = mm_tn(rank_b, mixed[...])
    table[2 * rank : first, :] = mm_tn(kq_b, mixed[...])
    for c in range(inner // blk):
        at = slice(c * blk, (c + 1) * blk)
        mix = mixed[:, at].astype(F32)
        grad_y = gy[:, at]
        total = grad_y * skip[:, at] + gmix[:, at]
        total = total + mm(kq_b, wk[:, at]) + mm_nt(rank_b, wd[at, :])
        grad = total * dsilu[:, at]
        pre = prex[:, at]
        row = lax.broadcasted_iota(jnp.int32, grad.shape, 0)
        out = None
        sums = []
        for j in range(taps):
            by = taps - 1 - j
            sums.append(jnp.sum(grad * shifted(pre, by, row), axis=0, keepdims=True))
            term = cw[j : j + 1, at] * shifted(grad, -by, row)
            out = term if out is None else out + term
        sums.append(jnp.sum(grad, axis=0, keepdims=True))
        sums.append(jnp.sum(grad_y * mix, axis=0, keepdims=True))
        sums.append(ups[rank : rank + 1, at])
        channel = lax.broadcasted_iota(jnp.int32, (1, blk), 1) + c * blk
        for value in (peak_high, peak - peak_high):
            sums.append(jnp.where(channel == place[0], jnp.broadcast_to(value, (1, blk)), 0.0))
        for i, line in enumerate(sums):
            table[first + i : first + i + 1, at] = line
        prex_b[:, at] = out.astype(BF16)
    table[first + len(sums) :, :] = jnp.zeros((table.shape[0] - first - len(sums), inner), F32)
    size = table.shape[0] // parts
    if parts != 8:
        keep[...] = table[...]
        return
    for dest, order in ((keep, (0, 4, 2, 6)), (send, (1, 5, 3, 7))):
        for i, p in enumerate(order):
            at = pl.ds(pl.multiple_of((place[0] ^ p) * size, SUB), size)
            dest[i] = table[at, :].astype(dest.dtype)


def conv_back(
    place, summed, grads, mixed, gy, gmix, dsilu, prex, ups, conv_weight, skip_gain, w_down,
    w_keyq, parts, pins,
):
    rows, inner = mixed.shape
    table = (8 * SMALL, inner)
    half = (4, SMALL, inner) if parts == 8 else table
    return pl.pallas_call(
        functools.partial(conv_kernel, len(pins), parts),
        in_specs=[pl.BlockSpec(memory_space=pltpu.SMEM)] + [WHOLE] * 14 + [ANY] * len(pins),
        out_specs=[WHOLE] * 3,
        out_shape=[
            pltpu.HBM((rows, inner), BF16),
            pltpu.HBM(half, F32),
            pltpu.HBM(half, BF16),
        ],
        scratch_shapes=[pltpu.VMEM(table, F32)],
        compiler_params=pltpu.CompilerParams(vmem_limit_bytes=26 * MIB),
        name="conv",
    )(
        place, *summed, *grads, mixed, gy, gmix, dsilu, prex, ups, in_hbm(conv_weight),
        in_hbm(skip_gain[None]), in_hbm(w_down), in_hbm(w_keyq), *pins,
    )


def unpack_kernel(place, rank, count, taps, g0, g1, g2, g3, up, down, keyq, lines, table):
    size = g0.shape[0]
    pieces = [(0, g0, 0), (4, g1, 0), (2, g2, 0), (6, g2, 1)]
    pieces += [(p, g3, i) for i, p in enumerate((1, 5, 3, 7))]
    for p, source, i in pieces:
        at = pl.ds(pl.multiple_of((place[0] ^ p) * size, SUB), size)
        table[at, :] = source[i * size : (i + 1) * size, :].astype(F32)
    up[...] = table[:rank, :]
    down[...] = jnp.transpose(table[rank : 2 * rank, :])
    keyq[...] = table[2 * rank : 2 * rank + count, :]
    first = 2 * rank + count
    lines[...] = table[first : first + lines.shape[0], :]


def unpack(place, pieces, rank, count, taps):
    inner = pieces[0].shape[1]
    kernel = lambda place, *refs: unpack_kernel(place, rank, count, taps, *refs)
    return pl.pallas_call(
        kernel,
        in_specs=[pl.BlockSpec(memory_space=pltpu.SMEM)] + [WHOLE] * 4,
        out_specs=[WHOLE] * 4,
        out_shape=[
            jax.ShapeDtypeStruct((rank, inner), F32),
            jax.ShapeDtypeStruct((inner, rank), F32),
            jax.ShapeDtypeStruct((count, inner), F32),
            jax.ShapeDtypeStruct((2 * SUB, inner), F32),
        ],
        scratch_shapes=[pltpu.VMEM((8 * SMALL, inner), F32)],
        compiler_params=pltpu.CompilerParams(vmem_limit_bytes=16 * MIB),
        name="unpack",
    )(place, *pieces)


def branch_kernel(place, gated, wo, tok, send, keep):
    i = pl.program_id(0)
    value = mm(gated[...], wo[...])

    @pl.when(i == 0)
    def _():
        keep[0] = value + tok[...].astype(F32)

    @pl.when(i == 2)
    def _():
        keep[0] = value

    @pl.when(i % 2 == 1)
    def _():
        send[0, 0] = value.astype(BF16)


def branch(place, gated, w_out, tokens, parts):
    rows, inner = gated.shape
    width = w_out.shape[1]
    own = width // parts
    return pl.pallas_call(
        branch_kernel,
        grid_spec=pltpu.PrefetchScalarGridSpec(
            num_scalar_prefetch=1,
            grid=(parts,),
            in_specs=[
                pl.BlockSpec((rows, inner), lambda i, place: (0, 0)),
                pl.BlockSpec((inner, own), lambda i, place: (0, place[1] ^ i)),
                pl.BlockSpec((rows, own), lambda i, place: (0, place[1])),
            ],
            out_specs=[
                pl.BlockSpec((1, 1, rows, own), lambda i, place: (i // 2, 0, 0, 0)),
                pl.BlockSpec((1, rows, own), lambda i, place: (i // 2, 0, 0)),
            ],
        ),
        out_shape=[
            pltpu.HBM((parts // 2, 2, rows, own), BF16),
            pltpu.HBM((parts // 2, rows, own), F32),
        ],
        compiler_params=pltpu.CompilerParams(vmem_limit_bytes=16 * MIB),
        name="branch",
    )(place, in_hbm(gated), in_hbm(w_out), in_hbm(tokens))


def input_kernel(
    place, ids, weights, half_sent, prex, prez, wx, wz, tok, tok_own, cot, gain,
    send, keep, stats, slope, shift, base, inv, dots,
):
    i = pl.program_id(0)
    rows, width = tok.shape

    @pl.when(i == 0)
    def _():
        value = tok[...].astype(F32)
        inv[...] = jnp.broadcast_to(
            lax.rsqrt(jnp.mean(value * value, axis=1, keepdims=True) + EPS), inv.shape
        )
        dots[...] = jnp.zeros_like(dots)

    value = mm_nt(prex[...], wx[...]) + mm_nt(prez[...], wz[...])
    rms = inv[:, 0:1]
    unit = tok_own[...].astype(F32) * rms
    by_unit = value * unit
    dots[...] += jnp.sum(by_unit * gain[...], axis=1, keepdims=True)
    line = jnp.sum(by_unit, axis=0, keepdims=True)
    own = line.shape[1] // LANES
    first = rows // LANES + (place[1] ^ i) * own
    for j in range(own):
        stats[pl.ds(first + j, 1), :] = line[:, j * LANES : (j + 1) * LANES]

    @pl.when(i == 0)
    def _():
        slope[...] = rms * gain[...]
        shift[...] = unit * rms * (1.0 / width)
        base[...] = cot[...].astype(F32) * weights[ids[0]]

    @pl.when(i % 2 == 0)
    def _():
        keep[0] = value

    @pl.when(i % 2 == 1)
    def _():
        send[0, 0] = value.astype(BF16)

    @pl.when(i == pl.num_programs(0) - 1)
    def _():
        flat = jnp.transpose(dots[...])
        for c in range(rows // LANES):
            stats[c : c + 1, :] = flat[0:1, c * LANES : (c + 1) * LANES]


def input_grad(
    place, group_ids, group_weights, half_sent, prex, prez, w_x, w_z, tokens, cotangent, norm_gain,
    parts,
):
    rows, inner = prex.shape
    width = tokens.shape[1]
    own = width // parts
    whole = lambda shape: pl.BlockSpec(shape, lambda i, place: (0, 0))
    part = pl.BlockSpec((own, inner), lambda i, place: (place[1] ^ i, 0))
    mine = pl.BlockSpec((rows, own), lambda i, place: (0, 0))
    smem = pl.BlockSpec(memory_space=pltpu.SMEM)
    stat_rows = rows // LANES + width // LANES
    return pl.pallas_call(
        input_kernel,
        grid_spec=pltpu.PrefetchScalarGridSpec(
            num_scalar_prefetch=1,
            grid=(parts,),
            in_specs=[
                smem,
                smem,
                ANY,
                whole((rows, inner)),
                whole((rows, inner)),
                part,
                part,
                whole((rows, width)),
                pl.BlockSpec((rows, own), lambda i, place: (0, place[1] ^ i)),
                pl.BlockSpec((rows, own), lambda i, place: (0, place[1])),
                pl.BlockSpec((1, own), lambda i, place: (0, place[1] ^ i)),
            ],
            out_specs=[
                pl.BlockSpec((1, 1, rows, own), lambda i, place: (i // 2, 1, 0, 0)),
                pl.BlockSpec((1, rows, own), lambda i, place: (i // 2, 0, 0)),
            ]
            + [whole((stat_rows, LANES)), mine, mine, mine],
            scratch_shapes=[pltpu.VMEM((rows, LANES), F32)] * 2,
        ),
        out_shape=[
            pltpu.HBM((parts // 2, 2, rows, own), BF16),
            pltpu.HBM((parts // 2, rows, own), F32),
            jax.ShapeDtypeStruct((stat_rows, LANES), F32),
        ]
        + [pltpu.HBM((rows, own), F32)] * 3,
        compiler_params=pltpu.CompilerParams(vmem_limit_bytes=24 * MIB),
        input_output_aliases={3: 0},
        name="inputs",
    )(
        place, group_ids, group_weights, in_hbm(half_sent), in_hbm(prex), in_hbm(prez), in_hbm(w_x), in_hbm(w_z), in_hbm(tokens),
        in_hbm(tokens), in_hbm(cotangent), in_hbm(norm_gain[None]),
    )


def out_weight_kernel(pins, l0, l1, r0, r1, *rest):
    keep, later, send = rest[pins:]
    own = keep.shape[1]
    total = mm_tn(l0[...], r0[...]) + mm_tn(l1[...], r1[...])
    keep[...] = total[:, :own]
    later[...] = total[:, own : 2 * own]
    send[...] = total[:, 2 * own :].astype(BF16)


def out_weight(lefts, rights, pins):
    rows, inner = lefts[0].shape
    own = rights[0].shape[1] // 4
    blk = 256
    whole = lambda value: pl.BlockSpec(value.shape, lambda i: (0,) * value.ndim)
    down = lambda wide: pl.BlockSpec((blk, wide), lambda i: (i, 0))
    return pl.pallas_call(
        functools.partial(out_weight_kernel, len(pins)),
        grid=(inner // blk,),
        in_specs=[pl.BlockSpec((rows, blk), lambda i: (0, i))] * 2
        + [whole(r) for r in rights]
        + [ANY] * len(pins),
        out_specs=[down(own), down(own), down(2 * own)],
        out_shape=[
            pltpu.HBM((inner, own), F32),
            pltpu.HBM((inner, own), F32),
            pltpu.HBM((inner, 2 * own), BF16),
        ],
        compiler_params=pltpu.CompilerParams(vmem_limit_bytes=20 * MIB),
        name="outw",
    )(*[in_hbm(value) for value in (*lefts, *rights)], *pins)


def in_weight_kernel(l0, l1, l2, l3, r0, r1, r2, r3, keep, send):
    i = pl.program_id(0)
    total = None
    for left, right in ((l0[...], r0), (l1[0], r1), (l2[...], r2), (l3[...], r3)):
        term = mm_tn(left, right[...])
        total = term if total is None else total + term

    @pl.when(i == 0)
    def _():
        send[...] = total.astype(BF16)

    @pl.when(i == 1)
    def _():
        keep[...] = total


def in_weight(lefts, rights):
    rows, inner = rights[0].shape
    own = lefts[0].shape[1] // 2
    whole = lambda value: pl.BlockSpec(value.shape, lambda i: (0,) * value.ndim)
    side = pl.BlockSpec((rows, own), lambda i: (0, 1 - i))
    return pl.pallas_call(
        in_weight_kernel,
        grid=(2,),
        in_specs=[side, pl.BlockSpec((1, rows, own), lambda i: (0, 0, 1 - i)), side, side]
        + [whole(r) for r in rights],
        out_specs=[pl.BlockSpec((own, inner), lambda i: (0, 0))] * 2,
        out_shape=[
            pltpu.HBM((own, inner), F32),
            pltpu.HBM((own, inner), BF16),
        ],
        compiler_params=pltpu.CompilerParams(vmem_limit_bytes=20 * MIB),
        name="inw",
    )(*[in_hbm(value) for value in (*lefts, *rights)])


def split_bits(axis):
    bits = bits_of(axis)
    return [bit for bit in (2, 1) if bit in bits], [bit for bit in reversed(bits) if bit > 2]


def gather_tokens(value, axis):
    pieces = [value]
    for bit in split_bits(axis)[0]:
        pieces = pieces + [swap(piece, axis, bit) for piece in pieces]
    return pieces


def exchange_cols(value, axis):
    size = lax.axis_size(axis)
    me = lax.axis_index(axis)
    gather, scatter = split_bits(axis)
    rows, cols = value.shape
    outer = 2 ** len(scatter)
    pieces = [value.reshape((rows, outer) + (2,) * len(gather) + (cols // size,))]
    for bit in gather:
        kept, sent = zip(*(halves(piece, 2, (me // bit) % 2) for piece in pieces))
        pieces = list(kept) + [swap(piece, axis, bit) for piece in sent]
    return [piece.reshape(rows, -1) for piece in pieces]


def scatter_sum(value, axis, dim):
    me = lax.axis_index(axis)
    scatter = split_bits(axis)[1]
    for bit in scatter:
        shape = value.shape
        split = shape[:dim] + (2, shape[dim] // 2) + shape[dim + 1 :]
        kept, sent = halves(value.reshape(split), dim, (me // bit) % 2)
        value = kept + swap(sent.astype(BF16), axis, bit).astype(F32)
    return value


def per_device(
    tokens,
    norm_gain,
    w_x,
    w_z,
    conv_weight,
    conv_bias,
    w_down,
    w_up,
    beta_bias,
    w_keyq,
    skip_gain,
    w_out,
    cotangent,
    group_ids,
    group_weights,
):
    rows, width = tokens.shape
    states = w_keyq.shape[1] // 2
    taps = conv_weight.shape[0]
    assert group_ids.shape[0] == 1
    parts = lax.axis_size("state")
    assert parts == 4
    dp_size = lax.axis_size("dp")
    own_width = width // parts
    state_index = lax.axis_index("state")
    place = jnp.stack([lax.axis_index("dp"), state_index]).astype(jnp.int32)
    blocked = dp_size if dp_size == 8 and width % (8 * LANES) == 0 else 0
    keyq_t = w_keyq.T

    normed, upstream_b, pre_x, mixed_b, dsilu, part, *blocks = front(
        place, group_ids, group_weights, tokens, cotangent, norm_gain, w_x,
        conv_weight, conv_bias, w_down, keyq_t, blocked,
    )
    summed = all_but_last(part, "state")
    pins_back = pins_conv = ()
    if blocked:
        far, near, own, up_far, up_own = blocks
        far = swap(far, "dp", 2)
        near = swap(near, "dp", 1)
        up_far = swap(up_far, "dp", 4)
        pins_back = (far, near)
    else:
        norm_parts = exchange_cols(normed, "dp")
        up_parts = exchange_cols(upstream_b, "dp")
    silu_z, dgate, grad_y = gate(normed, upstream_b, w_z, w_out)

    gated_b, prez_b, step_size, raw, peak, hist, last = scan_forward(
        summed, mixed_b, w_up, beta_bias, silu_z, dgate, skip_gain, states
    )
    if blocked:
        gated_far = swap(gated_b, "dp", 4)
        prez_far = swap(prez_b, "dp", 2)
        prez_near = swap(prez_b, "dp", 1)
        sides = (own, far, near, swap(far[1], "dp", 1))
        pins_conv = (gated_far, prez_far, prez_near, up_far, sides[3])

    gmix, pay, ups = scan_backward(
        place, summed, mixed_b, w_up, step_size, raw, grad_y, hist, last, peak, pins_back
    )
    grads = all_but_last(pay, "state")
    half_sent, out_keep = branch(place, gated_b, w_out, tokens, parts)

    prex_b, small, small_send = conv_back(
        place, summed, grads, mixed_b, grad_y, gmix, dsilu, pre_x, ups, conv_weight, skip_gain,
        w_down, keyq_t, dp_size, pins_conv,
    )

    def in_grad(value, far, near):
        pieces = (value, far, near, swap(far, "dp", 1))
        keep, send = in_weight(sides, pieces)
        return keep + swap(send, "dp", 4).astype(F32)

    if blocked:
        prex_far = swap(prex_b, "dp", 2)
        prex_near = swap(prex_b, "dp", 1)
        keep, later, send = out_weight((gated_b, gated_far), (up_own, up_far), ())
        come = swap(send, "dp", 1).astype(F32)
        cut = later.shape[1]
        come_far = swap((later + come[:, cut:]).astype(BF16), "dp", 2)
        grad_wout = keep + come[:, :cut] + come_far.astype(F32)
        grad_wz = in_grad(prez_b, prez_far, prez_near)
        grad_wx = in_grad(prex_b, prex_far, prex_near)
    else:

        def weight_grad(value, left):
            pieces = gather_tokens(value, "dp")
            pairs = zip(pieces, up_parts) if left else zip(norm_parts, pieces)
            return scatter_sum(sum(mm_tn(a, b) for a, b in pairs), "dp", 1 if left else 0)

        grad_wout = weight_grad(gated_b, True)
        grad_wz = weight_grad(prez_b, False)
        grad_wx = weight_grad(prex_b, False)

    send, keep, stats, slope, shift, base = input_grad(
        place, group_ids, group_weights, half_sent, prex_b, prez_b, w_x, w_z, tokens, cotangent,
        norm_gain, parts,
    )
    come = swap(send, "state", 1)
    pair = jnp.stack([out_keep[1], keep[1]]) + come[1].astype(F32)
    come_far = swap(pair.astype(BF16), "state", 2).astype(F32)
    block_out = (out_keep[0] + come[0, 0].astype(F32) + come_far[0]).astype(BF16)
    norm_grad = keep[0] + come[0, 1].astype(F32) + come_far[1]
    stats = all_sum(stats, "state")
    row_stat = stats[: rows // LANES].reshape(rows, 1)
    grad_in = norm_grad * slope - shift * row_stat + base
    gain_rows = own_width // LANES
    gain = lax.dynamic_slice_in_dim(
        stats, rows // LANES + state_index * gain_rows, gain_rows, 0
    )

    count = 2 * states
    rank = w_up.shape[0]
    if blocked:
        small = small + swap(small_send, "dp", 1).astype(F32)
        small = small[:2] + swap(small[2:].astype(BF16), "dp", 2).astype(F32)
        small = small[0] + swap(small[1].astype(BF16), "dp", 4).astype(F32)
        pieces = [small.astype(BF16)]
        gathered = pieces[0]
        for bit in (4, 2, 1):
            high = lax.reduce_precision(gain, 8, 7)
            rest = lax.reduce_precision(gain - high, 8, 7)
            line = jnp.concatenate([high.reshape(1, -1), rest.reshape(1, -1)], axis=1)
            tail = jnp.pad(line.astype(BF16), ((0, SUB - 1), (0, 0)))
            come = swap(jnp.concatenate([gathered, tail], axis=0), "dp", bit)
            pieces.append(come[:-SUB])
            gathered = jnp.concatenate([gathered, come[:-SUB]], axis=0)
            other = come[-SUB].astype(F32)
            gain = (high + rest) + (other[:own_width] + other[own_width:]).reshape(gain.shape)
        grad_gain = gain.reshape(-1)
        grad_up, down, keyq, lines = unpack(place, pieces, rank, count, taps)
    else:
        small = all_sum(small, "dp")
        grad_up = small[:rank]
        down = small[rank : 2 * rank].T
        keyq = small[2 * rank : 2 * rank + count]
        lines = small[2 * rank + count :]
        grad_gain = all_sum(gain, "dp").reshape(-1)
    return (
        block_out,
        grad_in,
        grad_gain,
        grad_wx,
        grad_wz,
        lines[:taps],
        lines[taps],
        down,
        grad_up,
        lines[taps + 2],
        keyq.T,
        lines[taps + 1],
        grad_wout,
        jnp.max(lines[taps + 3] + lines[taps + 4]),
    )


def solution(mesh):
    placed = (
        P("dp", None),
        P(),
        P(None, "state"),
        P(None, "state"),
        P(None, "state"),
        P("state"),
        P("state", None),
        P(None, "state"),
        P("state"),
        P("state", None),
        P("state"),
        P("state", None),
        P("dp", None),
        P("dp"),
        P(),
    )
    return jax.shard_map(
        per_device,
        mesh=mesh,
        in_specs=placed,
        out_specs=(
            P("dp", "state"),
            P("dp", "state"),
            P("state"),
            P("dp", "state"),
            P("dp", "state"),
            P(None, "state"),
            P("state"),
            P("state", None),
            P(None, "state"),
            P("state"),
            P("state", None),
            P("state"),
            P("state", "dp"),
            P(),
        ),
        check_vma=False,
    )
```

```python
import functools

import jax
import jax.numpy as jnp
from jax import lax
from jax.experimental import pallas as pl
from jax.experimental.pallas import tpu as pltpu
from jax.sharding import PartitionSpec as P

EPS = 1e-05
LANES = 128
SUB = 8
F32 = jnp.float32
BF16 = jnp.bfloat16
MIB = 2**20
WHOLE = pl.BlockSpec(memory_space=pltpu.VMEM)
ANY = pl.BlockSpec(memory_space=pl.ANY)
SMALL = 40


def mm(left, right):
    return jnp.dot(left, right, preferred_element_type=F32)


def mm_nt(left, right):
    return lax.dot_general(left, right, (((1,), (1,)), ((), ())), preferred_element_type=F32)


def mm_tn(left, right):
    return lax.dot_general(left, right, (((0,), (0,)), ((), ())), preferred_element_type=F32)


def swap(value, axis, bit):
    size = lax.axis_size(axis)
    return lax.ppermute(value, axis, [(i, i ^ bit) for i in range(size)])


def bits_of(axis):
    size = lax.axis_size(axis)
    bits, bit = [], 1
    while bit < size:
        bits.append(bit)
        bit *= 2
    return bits


def all_sum(value, axis):
    for bit in bits_of(axis):
        value = value + swap(value, axis, bit)
    return value


def all_max(value, axis):
    for bit in bits_of(axis):
        value = jnp.maximum(value, swap(value, axis, bit))
    return value


def halves(value, dim, bit_set):
    kept = lax.dynamic_index_in_dim(value, bit_set, dim, keepdims=False)
    sent = lax.dynamic_index_in_dim(value, 1 - bit_set, dim, keepdims=False)
    return kept, sent


def all_but_last(value, axis):
    bits = bits_of(axis)
    for bit in bits[:-1]:
        value = value + swap(value, axis, bit)
    return value, swap(value, axis, bits[-1])


def after(values, pins):
    def nothing(*refs):
        pass

    return pl.pallas_call(
        nothing,
        in_specs=[ANY] * (len(values) + len(pins)),
        out_specs=[ANY] * len(values),
        out_shape=[jax.ShapeDtypeStruct(value.shape, value.dtype) for value in values],
        input_output_aliases={i: i for i in range(len(values))},
        name="after",
    )(*values, *pins)


def in_hbm(value):
    return pltpu.with_memory_space_constraint(value, pltpu.HBM)


def shifted(value, by, rows):
    if by == 0:
        return value
    count = value.shape[0]
    moved = pltpu.roll(value, by % count, 0)
    keep = rows >= by if by > 0 else rows < count + by
    return jnp.where(keep, moved, 0.0)


def front_kernel(
    blocked, place, ids, weights, tok, cot, gain, wx, cw, cb, wd, wk,
    normed, up, prex, mixed, dsilu, part, *rest,
):
    step = pl.program_id(0)
    rows, width = tok.shape
    acc = rest[-1]

    @pl.when(step == 0)
    def _():
        value = tok[...].astype(F32)
        inv = lax.rsqrt(jnp.mean(value * value, axis=1, keepdims=True) + EPS)
        normed[...] = (value * inv * gain[...]).astype(BF16)
        part[...] = jnp.zeros_like(part)
        acc[...] = jnp.zeros_like(acc)

    pre = mm(normed[...], wx[...])
    prex[...] = pre
    row = lax.broadcasted_iota(jnp.int32, pre.shape, 0)
    taps = cw.shape[0]
    conv = cb[...] + sum(cw[j : j + 1, :] * shifted(pre, taps - 1 - j, row) for j in range(taps))
    sig = jax.nn.sigmoid(conv)
    mix = (conv * sig).astype(BF16)
    mixed[...] = mix
    dsilu[...] = sig * (1.0 + conv * (1.0 - sig))
    part[:rows, :] += mm(mix, wd[...])
    acc[...] += mm_nt(wk[...], mix)

    @pl.when(step == pl.num_programs(0) - 1)
    def _():
        wide = acc.shape[0]
        for c in range(rows // LANES):
            part[rows + c * wide : rows + (c + 1) * wide, :] = acc[:, c * LANES : (c + 1) * LANES]
        up[...] = (cot[...].astype(F32) * weights[ids[0]]).astype(BF16)
        if blocked:
            far, near, own, up_far, up_own = rest[:5]
            size = width // blocked
            for p in range(blocked):
                cols = pl.ds(pl.multiple_of((place[0] ^ p) * size, size), size)
                dest = near.at[p >> 1 & 1] if p & 1 else (far if p & 2 else own)
                dest[:, (p // 4) * size : (p // 4 + 1) * size] = normed[:, cols]
                at = (p & 1) * 2 + (p >> 1 & 1)
                at = slice(at * size, (at + 1) * size)
                if p & 4:
                    half = rows // 2
                    some = pl.ds(pl.multiple_of((place[1] & 1) * half, half), half)
                    up_far[:, at] = up[some, cols]
                else:
                    up_own[:, at] = up[:, cols]


def front(
    place, group_ids, group_weights, tokens, cotangent, norm_gain, w_x,
    conv_weight, conv_bias, w_down, w_keyq, blocked,
):
    rows, width = tokens.shape
    inner = w_x.shape[1]
    rank, kq = w_down.shape[1], w_keyq.shape[0]
    blk = min(inner, 256)
    whole = lambda shape: pl.BlockSpec(shape, lambda i: (0,) * len(shape))
    cols = lambda height: pl.BlockSpec((height, blk), lambda i: (0, i))
    smem = pl.BlockSpec(memory_space=pltpu.SMEM)
    part_rows = rows + kq * rows // LANES
    shapes = []
    if blocked:
        quarter, half = width // 4, width // 2
        shapes = [(rows, quarter), (2, rows, quarter), (rows, quarter), (rows // 2, half)]
        shapes += [(rows, half)]
    return pl.pallas_call(
        functools.partial(front_kernel, blocked),
        grid=(inner // blk,),
        in_specs=[
            smem,
            smem,
            smem,
            whole((rows, width)),
            whole((rows, width)),
            whole((1, width)),
            cols(width),
            cols(conv_weight.shape[0]),
            cols(1),
            pl.BlockSpec((blk, rank), lambda i: (i, 0)),
            cols(kq),
        ],
        out_specs=[
            whole((rows, width)),
            whole((rows, width)),
            cols(rows),
            cols(rows),
            cols(rows),
            whole((part_rows, LANES)),
        ]
        + [whole(shape) for shape in shapes],
        out_shape=[
            pltpu.HBM((rows, width), BF16),
            pltpu.HBM((rows, width), BF16),
            pltpu.HBM((rows, inner), F32),
            pltpu.HBM((rows, inner), BF16),
            pltpu.HBM((rows, inner), F32),
            jax.ShapeDtypeStruct((part_rows, LANES), F32),
        ]
        + [pltpu.HBM(shape, BF16) for shape in shapes],
        scratch_shapes=[pltpu.VMEM((kq, rows), F32)],
        compiler_params=pltpu.CompilerParams(vmem_limit_bytes=26 * MIB),
        name="front",
    )(
        place, group_ids, group_weights, in_hbm(tokens), in_hbm(cotangent),
        in_hbm(norm_gain[None]), in_hbm(w_x), in_hbm(conv_weight), in_hbm(conv_bias[None]),
        in_hbm(w_down), in_hbm(w_keyq),
    )


def gate_kernel(normed, up, wz, wo, silu, dgate, gy):
    pre = mm(normed[...], wz[...])
    back = mm_nt(up[...], wo[...])
    sig = jax.nn.sigmoid(pre)
    act = pre * sig
    silu[...] = act
    gy[...] = back * act
    dgate[...] = back * sig * (1.0 + pre * (1.0 - sig))


def gate(normed, upstream_b, w_z, w_out):
    rows, width = normed.shape
    inner = w_z.shape[1]
    blk = min(inner, 256)
    whole = lambda shape: pl.BlockSpec(shape, lambda i: (0, 0))
    cols = lambda height: pl.BlockSpec((height, blk), lambda i: (0, i))
    return pl.pallas_call(
        gate_kernel,
        grid=(inner // blk,),
        in_specs=[
            whole((rows, width)),
            whole((rows, width)),
            cols(width),
            pl.BlockSpec((blk, width), lambda i: (i, 0)),
        ],
        out_specs=[cols(rows)] * 3,
        out_shape=[jax.ShapeDtypeStruct((rows, inner), F32)] * 2 + [pltpu.HBM((rows, inner), F32)],
        compiler_params=pltpu.CompilerParams(vmem_limit_bytes=24 * MIB),
        name="gate",
    )(in_hbm(normed), in_hbm(upstream_b), in_hbm(w_z), in_hbm(w_out))


def key_query_of(one, two, rows, count):
    parts = []
    for c in range(rows // LANES):
        at = slice(rows + c * count, rows + (c + 1) * count)
        parts.append(one[at, :] + two[at, :])
    return jnp.transpose(jnp.concatenate(parts, axis=1))


def lay_tiles(dest, value, base=0):
    for j in range(SUB):
        dest[pl.ds(base * SUB + j, value.shape[0], stride=SUB), :] = value[
            :, j * LANES : (j + 1) * LANES
        ]


def lay_rows(source, count, j):
    return source[pl.ds(j, count, stride=SUB), :]


def spread(dest, key_query):
    rows, count = key_query.shape
    for n in range(count):
        dest[n * rows : (n + 1) * rows, :] = jnp.broadcast_to(
            key_query[:, n : n + 1], (rows, LANES)
        )


def pick(source, rows, n, t):
    return source[pl.ds(n * rows + t, SUB, stride=0), :]


def scan_kernel(
    unroll, one, two, mixed, wup, bias, silu, dgate, skip,
    gated, prez, step_out, raw_out, peak, hist, last, step_t, mix_t, out_t, kb, slots, sems,
):
    rows, inner = mixed.shape
    span = slots.shape[1]
    states = kb.shape[0] // rows // 2
    kq = key_query_of(one, two, rows, 2 * states)
    keys = kq[:, :states]
    norm = jnp.sum(keys * keys, axis=1, keepdims=True)
    spread(kb, kq)
    rank_b = (one[:rows, :] + two[:rows, :]).astype(BF16)
    raw = jax.nn.sigmoid(mm(rank_b, wup[...]) + bias[...])
    raw_out[...] = raw
    highest = jnp.max(jnp.max(raw, axis=0, keepdims=True), axis=1, keepdims=True)
    peak[...] = jnp.broadcast_to(highest, peak.shape)
    beta = raw.astype(BF16).astype(F32)
    size = beta / (1.0 + beta * norm)
    step_out[...] = size
    lay_tiles(step_t, size)
    lay_tiles(mix_t, mixed[...].astype(F32))

    def token(block, i, carried):
        t = block * span + i
        at = pl.ds(pl.multiple_of(t * SUB, SUB), SUB)
        size = step_t[at, :]
        mix = mix_t[at, :]
        sums = [None] * 4
        following = []
        for n in range(states):
            key = pick(kb, rows, n, t)
            query = pick(kb, rows, states + n, t)
            state = carried[n]
            slots[block % 2, i, n] = state
            state = state + (size * key) * (mix - key * state)
            term = query * state
            sums[n % 4] = term if sums[n % 4] is None else sums[n % 4] + term
            following.append(state)
        out_t[at, :] = (sums[0] + sums[1]) + (sums[2] + sums[3])
        return tuple(following)

    zero = jnp.zeros((SUB, LANES), F32)
    final = (zero,) * states
    copies = []
    for block in range(rows // span):
        if block >= 2:
            copies[block - 2].wait()
        final = lax.fori_loop(0, span, functools.partial(token, block), final, unroll=unroll)
        copies.append(
            pltpu.make_async_copy(
                slots.at[block % 2], hist.at[pl.ds(block * span, span)], sems.at[block % 2]
            )
        )
        copies[-1].start()
    for n in range(states):
        last[n] = final[n]
    for j in range(SUB):
        at = slice(j * LANES, (j + 1) * LANES)
        y = lay_rows(out_t, rows, j) + skip[:, at] * mixed[:, at].astype(F32)
        gated[:, at] = (y * silu[:, at]).astype(BF16)
        prez[:, at] = (y * dgate[:, at]).astype(BF16)
    for copy in copies[-2:]:
        copy.wait()


def scan_forward(summed, mixed, w_up, beta_bias, silu, dgate, skip_gain, states):
    rows, inner = mixed.shape
    full = lambda dtype: jax.ShapeDtypeStruct((rows, inner), dtype)
    return pl.pallas_call(
        functools.partial(scan_kernel, 4),
        in_specs=[WHOLE] * 8,
        out_specs=[WHOLE] * 5 + [pl.BlockSpec(memory_space=pl.ANY), WHOLE],
        out_shape=[
            pltpu.HBM((rows, inner), BF16),
            pltpu.HBM((rows, inner), BF16),
            full(F32),
            full(F32),
            jax.ShapeDtypeStruct((SUB, LANES), F32),
            pltpu.HBM((rows, states, SUB, LANES), F32),
            jax.ShapeDtypeStruct((states, SUB, LANES), F32),
        ],
        scratch_shapes=[pltpu.VMEM((rows * SUB, LANES), F32)] * 3
        + [
            pltpu.VMEM((2 * states * rows, LANES), F32),
            pltpu.VMEM((2, rows // 4, states, SUB, LANES), F32),
            pltpu.SemaphoreType.DMA((2,)),
        ],
        compiler_params=pltpu.CompilerParams(vmem_limit_bytes=26 * MIB),
        name="scan",
    )(*summed, in_hbm(mixed), in_hbm(w_up), in_hbm(beta_bias[None]), silu, dgate, in_hbm(skip_gain[None]))


def back_kernel(
    unroll, pins, place, one, two, mixed, wup, step_in, raw_in, gy, hist, last, peak, *rest, ):
    gmix, pay, ups, preb, step_t, mix_t, gs_t, kb, sum_d, sum_s, prods, zk, zq, slots, sems = rest[
        pins:
    ]
    rows, inner = mixed.shape
    states = last.shape[0]
    rank = wup.shape[0]
    span = zk.shape[0] // states
    chunk = slots.shape[1]
    chunks = rows // chunk

    def fetch(block):
        return pltpu.make_async_copy(
            hist.at[pl.ds(block * chunk, chunk)], slots.at[block % 2], sems.at[block % 2]
        )

    fetch(chunks - 1).start()
    fetch(chunks - 2).start()
    kq = key_query_of(one, two, rows, 2 * states)
    keys = kq[:, :states]
    norm = jnp.sum(keys * keys, axis=1, keepdims=True)
    spread(kb, kq)
    lay_tiles(step_t, step_in[...])
    lay_tiles(mix_t, mixed[...].astype(F32) * 0.5)
    gs_t[0:SUB, :] = jnp.zeros((SUB, LANES), F32)
    lay_tiles(gs_t, gy[...].astype(BF16).astype(F32), 1)

    def reduce_to(dest, row, terms, slot):
        base = slot * states * SUB
        for n in range(states):
            prods[pl.ds(base + n * SUB, SUB), :] = terms[n]
        for g in range(states // SUB):
            total = None
            for s in range(SUB):
                part = prods[pl.ds(base + g * SUB * SUB + s, SUB, stride=SUB), :]
                total = part if total is None else total + part
            dest[pl.ds(row + g * SUB * span, SUB, stride=span), :] = total

    tail = gs_t[pl.ds(rows * SUB, SUB), :]
    reduce_to(zq, rows, [last[n] * tail for n in range(states)], 0)

    def token(block, i, u, carried):
        t = block * chunk + i
        at = pl.ds(pl.multiple_of(t * SUB, SUB), SUB)
        size = step_t[at, :]
        half = mix_t[at, :]
        before = gs_t[at, :]
        grad = gs_t[pl.ds(pl.multiple_of(t * SUB + SUB, SUB), SUB), :]
        drive = size * half
        total_d, total_s = [None] * 2, [None] * 2
        following, for_key, for_query = [], [], []
        for n in range(states):
            key = pick(kb, rows, n, t)
            query = pick(kb, rows, states + n, t)
            state = slots[block % 2, i, n]
            full = query * grad + carried[n]
            by_key = full * key
            by_state = by_key * state
            term = key * by_state
            following.append(full - key * (size * by_key))
            for_key.append(full * drive - size * by_state)
            for_query.append(state * before)
            h = n % 2
            total_d[h] = by_key if total_d[h] is None else total_d[h] + by_key
            total_s[h] = term if total_s[h] is None else total_s[h] + term
        sum_d[at, :] = total_d[0] + total_d[1]
        sum_s[at, :] = total_s[0] + total_s[1]
        reduce_to(zk, t, for_key, 2 * u)
        reduce_to(zq, t, for_query, 2 * u + 1)
        return tuple(following)

    def some(block, i, carried):
        for u in range(unroll):
            carried = token(block, chunk - 1 - (i * unroll + u), u, carried)
        return carried

    zero = jnp.zeros((SUB, LANES), F32)
    carried = (zero,) * states
    for block in reversed(range(chunks)):
        fetch(block).wait()
        carried = lax.fori_loop(0, chunk // unroll, functools.partial(some, block), carried)
        if block >= 2:
            fetch(block - 2).start()

    total_norm = jnp.zeros((rows, 1), F32)
    for j in range(SUB):
        at = slice(j * LANES, (j + 1) * LANES)
        drive_grad = lay_rows(sum_d, rows, j)
        size = step_in[:, at]
        grad_step = drive_grad * mixed[:, at].astype(F32) - lay_rows(sum_s, rows, j)
        gmix[:, at] = drive_grad * size
        total_norm = total_norm - jnp.sum(grad_step * size * size, axis=1, keepdims=True)
        raw = raw_in[:, at]
        plus = 1.0 + raw.astype(BF16).astype(F32) * norm
        pre = grad_step / (plus * plus) * raw * (1.0 - raw)
        ups[rank : rank + SUB, at] = jnp.broadcast_to(
            jnp.sum(pre, axis=0, keepdims=True), (SUB, LANES)
        )
        preb[:, at] = pre.astype(BF16)
    pay[:rows, :] = mm_nt(preb[...], wup[...])
    rank_b = (one[:rows, :] + two[:rows, :]).astype(BF16)
    ups[:rank, :] = mm_tn(rank_b, preb[...])

    source = lax.broadcasted_iota(jnp.int32, (LANES, LANES), 1)
    lane = lax.broadcasted_iota(jnp.int32, (rows, LANES), 1)
    row = lax.broadcasted_iota(jnp.int32, (rows, LANES), 0)
    table = jnp.where(lane == 2 * states, jnp.broadcast_to(total_norm, (rows, LANES)), 0.0)
    mark = (lane == 2 * states + 1) & (row == place[1])
    table = jnp.where(mark, jnp.broadcast_to(peak[0:1, :], (rows, LANES)), table)
    for n in range(states):
        table = table + mm(
            zk[pl.ds(n * span, rows), :], jnp.where(source == n, 2.0, 0.0)
        )
        table = table + mm(
            zq[pl.ds(n * span + 1, rows), :], jnp.where(source == states + n, 1.0, 0.0)
        )
    flat = jnp.transpose(table)
    high = (pay.shape[0] - rows) * LANES // rows
    for c in range(rows // LANES):
        pay[rows + c * high : rows + (c + 1) * high, :] = flat[:high, c * LANES : (c + 1) * LANES]


def scan_backward(place, summed, mixed, w_up, step_in, raw, gy, hist, last, peak, pins):
    rows, inner = mixed.shape
    states = last.shape[0]
    unroll = 2
    span = rows + SUB
    high = 2 * states + SUB
    pay_rows = rows + high * rows // LANES
    return pl.pallas_call(
        functools.partial(back_kernel, unroll, len(pins)),
        in_specs=[pl.BlockSpec(memory_space=pltpu.SMEM)]
        + [WHOLE] * 7
        + [ANY]
        + [WHOLE] * 2
        + [ANY] * len(pins),
        out_specs=[WHOLE] * 3,
        out_shape=[
            pltpu.HBM((rows, inner), F32),
            jax.ShapeDtypeStruct((pay_rows, LANES), F32),
            pltpu.HBM((w_up.shape[0] + SUB, inner), F32),
        ],
        scratch_shapes=[
            pltpu.VMEM((rows, inner), BF16),
            pltpu.VMEM((rows * SUB, LANES), F32),
            pltpu.VMEM((rows * SUB, LANES), F32),
            pltpu.VMEM((rows * SUB + SUB, LANES), F32),
            pltpu.VMEM((2 * states * rows, LANES), F32),
            pltpu.VMEM((rows * SUB, LANES), F32),
            pltpu.VMEM((rows * SUB, LANES), F32),
            pltpu.VMEM((unroll * 2 * states * SUB, LANES), F32),
            pltpu.VMEM((states * span, LANES), F32),
            pltpu.VMEM((states * span, LANES), F32),
            pltpu.VMEM((2, rows // 4, states, SUB, LANES), F32),
            pltpu.SemaphoreType.DMA((2,)),
        ],
        compiler_params=pltpu.CompilerParams(vmem_limit_bytes=32 * MIB),
        name="back",
    )(
        place, *summed, in_hbm(mixed), in_hbm(w_up), step_in, raw, in_hbm(gy),
        in_hbm(hist), last, peak, *pins,
    )


def conv_kernel(
    pins, parts, place, one, two, grad_one, grad_two, mixed, gy, gmix, dsilu, prex, ups, cw, skip,
    wd, wk, *rest,
):
    prex_b, keep, send, table, keys, ranks, top = rest[pins:]
    step = pl.program_id(0)
    rows, blk = mixed.shape
    rank = wd.shape[1]
    count = wk.shape[0]

    @pl.when(step == 0)
    def _():
        high = (grad_one.shape[0] - rows) * LANES // rows
        kq = key_query_of(one, two, rows, count)
        gkq = key_query_of(grad_one, grad_two, rows, high)
        norm_grad = gkq[:, count : count + 1]
        lane = lax.broadcasted_iota(jnp.int32, (rows, count), 1)
        by_norm = jnp.where(lane < count // 2, 2.0 * kq * norm_grad, 0.0)
        keys[...] = (gkq[:, :count] + by_norm).astype(BF16)
        ranks[...] = (grad_one[:rows, :] + grad_two[:rows, :]).astype(BF16)
        peak = jnp.max(gkq[:, count + 1 : count + 2], axis=0, keepdims=True)
        top[...] = jnp.broadcast_to(peak, top.shape)

    kq_b = keys[...]
    rank_b = ranks[...]
    peak = top[0:1, 0:1]
    peak_high = peak.astype(BF16).astype(F32)
    taps = cw.shape[0]
    first = 2 * rank + count
    table[:rank, :] = ups[:rank, :]
    table[rank : 2 * rank, :] = mm_tn(rank_b, mixed[...])
    table[2 * rank : first, :] = mm_tn(kq_b, mixed[...])
    mix = mixed[...].astype(F32)
    grad_y = gy[...]
    total = grad_y * skip[...] + gmix[...]
    total = total + mm(kq_b, wk[...]) + mm_nt(rank_b, wd[...])
    grad = total * dsilu[...]
    pre = prex[...]
    row = lax.broadcasted_iota(jnp.int32, grad.shape, 0)
    out = None
    sums = []
    for j in range(taps):
        by = taps - 1 - j
        sums.append(jnp.sum(grad * shifted(pre, by, row), axis=0, keepdims=True))
        term = cw[j : j + 1, :] * shifted(grad, -by, row)
        out = term if out is None else out + term
    sums.append(jnp.sum(grad, axis=0, keepdims=True))
    sums.append(jnp.sum(grad_y * mix, axis=0, keepdims=True))
    sums.append(ups[rank : rank + 1, :])
    channel = lax.broadcasted_iota(jnp.int32, (1, blk), 1) + step * blk
    for value in (peak_high, peak - peak_high):
        sums.append(jnp.where(channel == place[0], jnp.broadcast_to(value, (1, blk)), 0.0))
    for i, line in enumerate(sums):
        table[first + i : first + i + 1, :] = line
    table[first + len(sums) :, :] = jnp.zeros((table.shape[0] - first - len(sums), blk), F32)
    prex_b[...] = out.astype(BF16)
    if parts != 8:
        keep[...] = table[...]
        return
    size = table.shape[0] // parts
    for dest, order in ((keep, (0, 4, 2, 6)), (send, (1, 5, 3, 7))):
        for i, p in enumerate(order):
            at = pl.ds(pl.multiple_of((place[0] ^ p) * size, SUB), size)
            dest[i] = table[at, :].astype(dest.dtype)


def conv_back(
    place, summed, grads, mixed, gy, gmix, dsilu, prex, ups, conv_weight, skip_gain, w_down,
    w_keyq, parts, pins,
):
    rows, inner = mixed.shape
    rank, count = w_down.shape[1], w_keyq.shape[0]
    blk = min(inner, 256)
    high = 8 * SMALL
    whole = lambda value: pl.BlockSpec(value.shape, lambda i: (0,) * value.ndim)
    cols = lambda height: pl.BlockSpec((height, blk), lambda i: (0, i))
    if parts == 8:
        half = (4, SMALL, inner)
        half_spec = pl.BlockSpec((4, SMALL, blk), lambda i: (0, 0, i))
    else:
        half = (high, inner)
        half_spec = cols(high)
    return pl.pallas_call(
        functools.partial(conv_kernel, len(pins), parts),
        grid=(inner // blk,),
        in_specs=[pl.BlockSpec(memory_space=pltpu.SMEM)]
        + [whole(value) for value in (*summed, *grads)]
        + [cols(rows)] * 5
        + [cols(ups.shape[0]), cols(conv_weight.shape[0]), cols(1)]
        + [pl.BlockSpec((blk, rank), lambda i: (i, 0)), cols(count)]
        + [ANY] * len(pins),
        out_specs=[cols(rows), half_spec, half_spec],
        out_shape=[
            pltpu.HBM((rows, inner), BF16),
            pltpu.HBM(half, F32),
            pltpu.HBM(half, BF16),
        ],
        scratch_shapes=[
            pltpu.VMEM((high, blk), F32),
            pltpu.VMEM((rows, count), BF16),
            pltpu.VMEM((rows, rank), BF16),
            pltpu.VMEM((SUB, LANES), F32),
        ],
        compiler_params=pltpu.CompilerParams(vmem_limit_bytes=26 * MIB),
        name="conv",
    )(
        place, *summed, *grads, in_hbm(mixed), in_hbm(gy), in_hbm(gmix), in_hbm(dsilu),
        in_hbm(prex), in_hbm(ups), in_hbm(conv_weight), in_hbm(skip_gain[None]), in_hbm(w_down),
        in_hbm(w_keyq), *pins,
    )


def branch_kernel(pins, place, gated, wo, tok, *rest):
    send, keep = rest[pins:]
    i = pl.program_id(0)
    value = mm(gated[...], wo[...])

    @pl.when(i == 0)
    def _():
        keep[0] = value + tok[...].astype(F32)

    @pl.when(i == 2)
    def _():
        keep[0] = value

    @pl.when(i % 2 == 1)
    def _():
        send[0, 0] = value.astype(BF16)


def branch(place, gated, w_out, tokens, parts, pins):
    rows, inner = gated.shape
    width = w_out.shape[1]
    own = width // parts
    return pl.pallas_call(
        functools.partial(branch_kernel, len(pins)),
        grid_spec=pltpu.PrefetchScalarGridSpec(
            num_scalar_prefetch=1,
            grid=(parts,),
            in_specs=[
                pl.BlockSpec((rows, inner), lambda i, place: (0, 0)),
                pl.BlockSpec((inner, own), lambda i, place: (0, place[1] ^ i)),
                pl.BlockSpec((rows, own), lambda i, place: (0, place[1])),
            ]
            + [ANY] * len(pins),
            out_specs=[
                pl.BlockSpec((1, 1, rows, own), lambda i, place: (i // 2, 0, 0, 0)),
                pl.BlockSpec((1, rows, own), lambda i, place: (i // 2, 0, 0)),
            ],
        ),
        out_shape=[
            pltpu.HBM((parts // 2, 2, rows, own), BF16),
            pltpu.HBM((parts // 2, rows, own), F32),
        ],
        compiler_params=pltpu.CompilerParams(vmem_limit_bytes=16 * MIB),
        name="branch",
    )(place, in_hbm(gated), in_hbm(w_out), in_hbm(tokens), *pins)


def input_kernel(
    pins, extra, place, ids, weights, half_sent, prex, prez, wx, wz, tok, tok_own, cot, gain, *rest
):
    if extra:
        keep_z, come_z = rest[:2]
        grad_z = rest[pins + 2 + 6]
        grad_z[...] = keep_z[...] + come_z[...].astype(F32)
        rest = rest[2 : pins + 2 + 6] + rest[pins + 2 + 7 :]
    send, keep, stats, slope, shift, base, inv, dots = rest[pins:]
    i = pl.program_id(0)
    rows, width = tok.shape

    @pl.when(i == 0)
    def _():
        value = tok[...].astype(F32)
        inv[...] = jnp.broadcast_to(
            lax.rsqrt(jnp.mean(value * value, axis=1, keepdims=True) + EPS), inv.shape
        )
        dots[...] = jnp.zeros_like(dots)

    value = mm_nt(prex[...], wx[...]) + mm_nt(prez[...], wz[...])
    rms = inv[:, 0:1]
    unit = tok_own[...].astype(F32) * rms
    by_unit = value * unit
    dots[...] += jnp.sum(by_unit * gain[...], axis=1, keepdims=True)
    line = jnp.sum(by_unit, axis=0, keepdims=True)
    own = line.shape[1] // LANES
    first = rows // LANES + (place[1] ^ i) * own
    for j in range(own):
        stats[pl.ds(first + j, 1), :] = line[:, j * LANES : (j + 1) * LANES]

    @pl.when(i == 0)
    def _():
        slope[...] = rms * gain[...]
        shift[...] = unit * rms * (1.0 / width)
        base[...] = cot[...].astype(F32) * weights[ids[0]]

    @pl.when(i % 2 == 0)
    def _():
        keep[0] = value

    @pl.when(i % 2 == 1)
    def _():
        send[0, 0] = value.astype(BF16)

    @pl.when(i == pl.num_programs(0) - 1)
    def _():
        flat = jnp.transpose(dots[...])
        for c in range(rows // LANES):
            stats[c : c + 1, :] = flat[0:1, c * LANES : (c + 1) * LANES]


def input_grad(
    place, group_ids, group_weights, half_sent, prex, prez, w_x, w_z, tokens, cotangent, norm_gain,
    parts, extra, pins,
):
    rows, inner = prex.shape
    width = tokens.shape[1]
    own = width // parts
    whole = lambda shape: pl.BlockSpec(shape, lambda i, place: (0, 0))
    part = pl.BlockSpec((own, inner), lambda i, place: (place[1] ^ i, 0))
    mine = pl.BlockSpec((rows, own), lambda i, place: (0, 0))
    smem = pl.BlockSpec(memory_space=pltpu.SMEM)
    strip = lambda value: pl.BlockSpec(
        (value.shape[0] // parts, value.shape[1]), lambda i, place: (i, 0)
    )
    stat_rows = rows // LANES + width // LANES
    return pl.pallas_call(
        functools.partial(input_kernel, len(pins), len(extra)),
        grid_spec=pltpu.PrefetchScalarGridSpec(
            num_scalar_prefetch=1,
            grid=(parts,),
            in_specs=[
                smem,
                smem,
                ANY,
                whole((rows, inner)),
                whole((rows, inner)),
                part,
                part,
                whole((rows, width)),
                pl.BlockSpec((rows, own), lambda i, place: (0, place[1] ^ i)),
                pl.BlockSpec((rows, own), lambda i, place: (0, place[1])),
                pl.BlockSpec((1, own), lambda i, place: (0, place[1] ^ i)),
            ]
            + [strip(value) for value in extra]
            + [ANY] * len(pins),
            out_specs=[
                pl.BlockSpec((1, 1, rows, own), lambda i, place: (i // 2, 1, 0, 0)),
                pl.BlockSpec((1, rows, own), lambda i, place: (i // 2, 0, 0)),
            ]
            + [whole((stat_rows, LANES)), mine, mine, mine]
            + [strip(value) for value in extra[:1]],
            scratch_shapes=[pltpu.VMEM((rows, LANES), F32)] * 2,
        ),
        out_shape=[
            pltpu.HBM((parts // 2, 2, rows, own), BF16),
            pltpu.HBM((parts // 2, rows, own), F32),
            jax.ShapeDtypeStruct((stat_rows, LANES), F32),
        ]
        + [pltpu.HBM((rows, own), F32)] * 3
        + [jax.ShapeDtypeStruct(value.shape, F32) for value in extra[:1]],
        compiler_params=pltpu.CompilerParams(vmem_limit_bytes=24 * MIB),
        input_output_aliases={3: 0},
        name="inputs",
    )(
        place, group_ids, group_weights, in_hbm(half_sent), in_hbm(prex), in_hbm(prez), in_hbm(w_x), in_hbm(w_z), in_hbm(tokens),
        in_hbm(tokens), in_hbm(cotangent), in_hbm(norm_gain[None]), *extra, *pins,
    )


def middle_kernel(
    place, gated, gated_far, up_own, up_a, up_b, every, wo, tok, small, small_come, *rest
):
    keep_out, later, send_out, send, keep, small_keep, small_send = rest[len(rest) - 7 :]
    i = pl.program_id(0)

    @pl.when(i == 0)
    def _():
        for j in range(2):
            small_keep[j] = small[j] + small_come[j].astype(F32)
            small_send[j] = (small[2 + j] + small_come[2 + j].astype(F32)).astype(BF16)

    rows = gated.shape[0]
    half = rows // 2
    first = (place[1] & 1) * half
    own = keep_out.shape[1]
    total = mm_tn(gated[...], up_own[...])
    total = total + mm_tn(gated_far[pl.ds(pl.multiple_of(first, half), half), :], up_a[...])
    other = pl.ds(pl.multiple_of(half - first, half), half)
    total = total + mm_tn(gated_far[other, :], up_b[...])
    keep_out[...] = total[:, :own]
    later[...] = total[:, own : 2 * own]
    send_out[...] = total[:, 2 * own :].astype(BF16)

    value = mm(every[...], wo[...])

    @pl.when(i == 0)
    def _():
        keep[0] = value + tok[...].astype(F32)

    @pl.when(i == 2)
    def _():
        keep[0] = value

    @pl.when(i % 2 == 1)
    def _():
        send[0, 0] = value.astype(BF16)


def middle(place, gated, gated_far, ups, w_out, tokens, small, small_come, parts, pins):
    rows, inner = gated.shape
    width = w_out.shape[1]
    own = width // parts
    blk = inner // parts
    out = ups[0].shape[1] // 4
    whole = lambda value: pl.BlockSpec(value.shape, lambda i, place: (0,) * value.ndim)
    cols = pl.BlockSpec((rows, blk), lambda i, place: (0, i))
    down = lambda wide: pl.BlockSpec((blk, wide), lambda i, place: (i, 0))
    return pl.pallas_call(
        middle_kernel,
        grid_spec=pltpu.PrefetchScalarGridSpec(
            num_scalar_prefetch=1,
            grid=(parts,),
            in_specs=[cols, cols]
            + [whole(value) for value in (*ups, gated)]
            + [
                pl.BlockSpec((inner, own), lambda i, place: (0, place[1] ^ i)),
                pl.BlockSpec((rows, own), lambda i, place: (0, place[1])),
                whole(small),
                whole(small_come),
            ]
            + [ANY] * len(pins),
            out_specs=[
                down(out),
                down(out),
                down(2 * out),
                pl.BlockSpec((1, 1, rows, own), lambda i, place: (i // 2, 0, 0, 0)),
                pl.BlockSpec((1, rows, own), lambda i, place: (i // 2, 0, 0)),
            ]
            + [pl.BlockSpec((2, SMALL, inner), lambda i, place: (0, 0, 0))] * 2,
        ),
        out_shape=[
            pltpu.HBM((inner, out), F32),
            pltpu.HBM((inner, out), F32),
            pltpu.HBM((inner, 2 * out), BF16),
            pltpu.HBM((parts // 2, 2, rows, own), BF16),
            pltpu.HBM((parts // 2, rows, own), F32),
            pltpu.HBM((2, SMALL, inner), F32),
            pltpu.HBM((2, SMALL, inner), BF16),
        ],
        compiler_params=pltpu.CompilerParams(vmem_limit_bytes=36 * MIB),
        name="middle",
    )(
        place, in_hbm(gated), gated_far, *ups, in_hbm(gated), in_hbm(w_out), in_hbm(tokens),
        in_hbm(small), small_come, *pins,
    )


def finale_kernel(
    rank, count, place, keep_x, come_x, keep_out, come_out, far_out, keep_a, keep_b, come_a,
    come_b, far_a, far_b, stats, slope, shift, base, g0, g2, g3,
    grad_x, grad_out, block, grad_in, up, down, keyq, conv, *rest,
):
    lines = rest[:3]
    top, table, dots = rest[3:]
    i = pl.program_id(0)

    @pl.when(i == 0)
    def _():
        tall = jnp.transpose(jnp.concatenate([stats[...]] * (SUB // stats.shape[0]), axis=0))
        for c in range(stats.shape[0]):
            dots[c * LANES : (c + 1) * LANES, :] = jnp.broadcast_to(
                tall[:, c : c + 1], (LANES, LANES)
            )

    grad_x[...] = keep_x[...] + come_x[...].astype(F32)
    grad_out[...] = keep_out[...] + come_out[...].astype(F32) + far_out[...].astype(F32)
    value = keep_a[0] + come_a[0, 0].astype(F32) + far_a[0].astype(F32)
    block[...] = value.astype(BF16)
    value = keep_b[0] + come_b[0, 0].astype(F32) + far_b[0].astype(F32)
    some = value.shape[0]
    dot = dots[pl.ds(pl.multiple_of(i * some, some), some), :][:, 0:1]
    grad_in[...] = value * slope[...] - shift[...] * dot + base[...]

    @pl.when(i == pl.num_programs(0) - 1)
    def _():
        size = g0.shape[0] // 2
        pieces = [(0, g0, 0), (4, g0, 1), (2, g2, 0), (6, g2, 1)]
        pieces += [(p, g3, i) for i, p in enumerate((1, 5, 3, 7))]
        for p, source, i in pieces:
            at = pl.ds(pl.multiple_of((place[0] ^ p) * size, SUB), size)
            table[at, :] = source[i * size : (i + 1) * size, :].astype(F32)
        up[...] = table[:rank, :]
        down[...] = jnp.transpose(table[rank : 2 * rank, :])
        keyq[...] = table[2 * rank : 2 * rank + count, :]
        first = 2 * rank + count
        conv[...] = table[first : first + conv.shape[0], :]
        first += conv.shape[0]
        for i, line in enumerate(lines):
            line[...] = table[first + i : first + i + 1, :]
        tops = table[first + len(lines) : first + len(lines) + 1, :]
        tops = tops + table[first + len(lines) + 1 : first + len(lines) + 2, :]
        top[...] = jnp.broadcast_to(jnp.max(tops, axis=1, keepdims=True), top.shape)


def finale(
    place, keep_x, come_x, keep_out, come_out, far_out, out_keep, keep, come, far, stats, slope,
    shift, base, pieces, rank, count, taps,
):
    size, inner = keep_x.shape
    rows, own = slope.shape
    steps = 4
    whole = lambda shape: pl.BlockSpec(shape, lambda i: (0,) * len(shape))
    strip = lambda high, wide: pl.BlockSpec((high // steps, wide), lambda i: (i, 0))
    kept = pl.BlockSpec((1, rows // steps, own), lambda i: (0, i, 0))
    came = lambda j: pl.BlockSpec((1, 1, rows // steps, own), lambda i: (0, j, i, 0))
    last = lambda j: pl.BlockSpec((1, rows // steps, own), lambda i: (j, i, 0))
    out = keep_out.shape[1]
    return pl.pallas_call(
        functools.partial(finale_kernel, rank, count),
        grid=(steps,),
        in_specs=[pl.BlockSpec(memory_space=pltpu.SMEM)]
        + [strip(size, inner)] * 2
        + [strip(inner, out)] * 3
        + [kept, kept, came(0), came(1), last(0), last(1)]
        + [whole(stats.shape)]
        + [strip(rows, own)] * 3
        + [whole(piece.shape) for piece in pieces],
        out_specs=[
            strip(size, inner),
            strip(inner, out),
            strip(rows, own),
            strip(rows, own),
            whole((rank, inner)),
            whole((inner, rank)),
            whole((count, inner)),
            whole((taps, inner)),
            *[whole((1, inner))] * 3,
            whole((SUB, LANES)),
        ],
        out_shape=[
            jax.ShapeDtypeStruct((size, inner), F32),
            jax.ShapeDtypeStruct((inner, out), F32),
            jax.ShapeDtypeStruct((rows, own), BF16),
            jax.ShapeDtypeStruct((rows, own), F32),
            jax.ShapeDtypeStruct((rank, inner), F32),
            jax.ShapeDtypeStruct((inner, rank), F32),
            jax.ShapeDtypeStruct((count, inner), F32),
            jax.ShapeDtypeStruct((taps, inner), F32),
            *[jax.ShapeDtypeStruct((1, inner), F32)] * 3,
            jax.ShapeDtypeStruct((SUB, LANES), F32),
        ],
        scratch_shapes=[pltpu.VMEM((8 * SMALL, inner), F32), pltpu.VMEM((rows, LANES), F32)],
        compiler_params=pltpu.CompilerParams(vmem_limit_bytes=24 * MIB),
        name="finale",
    )(
        place, in_hbm(keep_x), come_x, in_hbm(keep_out), come_out, far_out, in_hbm(out_keep),
        in_hbm(keep), come, come, far, far, stats, in_hbm(slope), in_hbm(shift), in_hbm(base),
        *pieces,
    )


def in_weight_kernel(pins, l0, l1, l2, l3, r0, r1, r2, r3, *rest):
    keep, send = rest[pins:]
    i = pl.program_id(0)
    total = None
    for left, right in ((l0[...], r0), (l1[...], r1), (l2[0], r2), (l3[...], r3)):
        term = mm_tn(left, right[...])
        total = term if total is None else total + term

    @pl.when(i == 0)
    def _():
        send[...] = total.astype(BF16)

    @pl.when(i == 1)
    def _():
        keep[...] = total


def in_weight(lefts, rights, pins):
    rows, inner = rights[0].shape
    own = lefts[0].shape[1] // 2
    whole = lambda value: pl.BlockSpec(value.shape, lambda i: (0,) * value.ndim)
    side = pl.BlockSpec((rows, own), lambda i: (0, 1 - i))
    return pl.pallas_call(
        functools.partial(in_weight_kernel, len(pins)),
        grid=(2,),
        in_specs=[side, side, pl.BlockSpec((1, rows, own), lambda i: (0, 0, 1 - i)), side]
        + [whole(r) for r in rights]
        + [ANY] * len(pins),
        out_specs=[pl.BlockSpec((own, inner), lambda i: (0, 0))] * 2,
        out_shape=[
            pltpu.HBM((own, inner), F32),
            pltpu.HBM((own, inner), BF16),
        ],
        compiler_params=pltpu.CompilerParams(vmem_limit_bytes=20 * MIB),
        name="inw",
    )(in_hbm(lefts[0]), *lefts[1:], in_hbm(rights[0]), *rights[1:], *pins)


def split_bits(axis):
    bits = bits_of(axis)
    return [bit for bit in (2, 1) if bit in bits], [bit for bit in reversed(bits) if bit > 2]


def gather_tokens(value, axis):
    pieces = [value]
    for bit in split_bits(axis)[0]:
        pieces = pieces + [swap(piece, axis, bit) for piece in pieces]
    return pieces


def exchange_cols(value, axis):
    size = lax.axis_size(axis)
    me = lax.axis_index(axis)
    gather, scatter = split_bits(axis)
    rows, cols = value.shape
    outer = 2 ** len(scatter)
    pieces = [value.reshape((rows, outer) + (2,) * len(gather) + (cols // size,))]
    for bit in gather:
        kept, sent = zip(*(halves(piece, 2, (me // bit) % 2) for piece in pieces))
        pieces = list(kept) + [swap(piece, axis, bit) for piece in sent]
    return [piece.reshape(rows, -1) for piece in pieces]


def scatter_sum(value, axis, dim):
    me = lax.axis_index(axis)
    scatter = split_bits(axis)[1]
    for bit in scatter:
        shape = value.shape
        split = shape[:dim] + (2, shape[dim] // 2) + shape[dim + 1 :]
        kept, sent = halves(value.reshape(split), dim, (me // bit) % 2)
        value = kept + swap(sent.astype(BF16), axis, bit).astype(F32)
    return value


def per_device(
    tokens,
    norm_gain,
    w_x,
    w_z,
    conv_weight,
    conv_bias,
    w_down,
    w_up,
    beta_bias,
    w_keyq,
    skip_gain,
    w_out,
    cotangent,
    group_ids,
    group_weights,
):
    rows, width = tokens.shape
    states = w_keyq.shape[1] // 2
    taps = conv_weight.shape[0]
    assert group_ids.shape[0] == 1
    parts = lax.axis_size("state")
    assert parts == 4
    dp_size = lax.axis_size("dp")
    own_width = width // parts
    state_index = lax.axis_index("state")
    place = jnp.stack([lax.axis_index("dp"), state_index]).astype(jnp.int32)
    blocked = dp_size if dp_size == 8 and width % (8 * LANES) == 0 else 0
    keyq_t = w_keyq.T

    normed, upstream_b, pre_x, mixed_b, dsilu, part, *blocks = front(
        place, group_ids, group_weights, tokens, cotangent, norm_gain, w_x,
        conv_weight, conv_bias, w_down, keyq_t, blocked,
    )
    summed = all_but_last(part, "state")
    pins_back = pins_conv = pins_inputs = extra = ()
    if blocked:
        far, near, own, up_far, up_own = blocks
        far = swap(far, "dp", 2)
        near = swap(near, "dp", 1)
        up_far = swap(up_far, "dp", 4)
        pins_back = (far, near, up_far)
    else:
        norm_parts = exchange_cols(normed, "dp")
        up_parts = exchange_cols(upstream_b, "dp")
    silu_z, dgate, grad_y = gate(normed, upstream_b, w_z, w_out)

    gated_b, prez_b, step_size, raw, peak, hist, last = scan_forward(
        summed, mixed_b, w_up, beta_bias, silu_z, dgate, skip_gain, states
    )
    if blocked:
        gated_far = swap(gated_b, "dp", 4)
        prez_far = swap(prez_b, "dp", 2)
        prez_near = swap(prez_b, "dp", 1)

    gmix, pay, ups = scan_backward(
        place, summed, mixed_b, w_up, step_size, raw, grad_y, hist, last, peak, pins_back
    )
    grads = all_but_last(pay, "state")
    if blocked:
        up_parts = (up_own, up_far, swap(up_far, "state", 1))
        (prez_far,) = after((prez_far,), (pay,))
        prez_last = swap(prez_far, "dp", 1)
        sides = (own, far, near, swap(near[1], "dp", 2))
        pins_conv = (gated_far, up_parts[2], prez_near, sides[3])

    prex_b, small, small_send = conv_back(
        place, summed, grads, mixed_b, grad_y, gmix, dsilu, pre_x, ups, conv_weight, skip_gain,
        w_down, keyq_t, dp_size, pins_conv,
    )

    if blocked:
        prex_far = swap(prex_b, "dp", 2)
        prex_near = swap(prex_b, "dp", 1)
        keep_z, send_z = in_weight(sides, (prez_b, prez_far, prez_near, prez_last), (prex_b,))
        come_z = swap(send_z, "dp", 4)
        keep_out, later, send_out, half_sent, out_keep, small, small_send = middle(
            place, gated_b, gated_far, up_parts, w_out, tokens, small,
            swap(small_send, "dp", 1), parts, (send_z, prex_far, prex_near),
        )
        prex_last = swap(prex_far, "dp", 1)
        come_out = swap(send_out, "dp", 1)
        keep_x, send_x = in_weight(
            sides, (prex_b, prex_far, prex_near, prex_last), (send_out, come_z)
        )
        come_x = swap(send_x, "dp", 4)
        (small_send,) = after((small_send,), (send_x,))
        small = small + swap(small_send, "dp", 2).astype(F32)
        pins_inputs = (send_x,)
        extra = (keep_z, come_z)
    else:
        half_sent, out_keep = branch(place, gated_b, w_out, tokens, parts, ())
    send, keep, stats, slope, shift, base, *grad_wz = input_grad(
        place, group_ids, group_weights, half_sent, prex_b, prez_b, w_x, w_z, tokens, cotangent,
        norm_gain, parts, extra, pins_inputs,
    )
    if blocked:
        (grad_wz,) = grad_wz
        cut = later.shape[1]
        far_out = swap((later + come_out[:, cut:].astype(F32)).astype(BF16), "dp", 2)
        send, stats, small = after((send, stats, small), (come_x, come_out))
    else:

        def weight_grad(value, left):
            pieces = gather_tokens(value, "dp")
            pairs = zip(pieces, up_parts) if left else zip(norm_parts, pieces)
            return scatter_sum(sum(mm_tn(a, b) for a, b in pairs), "dp", 1 if left else 0)

        grad_wout = weight_grad(gated_b, True)
        grad_wz = weight_grad(prez_b, False)
        grad_wx = weight_grad(prex_b, False)

    come = swap(send, "state", 1)
    pair = jnp.stack([out_keep[1], keep[1]]) + come[1].astype(F32)
    come_far = swap(pair.astype(BF16), "state", 2)
    stats = all_sum(stats, "state")
    if not blocked:
        block_out = out_keep[0] + come[0, 0].astype(F32) + come_far[0].astype(F32)
        block_out = block_out.astype(BF16)
        norm_grad = keep[0] + come[0, 1].astype(F32) + come_far[1].astype(F32)
        row_stat = stats[: rows // LANES].reshape(rows, 1)
        grad_in = norm_grad * slope - shift * row_stat + base
    gain_rows = own_width // LANES
    gain = lax.dynamic_slice_in_dim(
        stats, rows // LANES + state_index * gain_rows, gain_rows, 0
    )

    count = 2 * states
    rank = w_up.shape[0]
    if blocked:
        small = lax.reduce_precision(small.reshape(-1, small.shape[-1]), 8, 7)
        flipped = jnp.concatenate([small[SMALL:], small[:SMALL]], axis=0).astype(BF16)
        gathered = (small + swap(flipped, "dp", 4).astype(F32)).astype(BF16)
        gain = gain + swap(gain, "dp", 4)
        pieces = [gathered]
        for bit, pins in ((2, (come,)), (1, (come_far, far_out))):
            high = lax.reduce_precision(gain, 8, 7)
            rest = lax.reduce_precision(gain - high, 8, 7)
            line = jnp.concatenate([high.reshape(1, -1), rest.reshape(1, -1)], axis=1)
            tail = jnp.pad(line.astype(BF16), ((0, SUB - 1), (0, 0)))
            (whole,) = after((jnp.concatenate([gathered, tail], axis=0),), pins)
            got = swap(whole, "dp", bit)
            pieces.append(got[:-SUB])
            gathered = jnp.concatenate([gathered, got[:-SUB]], axis=0)
            other = got[-SUB].astype(F32)
            gain = (high + rest) + (other[:own_width] + other[own_width:]).reshape(gain.shape)
        grad_gain = gain.reshape(-1)
        grad_wx, grad_wout, block_out, grad_in, grad_up, down, keyq, *lines = finale(
            place, keep_x, come_x, keep_out, come_out, far_out, out_keep, keep, come, come_far,
            stats[: rows // LANES], slope, shift, base, pieces, rank, count, taps,
        )
    else:
        small = all_sum(small, "dp")
        grad_up = small[:rank]
        down = small[rank : 2 * rank].T
        keyq = small[2 * rank : 2 * rank + count]
        lines = small[2 * rank + count :]
        top = jnp.max(lines[taps + 3] + lines[taps + 4]).reshape(1, 1)
        lines = (lines[:taps], *[lines[taps + i : taps + i + 1] for i in range(3)], top)
        grad_gain = all_sum(gain, "dp").reshape(-1)
    grad_taps, grad_bias, grad_skip, grad_beta, top = lines
    return (
        block_out,
        grad_in,
        grad_gain,
        grad_wx,
        grad_wz,
        grad_taps,
        grad_bias[0],
        down,
        grad_up,
        grad_beta[0],
        keyq.T,
        grad_skip[0],
        grad_wout,
        top[0, 0],
    )


def solution(mesh):
    placed = (
        P("dp", None),
        P(),
        P(None, "state"),
        P(None, "state"),
        P(None, "state"),
        P("state"),
        P("state", None),
        P(None, "state"),
        P("state"),
        P("state", None),
        P("state"),
        P("state", None),
        P("dp", None),
        P("dp"),
        P(),
    )
    return jax.shard_map(
        per_device,
        mesh=mesh,
        in_specs=placed,
        out_specs=(
            P("dp", "state"),
            P("dp", "state"),
            P("state"),
            P("dp", "state"),
            P("dp", "state"),
            P(None, "state"),
            P("state"),
            P("state", None),
            P(None, "state"),
            P("state"),
            P("state", None),
            P("state"),
            P("state", "dp"),
            P(),
        ),
        check_vma=False,
    )
```

```python
import functools

import jax
import jax.numpy as jnp
from jax import lax
from jax.experimental import pallas as pl
from jax.experimental.pallas import tpu as pltpu
from jax.sharding import PartitionSpec as P

EPS = 1e-05
LANES = 128
SUB = 8
F32 = jnp.float32
BF16 = jnp.bfloat16
MIB = 2**20
WHOLE = pl.BlockSpec(memory_space=pltpu.VMEM)
ANY = pl.BlockSpec(memory_space=pl.ANY)
SMALL = 40


def mm(left, right):
    return jnp.dot(left, right, preferred_element_type=F32)


def mm_nt(left, right):
    return lax.dot_general(left, right, (((1,), (1,)), ((), ())), preferred_element_type=F32)


def mm_tn(left, right):
    return lax.dot_general(left, right, (((0,), (0,)), ((), ())), preferred_element_type=F32)


def swap(value, axis, bit):
    size = lax.axis_size(axis)
    return lax.ppermute(value, axis, [(i, i ^ bit) for i in range(size)])


def bits_of(axis):
    size = lax.axis_size(axis)
    bits, bit = [], 1
    while bit < size:
        bits.append(bit)
        bit *= 2
    return bits


def all_sum(value, axis):
    for bit in bits_of(axis):
        value = value + swap(value, axis, bit)
    return value


def all_max(value, axis):
    for bit in bits_of(axis):
        value = jnp.maximum(value, swap(value, axis, bit))
    return value


def halves(value, dim, bit_set):
    kept = lax.dynamic_index_in_dim(value, bit_set, dim, keepdims=False)
    sent = lax.dynamic_index_in_dim(value, 1 - bit_set, dim, keepdims=False)
    return kept, sent


def all_but_last(value, axis):
    bits = bits_of(axis)
    for bit in bits[:-1]:
        value = value + swap(value, axis, bit)
    return value, swap(value, axis, bits[-1])


def after(values, pins):
    def nothing(*refs):
        pass

    return pl.pallas_call(
        nothing,
        in_specs=[ANY] * (len(values) + len(pins)),
        out_specs=[ANY] * len(values),
        out_shape=[jax.ShapeDtypeStruct(value.shape, value.dtype) for value in values],
        input_output_aliases={i: i for i in range(len(values))},
        name="after",
    )(*values, *pins)


def in_hbm(value):
    return pltpu.with_memory_space_constraint(value, pltpu.HBM)


def shifted(value, by, rows):
    if by == 0:
        return value
    count = value.shape[0]
    moved = pltpu.roll(value, by % count, 0)
    keep = rows >= by if by > 0 else rows < count + by
    return jnp.where(keep, moved, 0.0)


def front_kernel(
    blocked, place, ids, weights, tok, cot, gain, wx, cw, cb, wd, wk,
    normed, up, prex, mixed, dsilu, part, *rest,
):
    step = pl.program_id(0)
    rows, width = tok.shape
    acc = rest[-1]

    @pl.when(step == 0)
    def _():
        value = tok[...].astype(F32)
        inv = lax.rsqrt(jnp.mean(value * value, axis=1, keepdims=True) + EPS)
        normed[...] = (value * inv * gain[...]).astype(BF16)
        part[...] = jnp.zeros_like(part)
        acc[...] = jnp.zeros_like(acc)

    pre = mm(normed[...], wx[...])
    prex[...] = pre
    row = lax.broadcasted_iota(jnp.int32, pre.shape, 0)
    taps = cw.shape[0]
    conv = cb[...] + sum(cw[j : j + 1, :] * shifted(pre, taps - 1 - j, row) for j in range(taps))
    sig = jax.nn.sigmoid(conv)
    mix = (conv * sig).astype(BF16)
    mixed[...] = mix
    dsilu[...] = sig * (1.0 + conv * (1.0 - sig))
    part[:rows, :] += mm(mix, wd[...])
    acc[...] += mm_nt(wk[...], mix)

    @pl.when(step == pl.num_programs(0) - 1)
    def _():
        wide = acc.shape[0]
        for c in range(rows // LANES):
            part[rows + c * wide : rows + (c + 1) * wide, :] = acc[:, c * LANES : (c + 1) * LANES]
        up[...] = (cot[...].astype(F32) * weights[ids[0]]).astype(BF16)
        if blocked:
            far, near, own, up_far, up_own = rest[:5]
            size = width // blocked
            for p in range(blocked):
                cols = pl.ds(pl.multiple_of((place[0] ^ p) * size, size), size)
                dest = near.at[p >> 1 & 1] if p & 1 else (far if p & 2 else own)
                dest[:, (p // 4) * size : (p // 4 + 1) * size] = normed[:, cols]
                at = (p & 1) * 2 + (p >> 1 & 1)
                at = slice(at * size, (at + 1) * size)
                if p & 4:
                    half = rows // 2
                    some = pl.ds(pl.multiple_of((place[1] & 1) * half, half), half)
                    up_far[:, at] = up[some, cols]
                else:
                    up_own[:, at] = up[:, cols]


def front(
    place, group_ids, group_weights, tokens, cotangent, norm_gain, w_x,
    conv_weight, conv_bias, w_down, w_keyq, blocked,
):
    rows, width = tokens.shape
    inner = w_x.shape[1]
    rank, kq = w_down.shape[1], w_keyq.shape[0]
    blk = min(inner, 512)
    whole = lambda shape: pl.BlockSpec(shape, lambda i: (0,) * len(shape))
    cols = lambda height: pl.BlockSpec((height, blk), lambda i: (0, i))
    smem = pl.BlockSpec(memory_space=pltpu.SMEM)
    part_rows = rows + kq * rows // LANES
    shapes = []
    if blocked:
        quarter, half = width // 4, width // 2
        shapes = [(rows, quarter), (2, rows, quarter), (rows, quarter), (rows // 2, half)]
        shapes += [(rows, half)]
    return pl.pallas_call(
        functools.partial(front_kernel, blocked),
        grid=(inner // blk,),
        in_specs=[
            smem,
            smem,
            smem,
            whole((rows, width)),
            whole((rows, width)),
            whole((1, width)),
            cols(width),
            cols(conv_weight.shape[0]),
            cols(1),
            pl.BlockSpec((blk, rank), lambda i: (i, 0)),
            cols(kq),
        ],
        out_specs=[
            whole((rows, width)),
            whole((rows, width)),
            cols(rows),
            cols(rows),
            cols(rows),
            whole((part_rows, LANES)),
        ]
        + [whole(shape) for shape in shapes],
        out_shape=[
            jax.ShapeDtypeStruct((rows, width), BF16),
            jax.ShapeDtypeStruct((rows, width), BF16),
            pltpu.HBM((rows, inner), F32),
            pltpu.HBM((rows, inner), BF16),
            pltpu.HBM((rows, inner), F32),
            jax.ShapeDtypeStruct((part_rows, LANES), F32),
        ]
        + [pltpu.HBM(shape, BF16) for shape in shapes],
        scratch_shapes=[pltpu.VMEM((kq, rows), F32)],
        compiler_params=pltpu.CompilerParams(vmem_limit_bytes=36 * MIB),
        name="front",
    )(
        place, group_ids, group_weights, in_hbm(tokens), in_hbm(cotangent),
        in_hbm(norm_gain[None]), in_hbm(w_x), in_hbm(conv_weight), in_hbm(conv_bias[None]),
        in_hbm(w_down), in_hbm(w_keyq),
    )


def gate_kernel(normed, up, wz, wo, silu, dgate, gy):
    pre = mm(normed[...], wz[...])
    back = mm_nt(up[...], wo[...])
    sig = jax.nn.sigmoid(pre)
    act = pre * sig
    silu[...] = act
    gy[...] = back * act
    dgate[...] = back * sig * (1.0 + pre * (1.0 - sig))


def gate(normed, upstream_b, w_z, w_out):
    rows, width = normed.shape
    inner = w_z.shape[1]
    blk = min(inner, 512)
    whole = lambda shape: pl.BlockSpec(shape, lambda i: (0, 0))
    cols = lambda height: pl.BlockSpec((height, blk), lambda i: (0, i))
    return pl.pallas_call(
        gate_kernel,
        grid=(inner // blk,),
        in_specs=[
            whole((rows, width)),
            whole((rows, width)),
            cols(width),
            pl.BlockSpec((blk, width), lambda i: (i, 0)),
        ],
        out_specs=[cols(rows)] * 3,
        out_shape=[jax.ShapeDtypeStruct((rows, inner), F32)] * 2 + [pltpu.HBM((rows, inner), F32)],
        compiler_params=pltpu.CompilerParams(vmem_limit_bytes=24 * MIB),
        name="gate",
    )(normed, upstream_b, in_hbm(w_z), in_hbm(w_out))


def key_query_of(one, two, rows, count):
    parts = []
    for c in range(rows // LANES):
        at = slice(rows + c * count, rows + (c + 1) * count)
        parts.append(one[at, :] + two[at, :])
    return jnp.transpose(jnp.concatenate(parts, axis=1))


def lay_tiles(dest, value, base=0):
    for j in range(SUB):
        dest[pl.ds(base * SUB + j, value.shape[0], stride=SUB), :] = value[
            :, j * LANES : (j + 1) * LANES
        ]


def lay_rows(source, count, j):
    return source[pl.ds(j, count, stride=SUB), :]


def spread(dest, key_query):
    rows, count = key_query.shape
    for n in range(count):
        dest[n * rows : (n + 1) * rows, :] = jnp.broadcast_to(
            key_query[:, n : n + 1], (rows, LANES)
        )


def pick(source, rows, n, t):
    return source[pl.ds(n * rows + t, SUB, stride=0), :]


def scan_kernel(
    unroll, one, two, mixed, wup, bias, silu, dgate, skip,
    gated, prez, step_out, raw_out, peak, hist, last, step_t, mix_t, out_t, kb, slots, sems,
):
    rows, inner = mixed.shape
    span = slots.shape[1]
    states = kb.shape[0] // rows // 2
    kq = key_query_of(one, two, rows, 2 * states)
    keys = kq[:, :states]
    norm = jnp.sum(keys * keys, axis=1, keepdims=True)
    spread(kb, kq)
    rank_b = (one[:rows, :] + two[:rows, :]).astype(BF16)
    raw = jax.nn.sigmoid(mm(rank_b, wup[...]) + bias[...])
    raw_out[...] = raw
    highest = jnp.max(jnp.max(raw, axis=0, keepdims=True), axis=1, keepdims=True)
    peak[...] = jnp.broadcast_to(highest, peak.shape)
    beta = raw.astype(BF16).astype(F32)
    size = beta / (1.0 + beta * norm)
    step_out[...] = size
    lay_tiles(step_t, size)
    lay_tiles(mix_t, mixed[...].astype(F32))

    def token(block, i, carried):
        t = block * span + i
        at = pl.ds(pl.multiple_of(t * SUB, SUB), SUB)
        size = step_t[at, :]
        mix = mix_t[at, :]
        sums = [None] * 4
        following = []
        for n in range(states):
            key = pick(kb, rows, n, t)
            query = pick(kb, rows, states + n, t)
            state = carried[n]
            if n % 2:
                pair = jnp.concatenate([carried[n - 1], state], axis=0)
                slots[block % 2, i, n // 2] = pair.astype(BF16)
            state = state + (size * key) * (mix - key * state)
            term = query * state
            sums[n % 4] = term if sums[n % 4] is None else sums[n % 4] + term
            following.append(state)
        out_t[at, :] = (sums[0] + sums[1]) + (sums[2] + sums[3])
        return tuple(following)

    zero = jnp.zeros((SUB, LANES), F32)
    final = (zero,) * states
    copies = []
    for block in range(rows // span):
        if block >= 2:
            copies[block - 2].wait()
        final = lax.fori_loop(0, span, functools.partial(token, block), final, unroll=unroll)
        copies.append(
            pltpu.make_async_copy(
                slots.at[block % 2], hist.at[pl.ds(block * span, span)], sems.at[block % 2]
            )
        )
        copies[-1].start()
    for n in range(states):
        last[n] = final[n]
    for j in range(SUB):
        at = slice(j * LANES, (j + 1) * LANES)
        y = lay_rows(out_t, rows, j) + skip[:, at] * mixed[:, at].astype(F32)
        gated[:, at] = (y * silu[:, at]).astype(BF16)
        prez[:, at] = (y * dgate[:, at]).astype(BF16)
    for copy in copies[-2:]:
        copy.wait()


def scan_forward(summed, mixed, w_up, beta_bias, silu, dgate, skip_gain, states):
    rows, inner = mixed.shape
    full = lambda dtype: jax.ShapeDtypeStruct((rows, inner), dtype)
    return pl.pallas_call(
        functools.partial(scan_kernel, 4),
        in_specs=[WHOLE] * 8,
        out_specs=[WHOLE] * 5 + [pl.BlockSpec(memory_space=pl.ANY), WHOLE],
        out_shape=[
            pltpu.HBM((rows, inner), BF16),
            pltpu.HBM((rows, inner), BF16),
            full(F32),
            full(F32),
            jax.ShapeDtypeStruct((SUB, LANES), F32),
            pltpu.HBM((rows, states // 2, 2 * SUB, LANES), BF16),
            jax.ShapeDtypeStruct((states, SUB, LANES), F32),
        ],
        scratch_shapes=[pltpu.VMEM((rows * SUB, LANES), F32)] * 3
        + [
            pltpu.VMEM((2 * states * rows, LANES), F32),
            pltpu.VMEM((2, rows // 8, states // 2, 2 * SUB, LANES), BF16),
            pltpu.SemaphoreType.DMA((2,)),
        ],
        compiler_params=pltpu.CompilerParams(vmem_limit_bytes=26 * MIB),
        name="scan",
    )(*summed, in_hbm(mixed), in_hbm(w_up), in_hbm(beta_bias[None]), silu, dgate, in_hbm(skip_gain[None]))


def back_kernel(
    unroll, pins, place, one, two, mixed, wup, step_in, raw_in, gy, hist, last, peak, *rest, ):
    gmix, pay, ups, preb, step_t, mix_t, gs_t, kb, sum_d, sum_s, prods, zk, zq, slots, sems = rest[
        pins:
    ]
    rows, inner = mixed.shape
    states = last.shape[0]
    rank = wup.shape[0]
    span = zk.shape[0] // states
    chunk = slots.shape[1]
    chunks = rows // chunk

    def fetch(block):
        return pltpu.make_async_copy(
            hist.at[pl.ds(block * chunk, chunk)], slots.at[block % 2], sems.at[block % 2]
        )

    fetch(chunks - 1).start()
    fetch(chunks - 2).start()
    kq = key_query_of(one, two, rows, 2 * states)
    keys = kq[:, :states]
    norm = jnp.sum(keys * keys, axis=1, keepdims=True)
    spread(kb, kq)
    lay_tiles(step_t, step_in[...])
    lay_tiles(mix_t, mixed[...].astype(F32) * 0.5)
    gs_t[0:SUB, :] = jnp.zeros((SUB, LANES), F32)
    lay_tiles(gs_t, gy[...].astype(BF16).astype(F32), 1)

    def reduce_to(dest, row, terms, slot):
        base = slot * states * SUB
        for n in range(states):
            prods[pl.ds(base + n * SUB, SUB), :] = terms[n]
        for g in range(states // SUB):
            total = None
            for s in range(SUB):
                part = prods[pl.ds(base + g * SUB * SUB + s, SUB, stride=SUB), :]
                total = part if total is None else total + part
            dest[pl.ds(row + g * SUB * span, SUB, stride=span), :] = total

    tail = gs_t[pl.ds(rows * SUB, SUB), :]
    reduce_to(zq, rows, [last[n] * tail for n in range(states)], 0)

    def token(block, i, u, carried):
        t = block * chunk + i
        at = pl.ds(pl.multiple_of(t * SUB, SUB), SUB)
        size = step_t[at, :]
        half = mix_t[at, :]
        before = gs_t[at, :]
        grad = gs_t[pl.ds(pl.multiple_of(t * SUB + SUB, SUB), SUB), :]
        drive = size * half
        total_d, total_s = [None] * 2, [None] * 2
        following, for_key, for_query = [], [], []
        for n in range(states):
            key = pick(kb, rows, n, t)
            query = pick(kb, rows, states + n, t)
            if n % 2 == 0:
                pair = slots[block % 2, i, n // 2].astype(F32)
            state = pair[n % 2 * SUB : (n % 2 + 1) * SUB]
            full = query * grad + carried[n]
            by_key = full * key
            by_state = by_key * state
            term = key * by_state
            following.append(full - key * (size * by_key))
            for_key.append(full * drive - size * by_state)
            for_query.append(state * before)
            h = n % 2
            total_d[h] = by_key if total_d[h] is None else total_d[h] + by_key
            total_s[h] = term if total_s[h] is None else total_s[h] + term
        sum_d[at, :] = total_d[0] + total_d[1]
        sum_s[at, :] = total_s[0] + total_s[1]
        reduce_to(zk, t, for_key, 2 * u)
        reduce_to(zq, t, for_query, 2 * u + 1)
        return tuple(following)

    def some(block, i, carried):
        for u in range(unroll):
            carried = token(block, chunk - 1 - (i * unroll + u), u, carried)
        return carried

    zero = jnp.zeros((SUB, LANES), F32)
    carried = (zero,) * states
    for block in reversed(range(chunks)):
        fetch(block).wait()
        carried = lax.fori_loop(0, chunk // unroll, functools.partial(some, block), carried)
        if block >= 2:
            fetch(block - 2).start()

    total_norm = jnp.zeros((rows, LANES), F32)
    for j in range(SUB):
        at = slice(j * LANES, (j + 1) * LANES)
        drive_grad = lay_rows(sum_d, rows, j)
        size = step_in[:, at]
        grad_step = drive_grad * mixed[:, at].astype(F32) - lay_rows(sum_s, rows, j)
        gmix[:, at] = drive_grad * size
        total_norm = total_norm - grad_step * size * size
        raw = raw_in[:, at]
        plus = 1.0 + raw.astype(BF16).astype(F32) * norm
        pre = grad_step / (plus * plus) * raw * (1.0 - raw)
        ups[rank : rank + SUB, at] = jnp.broadcast_to(
            jnp.sum(pre, axis=0, keepdims=True), (SUB, LANES)
        )
        preb[:, at] = pre.astype(BF16)
    pay[:rows, :] = mm_nt(preb[...], wup[...])
    rank_b = (one[:rows, :] + two[:rows, :]).astype(BF16)
    ups[:rank, :] = mm_tn(rank_b, preb[...])

    blocks = [zk[pl.ds(n * span, rows), :].astype(BF16) for n in range(states)]
    blocks += [zq[pl.ds(n * span + 1, rows), :].astype(BF16) for n in range(states)]
    norm_high = total_norm.astype(BF16)
    blocks += [norm_high, (total_norm - norm_high.astype(F32)).astype(BF16)]
    shape = (LANES * len(blocks), LANES)
    block = lax.broadcasted_iota(jnp.int32, shape, 0) // LANES
    target = jnp.minimum(block, 2 * states)
    weight = jnp.where(block < states, 2.0, 1.0)
    chosen = jnp.where(target == lax.broadcasted_iota(jnp.int32, shape, 1), weight, 0.0)
    table = mm(jnp.concatenate(blocks, axis=1), chosen.astype(BF16))
    lane = lax.broadcasted_iota(jnp.int32, (rows, LANES), 1)
    row = lax.broadcasted_iota(jnp.int32, (rows, LANES), 0)
    mark = (lane == 2 * states + 1) & (row == place[1])
    table = jnp.where(mark, jnp.broadcast_to(peak[0:1, :], (rows, LANES)), table)
    flat = jnp.transpose(table)
    high = (pay.shape[0] - rows) * LANES // rows
    for c in range(rows // LANES):
        pay[rows + c * high : rows + (c + 1) * high, :] = flat[:high, c * LANES : (c + 1) * LANES]


def scan_backward(place, summed, mixed, w_up, step_in, raw, gy, hist, last, peak, pins):
    rows, inner = mixed.shape
    states = last.shape[0]
    unroll = 2
    span = rows + SUB
    high = 2 * states + SUB
    pay_rows = rows + high * rows // LANES
    return pl.pallas_call(
        functools.partial(back_kernel, unroll, len(pins)),
        in_specs=[pl.BlockSpec(memory_space=pltpu.SMEM)]
        + [WHOLE] * 7
        + [ANY]
        + [WHOLE] * 2
        + [ANY] * len(pins),
        out_specs=[WHOLE] * 3,
        out_shape=[
            pltpu.HBM((rows, inner), F32),
            jax.ShapeDtypeStruct((pay_rows, LANES), F32),
            pltpu.HBM((w_up.shape[0] + SUB, inner), F32),
        ],
        scratch_shapes=[
            pltpu.VMEM((rows, inner), BF16),
            pltpu.VMEM((rows * SUB, LANES), F32),
            pltpu.VMEM((rows * SUB, LANES), F32),
            pltpu.VMEM((rows * SUB + SUB, LANES), F32),
            pltpu.VMEM((2 * states * rows, LANES), F32),
            pltpu.VMEM((rows * SUB, LANES), F32),
            pltpu.VMEM((rows * SUB, LANES), F32),
            pltpu.VMEM((unroll * 2 * states * SUB, LANES), F32),
            pltpu.VMEM((states * span, LANES), F32),
            pltpu.VMEM((states * span, LANES), F32),
            pltpu.VMEM((2, rows // 8, states // 2, 2 * SUB, LANES), BF16),
            pltpu.SemaphoreType.DMA((2,)),
        ],
        compiler_params=pltpu.CompilerParams(vmem_limit_bytes=32 * MIB),
        name="back",
    )(
        place, *summed, in_hbm(mixed), in_hbm(w_up), step_in, raw, in_hbm(gy),
        in_hbm(hist), last, peak, *pins,
    )


def conv_kernel(
    pins, parts, place, one, two, grad_one, grad_two, mixed, gy, gmix, dsilu, prex, ups, cw, skip,
    wd, wk, *rest,
):
    prex_b, keep, send, table, keys, ranks, top = rest[pins:]
    step = pl.program_id(0)
    rows, blk = mixed.shape
    rank = wd.shape[1]
    count = wk.shape[0]

    @pl.when(step == 0)
    def _():
        high = (grad_one.shape[0] - rows) * LANES // rows
        kq = key_query_of(one, two, rows, count)
        gkq = key_query_of(grad_one, grad_two, rows, high)
        norm_grad = gkq[:, count : count + 1]
        lane = lax.broadcasted_iota(jnp.int32, (rows, count), 1)
        by_norm = jnp.where(lane < count // 2, 2.0 * kq * norm_grad, 0.0)
        keys[...] = (gkq[:, :count] + by_norm).astype(BF16)
        ranks[...] = (grad_one[:rows, :] + grad_two[:rows, :]).astype(BF16)
        peak = jnp.max(gkq[:, count + 1 : count + 2], axis=0, keepdims=True)
        top[...] = jnp.broadcast_to(peak, top.shape)

    kq_b = keys[...]
    rank_b = ranks[...]
    peak = top[0:1, 0:1]
    peak_high = peak.astype(BF16).astype(F32)
    taps = cw.shape[0]
    first = 2 * rank + count
    table[:rank, :] = ups[:rank, :]
    table[rank : 2 * rank, :] = mm_tn(rank_b, mixed[...])
    table[2 * rank : first, :] = mm_tn(kq_b, mixed[...])
    mix = mixed[...].astype(F32)
    grad_y = gy[...]
    total = grad_y * skip[...] + gmix[...]
    total = total + mm(kq_b, wk[...]) + mm_nt(rank_b, wd[...])
    grad = total * dsilu[...]
    pre = prex[...]
    row = lax.broadcasted_iota(jnp.int32, grad.shape, 0)
    out = None
    sums = []
    for j in range(taps):
        by = taps - 1 - j
        sums.append(jnp.sum(grad * shifted(pre, by, row), axis=0, keepdims=True))
        term = cw[j : j + 1, :] * shifted(grad, -by, row)
        out = term if out is None else out + term
    sums.append(jnp.sum(grad, axis=0, keepdims=True))
    sums.append(jnp.sum(grad_y * mix, axis=0, keepdims=True))
    sums.append(ups[rank : rank + 1, :])
    channel = lax.broadcasted_iota(jnp.int32, (1, blk), 1) + step * blk
    for value in (peak_high, peak - peak_high):
        sums.append(jnp.where(channel == place[0], jnp.broadcast_to(value, (1, blk)), 0.0))
    for i, line in enumerate(sums):
        table[first + i : first + i + 1, :] = line
    table[first + len(sums) :, :] = jnp.zeros((table.shape[0] - first - len(sums), blk), F32)
    prex_b[...] = out.astype(BF16)
    if parts != 8:
        keep[...] = table[...]
        return
    size = table.shape[0] // parts
    for dest, order in ((keep, (0, 4, 2, 6)), (send, (1, 5, 3, 7))):
        for i, p in enumerate(order):
            at = pl.ds(pl.multiple_of((place[0] ^ p) * size, SUB), size)
            dest[i] = table[at, :].astype(dest.dtype)


def conv_back(
    place, summed, grads, mixed, gy, gmix, dsilu, prex, ups, conv_weight, skip_gain, w_down,
    w_keyq, parts, pins,
):
    rows, inner = mixed.shape
    rank, count = w_down.shape[1], w_keyq.shape[0]
    blk = min(inner, 512)
    high = 8 * SMALL
    whole = lambda value: pl.BlockSpec(value.shape, lambda i: (0,) * value.ndim)
    cols = lambda height: pl.BlockSpec((height, blk), lambda i: (0, i))
    if parts == 8:
        half = (4, SMALL, inner)
        half_spec = pl.BlockSpec((4, SMALL, blk), lambda i: (0, 0, i))
    else:
        half = (high, inner)
        half_spec = cols(high)
    return pl.pallas_call(
        functools.partial(conv_kernel, len(pins), parts),
        grid=(inner // blk,),
        in_specs=[pl.BlockSpec(memory_space=pltpu.SMEM)]
        + [whole(value) for value in (*summed, *grads)]
        + [cols(rows)] * 5
        + [cols(ups.shape[0]), cols(conv_weight.shape[0]), cols(1)]
        + [pl.BlockSpec((blk, rank), lambda i: (i, 0)), cols(count)]
        + [ANY] * len(pins),
        out_specs=[cols(rows), half_spec, half_spec],
        out_shape=[
            pltpu.HBM((rows, inner), BF16),
            pltpu.HBM(half, F32),
            pltpu.HBM(half, BF16),
        ],
        scratch_shapes=[
            pltpu.VMEM((high, blk), F32),
            pltpu.VMEM((rows, count), BF16),
            pltpu.VMEM((rows, rank), BF16),
            pltpu.VMEM((SUB, LANES), F32),
        ],
        compiler_params=pltpu.CompilerParams(vmem_limit_bytes=26 * MIB),
        name="conv",
    )(
        place, *summed, *grads, in_hbm(mixed), in_hbm(gy), in_hbm(gmix), in_hbm(dsilu),
        in_hbm(prex), in_hbm(ups), in_hbm(conv_weight), in_hbm(skip_gain[None]), in_hbm(w_down),
        in_hbm(w_keyq), *pins,
    )


def branch_kernel(pins, place, gated, wo, tok, *rest):
    send, keep, keep_far = rest[pins:]
    i = pl.program_id(0)
    value = mm(gated[...], wo[...])

    @pl.when(i == 0)
    def _():
        keep[...] = value + tok[...].astype(F32)

    @pl.when(i == 2)
    def _():
        keep_far[...] = value

    @pl.when(i % 2 == 1)
    def _():
        send[0, 0] = value.astype(BF16)


def branch(place, gated, w_out, tokens, parts, pins):
    rows, inner = gated.shape
    width = w_out.shape[1]
    own = width // parts
    return pl.pallas_call(
        functools.partial(branch_kernel, len(pins)),
        grid_spec=pltpu.PrefetchScalarGridSpec(
            num_scalar_prefetch=1,
            grid=(parts,),
            in_specs=[
                pl.BlockSpec((rows, inner), lambda i, place: (0, 0)),
                pl.BlockSpec((inner, own), lambda i, place: (0, place[1] ^ i)),
                pl.BlockSpec((rows, own), lambda i, place: (0, place[1])),
            ]
            + [ANY] * len(pins),
            out_specs=[
                pl.BlockSpec((1, 1, rows, own), lambda i, place: (i // 2, 0, 0, 0)),
                pl.BlockSpec((rows, own), lambda i, place: (0, 0)),
                pl.BlockSpec((rows, own), lambda i, place: (0, 0)),
            ],
        ),
        out_shape=[
            pltpu.HBM((parts // 2, 2, rows, own), BF16),
            pltpu.HBM((rows, own), F32),
            pltpu.HBM((rows, own), F32),
        ],
        compiler_params=pltpu.CompilerParams(vmem_limit_bytes=16 * MIB),
        name="branch",
    )(place, in_hbm(gated), in_hbm(w_out), in_hbm(tokens), *pins)


def input_kernel(
    pins, extra, place, ids, weights, half_sent, prex, prez, wx, wz, tok, tok_own, cot, gain, *rest
):
    if extra:
        keep_z, come_z = rest[:2]
        grad_z = rest[pins + 2 + 7]
        grad_z[...] = keep_z[...] + come_z[...].astype(F32)
        rest = rest[2 : pins + 2 + 7] + rest[pins + 2 + 8 :]
    send, keep, keep_far, stats, slope, shift, base, inv, dots = rest[pins:]
    i = pl.program_id(0)
    rows, width = tok.shape

    @pl.when(i == 0)
    def _():
        value = tok[...].astype(F32)
        inv[...] = jnp.broadcast_to(
            lax.rsqrt(jnp.mean(value * value, axis=1, keepdims=True) + EPS), inv.shape
        )
        dots[...] = jnp.zeros_like(dots)

    value = mm_nt(prex[...], wx[...]) + mm_nt(prez[...], wz[...])
    rms = inv[:, 0:1]
    unit = tok_own[...].astype(F32) * rms
    by_unit = value * unit
    dots[...] += jnp.sum(by_unit * gain[...], axis=1, keepdims=True)
    line = jnp.sum(by_unit, axis=0, keepdims=True)
    own = line.shape[1] // LANES
    first = rows // LANES + (place[1] ^ i) * own
    for j in range(own):
        stats[pl.ds(first + j, 1), :] = line[:, j * LANES : (j + 1) * LANES]

    @pl.when(i == 0)
    def _():
        slope[...] = rms * gain[...]
        shift[...] = unit * rms * (1.0 / width)
        base[...] = cot[...].astype(F32) * weights[ids[0]]

    @pl.when(i == 0)
    def _():
        keep[...] = value

    @pl.when(i == 2)
    def _():
        keep_far[...] = value

    @pl.when(i % 2 == 1)
    def _():
        send[0, 0] = value.astype(BF16)

    @pl.when(i == pl.num_programs(0) - 1)
    def _():
        flat = jnp.transpose(dots[...])
        for c in range(rows // LANES):
            stats[c : c + 1, :] = flat[0:1, c * LANES : (c + 1) * LANES]


def input_grad(
    place, group_ids, group_weights, half_sent, prex, prez, w_x, w_z, tokens, cotangent, norm_gain,
    parts, extra, pins,
):
    rows, inner = prex.shape
    width = tokens.shape[1]
    own = width // parts
    whole = lambda shape: pl.BlockSpec(shape, lambda i, place: (0, 0))
    part = pl.BlockSpec((own, inner), lambda i, place: (place[1] ^ i, 0))
    mine = pl.BlockSpec((rows, own), lambda i, place: (0, 0))
    smem = pl.BlockSpec(memory_space=pltpu.SMEM)
    strip = lambda value: pl.BlockSpec(
        (value.shape[0] // parts, value.shape[1]), lambda i, place: (i, 0)
    )
    stat_rows = rows // LANES + width // LANES
    return pl.pallas_call(
        functools.partial(input_kernel, len(pins), len(extra)),
        grid_spec=pltpu.PrefetchScalarGridSpec(
            num_scalar_prefetch=1,
            grid=(parts,),
            in_specs=[
                smem,
                smem,
                ANY,
                whole((rows, inner)),
                whole((rows, inner)),
                part,
                part,
                whole((rows, width)),
                pl.BlockSpec((rows, own), lambda i, place: (0, place[1] ^ i)),
                pl.BlockSpec((rows, own), lambda i, place: (0, place[1])),
                pl.BlockSpec((1, own), lambda i, place: (0, place[1] ^ i)),
            ]
            + [strip(value) for value in extra]
            + [ANY] * len(pins),
            out_specs=[
                pl.BlockSpec((1, 1, rows, own), lambda i, place: (i // 2, 1, 0, 0)),
                mine,
                mine,
            ]
            + [whole((stat_rows, LANES)), mine, mine, mine]
            + [strip(value) for value in extra[:1]],
            scratch_shapes=[pltpu.VMEM((rows, LANES), F32)] * 2,
        ),
        out_shape=[
            pltpu.HBM((parts // 2, 2, rows, own), BF16),
            pltpu.HBM((rows, own), F32),
            pltpu.HBM((rows, own), F32),
            jax.ShapeDtypeStruct((stat_rows, LANES), F32),
        ]
        + [pltpu.HBM((rows, own), F32)] * 3
        + [jax.ShapeDtypeStruct(value.shape, F32) for value in extra[:1]],
        compiler_params=pltpu.CompilerParams(vmem_limit_bytes=24 * MIB),
        input_output_aliases={3: 0},
        name="inputs",
    )(
        place, group_ids, group_weights, in_hbm(half_sent), in_hbm(prex), in_hbm(prez), in_hbm(w_x), in_hbm(w_z), in_hbm(tokens),
        in_hbm(tokens), in_hbm(cotangent), in_hbm(norm_gain[None]),
        *[in_hbm(value) for value in extra[:1]], *extra[1:], *pins,
    )


def middle_kernel(
    place, gated, gated_far, up_own, up_a, up_b, every, wo, tok, small, small_come, *rest
):
    keep_out, later, send_out, send, keep, keep_far, small_keep, small_send = rest[len(rest) - 8 :]
    i = pl.program_id(0)

    @pl.when(i == 0)
    def _():
        for j in range(2):
            small_keep[j] = small[j] + small_come[j].astype(F32)
            small_send[j] = (small[2 + j] + small_come[2 + j].astype(F32)).astype(BF16)

    rows = gated.shape[0]
    half = rows // 2
    first = (place[1] & 1) * half
    own = keep_out.shape[1]
    total = mm_tn(gated[...], up_own[...])
    total = total + mm_tn(gated_far[pl.ds(pl.multiple_of(first, half), half), :], up_a[...])
    other = pl.ds(pl.multiple_of(half - first, half), half)
    total = total + mm_tn(gated_far[other, :], up_b[...])
    keep_out[...] = total[:, :own]
    later[...] = total[:, own : 2 * own]
    send_out[0] = total[:, 2 * own : 3 * own].astype(BF16)
    send_out[1] = total[:, 3 * own :].astype(BF16)

    value = mm(every[...], wo[...])

    @pl.when(i == 0)
    def _():
        keep[...] = value + tok[...].astype(F32)

    @pl.when(i == 2)
    def _():
        keep_far[...] = value

    @pl.when(i % 2 == 1)
    def _():
        send[0, 0] = value.astype(BF16)


def middle(place, gated, gated_far, ups, w_out, tokens, small, small_come, parts, pins):
    rows, inner = gated.shape
    width = w_out.shape[1]
    own = width // parts
    blk = inner // parts
    out = ups[0].shape[1] // 4
    whole = lambda value: pl.BlockSpec(value.shape, lambda i, place: (0,) * value.ndim)
    cols = pl.BlockSpec((rows, blk), lambda i, place: (0, i))
    down = lambda wide: pl.BlockSpec((blk, wide), lambda i, place: (i, 0))
    return pl.pallas_call(
        middle_kernel,
        grid_spec=pltpu.PrefetchScalarGridSpec(
            num_scalar_prefetch=1,
            grid=(parts,),
            in_specs=[cols, cols]
            + [whole(value) for value in (*ups, gated)]
            + [
                pl.BlockSpec((inner, own), lambda i, place: (0, place[1] ^ i)),
                pl.BlockSpec((rows, own), lambda i, place: (0, place[1])),
                whole(small),
                whole(small_come),
            ]
            + [ANY] * len(pins),
            out_specs=[
                down(out),
                down(out),
                pl.BlockSpec((2, blk, out), lambda i, place: (0, i, 0)),
                pl.BlockSpec((1, 1, rows, own), lambda i, place: (i // 2, 0, 0, 0)),
                pl.BlockSpec((rows, own), lambda i, place: (0, 0)),
                pl.BlockSpec((rows, own), lambda i, place: (0, 0)),
            ]
            + [pl.BlockSpec((2, SMALL, inner), lambda i, place: (0, 0, 0))] * 2,
        ),
        out_shape=[
            pltpu.HBM((inner, out), F32),
            pltpu.HBM((inner, out), F32),
            pltpu.HBM((2, inner, out), BF16),
            pltpu.HBM((parts // 2, 2, rows, own), BF16),
            pltpu.HBM((rows, own), F32),
            pltpu.HBM((rows, own), F32),
            pltpu.HBM((2, SMALL, inner), F32),
            pltpu.HBM((2, SMALL, inner), BF16),
        ],
        compiler_params=pltpu.CompilerParams(vmem_limit_bytes=36 * MIB),
        name="middle",
    )(
        place, in_hbm(gated), gated_far, *ups, in_hbm(gated), in_hbm(w_out), in_hbm(tokens),
        in_hbm(small), small_come, *pins,
    )


def finale_kernel(
    rank, count, place, keep_x, come_x, keep_out, come_out, far_out, keep_a, keep_b, come_a,
    come_b, far_a, far_b, stats, slope, shift, base, g0, g2, g3,
    grad_x, grad_out, block, grad_in, up, down, keyq, conv, *rest,
):
    lines = rest[:3]
    top, table, dots = rest[3:]
    i = pl.program_id(0)

    @pl.when(i == 0)
    def _():
        tall = jnp.transpose(jnp.concatenate([stats[...]] * (SUB // stats.shape[0]), axis=0))
        for c in range(stats.shape[0]):
            dots[c * LANES : (c + 1) * LANES, :] = jnp.broadcast_to(
                tall[:, c : c + 1], (LANES, LANES)
            )

    grad_x[...] = keep_x[...] + come_x[...].astype(F32)
    grad_out[...] = keep_out[...] + come_out[0].astype(F32) + far_out[...].astype(F32)
    value = keep_a[...] + come_a[0, 0].astype(F32) + far_a[0].astype(F32)
    block[...] = value.astype(BF16)
    value = keep_b[...] + come_b[0, 0].astype(F32) + far_b[0].astype(F32)
    some = value.shape[0]
    dot = dots[pl.ds(pl.multiple_of(i * some, some), some), :][:, 0:1]
    grad_in[...] = value * slope[...] - shift[...] * dot + base[...]

    @pl.when(i == pl.num_programs(0) - 1)
    def _():
        size = g0.shape[0] // 2
        pieces = [(0, g0, 0), (4, g0, 1), (1, g2, 0), (5, g2, 1)]
        pieces += [(p, g3, i) for i, p in enumerate((2, 6, 3, 7))]
        for p, source, i in pieces:
            at = pl.ds(pl.multiple_of((place[0] ^ p) * size, SUB), size)
            table[at, :] = source[i * size : (i + 1) * size, :].astype(F32)
        up[...] = table[:rank, :]
        down[...] = jnp.transpose(table[rank : 2 * rank, :])
        keyq[...] = table[2 * rank : 2 * rank + count, :]
        first = 2 * rank + count
        conv[...] = table[first : first + conv.shape[0], :]
        first += conv.shape[0]
        for i, line in enumerate(lines):
            line[...] = table[first + i : first + i + 1, :]
        tops = table[first + len(lines) : first + len(lines) + 1, :]
        tops = tops + table[first + len(lines) + 1 : first + len(lines) + 2, :]
        top[...] = jnp.broadcast_to(jnp.max(tops, axis=1, keepdims=True), top.shape)


def finale(
    place, keep_x, come_x, keep_out, come_out, far_out, out_keep, keep, come, far, stats, slope,
    shift, base, pieces, rank, count, taps,
):
    size, inner = keep_x.shape
    rows, own = slope.shape
    steps = 2
    whole = lambda shape: pl.BlockSpec(shape, lambda i: (0,) * len(shape))
    strip = lambda high, wide: pl.BlockSpec((high // steps, wide), lambda i: (i, 0))
    kept = strip(rows, own)
    came = lambda j: pl.BlockSpec((1, 1, rows // steps, own), lambda i: (0, j, i, 0))
    last = lambda j: pl.BlockSpec((1, rows // steps, own), lambda i: (j, i, 0))
    out = keep_out.shape[1]
    return pl.pallas_call(
        functools.partial(finale_kernel, rank, count),
        grid=(steps,),
        in_specs=[pl.BlockSpec(memory_space=pltpu.SMEM)]
        + [strip(size, inner)] * 2
        + [strip(inner, out)]
        + [pl.BlockSpec((1, inner // steps, out), lambda i: (0, i, 0)), strip(inner, out)]
        + [kept, kept, came(0), came(1), last(0), last(1)]
        + [whole(stats.shape)]
        + [strip(rows, own)] * 3
        + [whole(piece.shape) for piece in pieces],
        out_specs=[
            strip(size, inner),
            strip(inner, out),
            strip(rows, own),
            strip(rows, own),
            whole((rank, inner)),
            whole((inner, rank)),
            whole((count, inner)),
            whole((taps, inner)),
            *[whole((1, inner))] * 3,
            whole((SUB, LANES)),
        ],
        out_shape=[
            jax.ShapeDtypeStruct((size, inner), F32),
            jax.ShapeDtypeStruct((inner, out), F32),
            jax.ShapeDtypeStruct((rows, own), BF16),
            jax.ShapeDtypeStruct((rows, own), F32),
            jax.ShapeDtypeStruct((rank, inner), F32),
            jax.ShapeDtypeStruct((inner, rank), F32),
            jax.ShapeDtypeStruct((count, inner), F32),
            jax.ShapeDtypeStruct((taps, inner), F32),
            *[jax.ShapeDtypeStruct((1, inner), F32)] * 3,
            jax.ShapeDtypeStruct((SUB, LANES), F32),
        ],
        scratch_shapes=[pltpu.VMEM((8 * SMALL, inner), F32), pltpu.VMEM((rows, LANES), F32)],
        compiler_params=pltpu.CompilerParams(vmem_limit_bytes=32 * MIB),
        name="finale",
    )(
        place, in_hbm(keep_x), in_hbm(come_x), in_hbm(keep_out), in_hbm(come_out), in_hbm(far_out),
        in_hbm(out_keep), in_hbm(keep), in_hbm(come), in_hbm(come), in_hbm(far), in_hbm(far), stats, in_hbm(slope), in_hbm(shift), in_hbm(base),
        *pieces,
    )


def in_weight_kernel(pins, l0, l1, l2, l3, r0, r1, r2, r3, *rest):
    keep, send = rest[pins:]
    i = pl.program_id(0)
    total = None
    for left, right in ((l0[...], r0), (l1[...], r1), (l2[0], r2), (l3[...], r3)):
        term = mm_tn(left, right[...])
        total = term if total is None else total + term

    @pl.when(i == 0)
    def _():
        send[...] = total.astype(BF16)

    @pl.when(i == 1)
    def _():
        keep[...] = total


def in_weight(lefts, rights, pins):
    rows, inner = rights[0].shape
    own = lefts[0].shape[1] // 2
    whole = lambda value: pl.BlockSpec(value.shape, lambda i: (0,) * value.ndim)
    side = pl.BlockSpec((rows, own), lambda i: (0, 1 - i))
    return pl.pallas_call(
        functools.partial(in_weight_kernel, len(pins)),
        grid=(2,),
        in_specs=[side, side, pl.BlockSpec((1, rows, own), lambda i: (0, 0, 1 - i)), side]
        + [whole(r) for r in rights]
        + [ANY] * len(pins),
        out_specs=[pl.BlockSpec((own, inner), lambda i: (0, 0))] * 2,
        out_shape=[
            pltpu.HBM((own, inner), F32),
            pltpu.HBM((own, inner), BF16),
        ],
        compiler_params=pltpu.CompilerParams(vmem_limit_bytes=20 * MIB),
        name="inw",
    )(in_hbm(lefts[0]), *lefts[1:], in_hbm(rights[0]), *rights[1:], *pins)


def split_bits(axis):
    bits = bits_of(axis)
    return [bit for bit in (2, 1) if bit in bits], [bit for bit in reversed(bits) if bit > 2]


def gather_tokens(value, axis):
    pieces = [value]
    for bit in split_bits(axis)[0]:
        pieces = pieces + [swap(piece, axis, bit) for piece in pieces]
    return pieces


def exchange_cols(value, axis):
    size = lax.axis_size(axis)
    me = lax.axis_index(axis)
    gather, scatter = split_bits(axis)
    rows, cols = value.shape
    outer = 2 ** len(scatter)
    pieces = [value.reshape((rows, outer) + (2,) * len(gather) + (cols // size,))]
    for bit in gather:
        kept, sent = zip(*(halves(piece, 2, (me // bit) % 2) for piece in pieces))
        pieces = list(kept) + [swap(piece, axis, bit) for piece in sent]
    return [piece.reshape(rows, -1) for piece in pieces]


def scatter_sum(value, axis, dim):
    me = lax.axis_index(axis)
    scatter = split_bits(axis)[1]
    for bit in scatter:
        shape = value.shape
        split = shape[:dim] + (2, shape[dim] // 2) + shape[dim + 1 :]
        kept, sent = halves(value.reshape(split), dim, (me // bit) % 2)
        value = kept + swap(sent.astype(BF16), axis, bit).astype(F32)
    return value


def per_device(
    tokens,
    norm_gain,
    w_x,
    w_z,
    conv_weight,
    conv_bias,
    w_down,
    w_up,
    beta_bias,
    w_keyq,
    skip_gain,
    w_out,
    cotangent,
    group_ids,
    group_weights,
):
    rows, width = tokens.shape
    states = w_keyq.shape[1] // 2
    taps = conv_weight.shape[0]
    assert group_ids.shape[0] == 1
    parts = lax.axis_size("state")
    assert parts == 4
    dp_size = lax.axis_size("dp")
    own_width = width // parts
    state_index = lax.axis_index("state")
    place = jnp.stack([lax.axis_index("dp"), state_index]).astype(jnp.int32)
    blocked = dp_size if dp_size == 8 and width % (8 * LANES) == 0 else 0
    keyq_t = w_keyq.T

    normed, upstream_b, pre_x, mixed_b, dsilu, part, *blocks = front(
        place, group_ids, group_weights, tokens, cotangent, norm_gain, w_x,
        conv_weight, conv_bias, w_down, keyq_t, blocked,
    )
    summed = all_but_last(part, "state")
    pins_back = pins_conv = pins_inputs = extra = ()
    if blocked:
        far, near, own, up_far, up_own = blocks
        far = swap(far, "dp", 2)
        near = swap(near, "dp", 1)
        up_far = swap(up_far, "dp", 4)
        pins_back = (far, near, up_far)
    else:
        norm_parts = exchange_cols(normed, "dp")
        up_parts = exchange_cols(upstream_b, "dp")
    silu_z, dgate, grad_y = gate(normed, upstream_b, w_z, w_out)

    gated_b, prez_b, step_size, raw, peak, hist, last = scan_forward(
        summed, mixed_b, w_up, beta_bias, silu_z, dgate, skip_gain, states
    )
    if blocked:
        gated_far = swap(gated_b, "dp", 4)
        prez_far = swap(prez_b, "dp", 2)
        prez_near = swap(prez_b, "dp", 1)

    gmix, pay, ups = scan_backward(
        place, summed, mixed_b, w_up, step_size, raw, grad_y, hist, last, peak, pins_back
    )
    grads = all_but_last(pay, "state")
    if blocked:
        up_parts = (up_own, up_far, swap(up_far, "state", 1))
        (prez_far,) = after((prez_far,), (pay,))
        prez_last = swap(prez_far, "dp", 1)
        sides = (own, far, near, swap(near[1], "dp", 2))
        pins_conv = (gated_far, up_parts[2], prez_near, sides[3])

    prex_b, small, small_send = conv_back(
        place, summed, grads, mixed_b, grad_y, gmix, dsilu, pre_x, ups, conv_weight, skip_gain,
        w_down, keyq_t, dp_size, pins_conv,
    )

    if blocked:
        prex_far = swap(prex_b, "dp", 2)
        prex_near = swap(prex_b, "dp", 1)
        keep_z, send_z = in_weight(
            sides, (prez_b, prez_far, prez_near, prez_last), (in_hbm(prex_b),)
        )
        come_z = swap(send_z, "dp", 4)
        keep_out, later, send_out, half_sent, out_keep, out_far, small, small_send = middle(
            place, gated_b, gated_far, up_parts, w_out, tokens, small,
            swap(small_send, "dp", 1), parts,
            (in_hbm(send_z), prex_far, prex_near),
        )
        prex_last = swap(prex_far, "dp", 1)
        keep_x, send_x = in_weight(
            sides, (prex_b, prex_far, prex_near, prex_last), (in_hbm(send_out), come_z)
        )
        come_x = swap(send_x, "dp", 4)
        come_out = swap(send_out, "dp", 1)
        (small_send,) = after((small_send,), (in_hbm(send_x),))
        small = small + swap(small_send, "dp", 2).astype(F32)
        pins_inputs = (in_hbm(send_x),)
        extra = (keep_z, come_z)
    else:
        half_sent, out_keep, out_far = branch(place, gated_b, w_out, tokens, parts, ())
    send, keep, keep_far, stats, slope, shift, base, *grad_wz = input_grad(
        place, group_ids, group_weights, half_sent, prex_b, prez_b, w_x, w_z, tokens, cotangent,
        norm_gain, parts, extra, pins_inputs,
    )
    if blocked:
        (grad_wz,) = grad_wz
        far_send = (later + come_out[1].astype(F32)).astype(BF16)
        far_out = swap(far_send, "dp", 2)
        stats, small = after((stats, small), (in_hbm(come_x), in_hbm(come_out)))
    else:

        def weight_grad(value, left):
            pieces = gather_tokens(value, "dp")
            pairs = zip(pieces, up_parts) if left else zip(norm_parts, pieces)
            return scatter_sum(sum(mm_tn(a, b) for a, b in pairs), "dp", 1 if left else 0)

        grad_wout = weight_grad(gated_b, True)
        grad_wz = weight_grad(prez_b, False)
        grad_wx = weight_grad(prex_b, False)

    come = swap(send, "state", 1)
    pair = [(a + b.astype(F32)).astype(BF16) for a, b in zip((out_far, keep_far), come[1])]
    come_far = swap(jnp.stack(pair), "state", 2)
    stats = all_sum(stats, "state")
    if not blocked:
        block_out = out_keep + come[0, 0].astype(F32) + come_far[0].astype(F32)
        block_out = block_out.astype(BF16)
        norm_grad = keep + come[0, 1].astype(F32) + come_far[1].astype(F32)
        row_stat = stats[: rows // LANES].reshape(rows, 1)
        grad_in = norm_grad * slope - shift * row_stat + base
    gain_rows = own_width // LANES
    gain = lax.dynamic_slice_in_dim(
        stats, rows // LANES + state_index * gain_rows, gain_rows, 0
    )

    count = 2 * states
    rank = w_up.shape[0]
    if blocked:
        small = lax.reduce_precision(small.reshape(-1, small.shape[-1]), 8, 7)
        flipped = jnp.concatenate([small[SMALL:], small[:SMALL]], axis=0).astype(BF16)
        gathered = (small + swap(flipped, "dp", 4).astype(F32)).astype(BF16)
        gain = gain + swap(gain, "dp", 4)
        pieces = [gathered]
        for bit, pins in ((1, (in_hbm(come), in_hbm(far_send))), (2, ())):
            high = lax.reduce_precision(gain, 8, 7)
            rest = lax.reduce_precision(gain - high, 8, 7)
            line = jnp.concatenate([high.reshape(1, -1), rest.reshape(1, -1)], axis=1)
            tail = jnp.pad(line.astype(BF16), ((0, SUB - 1), (0, 0)))
            whole = jnp.concatenate([gathered, tail], axis=0)
            if pins:
                (whole,) = after((whole,), pins)
            got = swap(whole, "dp", bit)
            pieces.append(got[:-SUB])
            gathered = jnp.concatenate([gathered, got[:-SUB]], axis=0)
            other = got[-SUB].astype(F32)
            gain = (high + rest) + (other[:own_width] + other[own_width:]).reshape(gain.shape)
        grad_gain = gain.reshape(-1)
        grad_wx, grad_wout, block_out, grad_in, grad_up, down, keyq, *lines = finale(
            place, keep_x, come_x, keep_out, come_out, far_out, out_keep, keep, come, come_far,
            stats[: rows // LANES], slope, shift, base, pieces, rank, count, taps,
        )
    else:
        small = all_sum(small, "dp")
        grad_up = small[:rank]
        down = small[rank : 2 * rank].T
        keyq = small[2 * rank : 2 * rank + count]
        lines = small[2 * rank + count :]
        top = jnp.max(lines[taps + 3] + lines[taps + 4]).reshape(1, 1)
        lines = (lines[:taps], *[lines[taps + i : taps + i + 1] for i in range(3)], top)
        grad_gain = all_sum(gain, "dp").reshape(-1)
    grad_taps, grad_bias, grad_skip, grad_beta, top = lines
    return (
        block_out,
        grad_in,
        grad_gain,
        grad_wx,
        grad_wz,
        grad_taps,
        grad_bias[0],
        down,
        grad_up,
        grad_beta[0],
        keyq.T,
        grad_skip[0],
        grad_wout,
        top[0, 0],
    )


def solution(mesh):
    placed = (
        P("dp", None),
        P(),
        P(None, "state"),
        P(None, "state"),
        P(None, "state"),
        P("state"),
        P("state", None),
        P(None, "state"),
        P("state"),
        P("state", None),
        P("state"),
        P("state", None),
        P("dp", None),
        P("dp"),
        P(),
    )
    return jax.shard_map(
        per_device,
        mesh=mesh,
        in_specs=placed,
        out_specs=(
            P("dp", "state"),
            P("dp", "state"),
            P("state"),
            P("dp", "state"),
            P("dp", "state"),
            P(None, "state"),
            P("state"),
            P("state", None),
            P(None, "state"),
            P("state"),
            P("state", None),
            P("state"),
            P("state", "dp"),
            P(),
        ),
        check_vma=False,
    )
```

```python
import functools

import jax
import jax.numpy as jnp
from jax import lax
from jax.experimental import pallas as pl
from jax.experimental.pallas import tpu as pltpu
from jax.sharding import PartitionSpec as P

EPS = 1e-05
LANES = 128
SUB = 8
F32 = jnp.float32
BF16 = jnp.bfloat16
MIB = 2**20
WHOLE = pl.BlockSpec(memory_space=pltpu.VMEM)
ANY = pl.BlockSpec(memory_space=pl.ANY)
SMALL = 40


def mm(left, right):
    return jnp.dot(left, right, preferred_element_type=F32)


def mm_nt(left, right):
    return lax.dot_general(left, right, (((1,), (1,)), ((), ())), preferred_element_type=F32)


def mm_tn(left, right):
    return lax.dot_general(left, right, (((0,), (0,)), ((), ())), preferred_element_type=F32)


def swap(value, axis, bit):
    size = lax.axis_size(axis)
    return lax.ppermute(value, axis, [(i, i ^ bit) for i in range(size)])


def bits_of(axis):
    size = lax.axis_size(axis)
    bits, bit = [], 1
    while bit < size:
        bits.append(bit)
        bit *= 2
    return bits


def all_sum(value, axis):
    for bit in bits_of(axis):
        value = value + swap(value, axis, bit)
    return value


def all_max(value, axis):
    for bit in bits_of(axis):
        value = jnp.maximum(value, swap(value, axis, bit))
    return value


def halves(value, dim, bit_set):
    kept = lax.dynamic_index_in_dim(value, bit_set, dim, keepdims=False)
    sent = lax.dynamic_index_in_dim(value, 1 - bit_set, dim, keepdims=False)
    return kept, sent


def all_but_last(value, axis):
    bits = bits_of(axis)
    for bit in bits[:-1]:
        value = value + swap(value, axis, bit)
    return value, swap(value, axis, bits[-1])


def after(values, pins):
    def nothing(*refs):
        pass

    return pl.pallas_call(
        nothing,
        in_specs=[ANY] * (len(values) + len(pins)),
        out_specs=[ANY] * len(values),
        out_shape=[jax.ShapeDtypeStruct(value.shape, value.dtype) for value in values],
        input_output_aliases={i: i for i in range(len(values))},
        name="after",
    )(*values, *pins)


def in_hbm(value):
    return pltpu.with_memory_space_constraint(value, pltpu.HBM)


def shifted(value, by, rows):
    if by == 0:
        return value
    count = value.shape[0]
    moved = pltpu.roll(value, by % count, 0)
    keep = rows >= by if by > 0 else rows < count + by
    return jnp.where(keep, moved, 0.0)


def front_kernel(
    blocked, place, ids, weights, tok, cot, gain, wx, cw, cb, wd, wk,
    normed, up, prex, mixed, dsilu, part, *rest,
):
    step = pl.program_id(0)
    rows, width = tok.shape
    acc = rest[-1]

    @pl.when(step == 0)
    def _():
        value = tok[...].astype(F32)
        inv = lax.rsqrt(jnp.mean(value * value, axis=1, keepdims=True) + EPS)
        normed[...] = (value * inv * gain[...]).astype(BF16)
        part[...] = jnp.zeros_like(part)
        acc[...] = jnp.zeros_like(acc)

    pre = mm(normed[...], wx[...])
    prex[...] = pre
    row = lax.broadcasted_iota(jnp.int32, pre.shape, 0)
    taps = cw.shape[0]
    conv = cb[...] + sum(cw[j : j + 1, :] * shifted(pre, taps - 1 - j, row) for j in range(taps))
    sig = jax.nn.sigmoid(conv)
    mix = (conv * sig).astype(BF16)
    mixed[...] = mix
    dsilu[...] = sig * (1.0 + conv * (1.0 - sig))
    part[:rows, :] += mm(mix, wd[...])
    acc[...] += mm_nt(wk[...], mix)

    @pl.when(step == pl.num_programs(0) - 1)
    def _():
        wide = acc.shape[0]
        for c in range(rows // LANES):
            part[rows + c * wide : rows + (c + 1) * wide, :] = acc[:, c * LANES : (c + 1) * LANES]
        up[...] = (cot[...].astype(F32) * weights[ids[0]]).astype(BF16)
        if blocked:
            far, near, own, up_far, up_own = rest[:5]
            size = width // blocked
            for p in range(blocked):
                cols = pl.ds(pl.multiple_of((place[0] ^ p) * size, size), size)
                dest = near.at[p >> 1 & 1] if p & 1 else (far if p & 2 else own)
                dest[:, (p // 4) * size : (p // 4 + 1) * size] = normed[:, cols]
                at = (p & 1) * 2 + (p >> 1 & 1)
                at = slice(at * size, (at + 1) * size)
                if p & 4:
                    half = rows // 2
                    some = pl.ds(pl.multiple_of((place[1] & 1) * half, half), half)
                    up_far[:, at] = up[some, cols]
                else:
                    up_own[:, at] = up[:, cols]


def front(
    place, group_ids, group_weights, tokens, cotangent, norm_gain, w_x,
    conv_weight, conv_bias, w_down, w_keyq, blocked,
):
    rows, width = tokens.shape
    inner = w_x.shape[1]
    rank, kq = w_down.shape[1], w_keyq.shape[0]
    blk = min(inner, 512)
    whole = lambda shape: pl.BlockSpec(shape, lambda i: (0,) * len(shape))
    cols = lambda height: pl.BlockSpec((height, blk), lambda i: (0, i))
    smem = pl.BlockSpec(memory_space=pltpu.SMEM)
    part_rows = rows + kq * rows // LANES
    shapes = []
    if blocked:
        quarter, half = width // 4, width // 2
        shapes = [(rows, quarter), (2, rows, quarter), (rows, quarter), (rows // 2, half)]
        shapes += [(rows, half)]
    return pl.pallas_call(
        functools.partial(front_kernel, blocked),
        grid=(inner // blk,),
        in_specs=[
            smem,
            smem,
            smem,
            whole((rows, width)),
            whole((rows, width)),
            whole((1, width)),
            cols(width),
            cols(conv_weight.shape[0]),
            cols(1),
            pl.BlockSpec((blk, rank), lambda i: (i, 0)),
            cols(kq),
        ],
        out_specs=[
            whole((rows, width)),
            whole((rows, width)),
            cols(rows),
            cols(rows),
            cols(rows),
            whole((part_rows, LANES)),
        ]
        + [whole(shape) for shape in shapes],
        out_shape=[
            jax.ShapeDtypeStruct((rows, width), BF16),
            jax.ShapeDtypeStruct((rows, width), BF16),
            pltpu.HBM((rows, inner), F32),
            pltpu.HBM((rows, inner), BF16),
            pltpu.HBM((rows, inner), F32),
            jax.ShapeDtypeStruct((part_rows, LANES), F32),
        ]
        + [pltpu.HBM(shape, BF16) for shape in shapes],
        scratch_shapes=[pltpu.VMEM((kq, rows), F32)],
        compiler_params=pltpu.CompilerParams(vmem_limit_bytes=36 * MIB),
        name="front",
    )(
        place, group_ids, group_weights, in_hbm(tokens), in_hbm(cotangent),
        in_hbm(norm_gain[None]), in_hbm(w_x), in_hbm(conv_weight), in_hbm(conv_bias[None]),
        in_hbm(w_down), in_hbm(w_keyq),
    )


def gate_kernel(normed, up, wz, wo, silu, dgate, gy):
    pre = mm(normed[...], wz[...])
    back = mm_nt(up[...], wo[...])
    sig = jax.nn.sigmoid(pre)
    act = pre * sig
    silu[...] = act
    gy[...] = back * act
    dgate[...] = back * sig * (1.0 + pre * (1.0 - sig))


def gate(normed, upstream_b, w_z, w_out):
    rows, width = normed.shape
    inner = w_z.shape[1]
    blk = min(inner, 512)
    whole = lambda shape: pl.BlockSpec(shape, lambda i: (0, 0))
    cols = lambda height: pl.BlockSpec((height, blk), lambda i: (0, i))
    return pl.pallas_call(
        gate_kernel,
        grid=(inner // blk,),
        in_specs=[
            whole((rows, width)),
            whole((rows, width)),
            cols(width),
            pl.BlockSpec((blk, width), lambda i: (i, 0)),
        ],
        out_specs=[cols(rows)] * 3,
        out_shape=[jax.ShapeDtypeStruct((rows, inner), F32)] * 2 + [pltpu.HBM((rows, inner), F32)],
        compiler_params=pltpu.CompilerParams(vmem_limit_bytes=24 * MIB),
        name="gate",
    )(normed, upstream_b, in_hbm(w_z), in_hbm(w_out))


def key_query_of(one, two, rows, count):
    parts = []
    for c in range(rows // LANES):
        at = slice(rows + c * count, rows + (c + 1) * count)
        parts.append(one[at, :] + two[at, :])
    return jnp.transpose(jnp.concatenate(parts, axis=1))


def lay_tiles(dest, value, base=0):
    for j in range(SUB):
        dest[pl.ds(base * SUB + j, value.shape[0], stride=SUB), :] = value[
            :, j * LANES : (j + 1) * LANES
        ]


def lay_rows(source, count, j):
    return source[pl.ds(j, count, stride=SUB), :]


def spread(dest, key_query):
    rows, count = key_query.shape
    for n in range(count):
        dest[n * rows : (n + 1) * rows, :] = jnp.broadcast_to(
            key_query[:, n : n + 1], (rows, LANES)
        )


def pick(source, rows, n, t):
    return source[pl.ds(n * rows + t, SUB, stride=0), :]


def scan_kernel(
    unroll, one, two, mixed, wup, bias, silu, dgate, skip,
    gated, prez, step_out, raw_out, peak, hist, last, step_t, mix_t, out_t, kb, slots, sems,
):
    rows, inner = mixed.shape
    span = slots.shape[1]
    states = kb.shape[0] // rows // 2
    kq = key_query_of(one, two, rows, 2 * states)
    keys = kq[:, :states]
    norm = jnp.sum(keys * keys, axis=1, keepdims=True)
    spread(kb, kq)
    rank_b = (one[:rows, :] + two[:rows, :]).astype(BF16)
    raw = jax.nn.sigmoid(mm(rank_b, wup[...]) + bias[...])
    raw_out[...] = raw
    highest = jnp.max(jnp.max(raw, axis=0, keepdims=True), axis=1, keepdims=True)
    peak[...] = jnp.broadcast_to(highest, peak.shape)
    beta = raw.astype(BF16).astype(F32)
    size = beta / (1.0 + beta * norm)
    step_out[...] = size
    lay_tiles(step_t, size)
    lay_tiles(mix_t, mixed[...].astype(F32))

    def token(block, i, carried):
        t = block * span + i
        at = pl.ds(pl.multiple_of(t * SUB, SUB), SUB)
        size = step_t[at, :]
        mix = mix_t[at, :]
        sums = [None] * 4
        following = []
        for n in range(states):
            key = pick(kb, rows, n, t)
            query = pick(kb, rows, states + n, t)
            state = carried[n]
            if n % 2:
                pair = jnp.concatenate([carried[n - 1], state], axis=0)
                slots[block % 2, i, n // 2] = pair.astype(BF16)
            state = state + (size * key) * (mix - key * state)
            term = query * state
            sums[n % 4] = term if sums[n % 4] is None else sums[n % 4] + term
            following.append(state)
        out_t[at, :] = (sums[0] + sums[1]) + (sums[2] + sums[3])
        return tuple(following)

    zero = jnp.zeros((SUB, LANES), F32)
    final = (zero,) * states
    copies = []
    for block in range(rows // span):
        if block >= 2:
            copies[block - 2].wait()
        final = lax.fori_loop(0, span, functools.partial(token, block), final, unroll=unroll)
        copies.append(
            pltpu.make_async_copy(
                slots.at[block % 2], hist.at[pl.ds(block * span, span)], sems.at[block % 2]
            )
        )
        copies[-1].start()
    for n in range(states):
        last[n] = final[n]
    for j in range(SUB):
        at = slice(j * LANES, (j + 1) * LANES)
        y = lay_rows(out_t, rows, j) + skip[:, at] * mixed[:, at].astype(F32)
        gated[:, at] = (y * silu[:, at]).astype(BF16)
        prez[:, at] = (y * dgate[:, at]).astype(BF16)
    for copy in copies[-2:]:
        copy.wait()


def scan_forward(summed, mixed, w_up, beta_bias, silu, dgate, skip_gain, states):
    rows, inner = mixed.shape
    full = lambda dtype: jax.ShapeDtypeStruct((rows, inner), dtype)
    return pl.pallas_call(
        functools.partial(scan_kernel, 4),
        in_specs=[WHOLE] * 8,
        out_specs=[WHOLE] * 5 + [pl.BlockSpec(memory_space=pl.ANY), WHOLE],
        out_shape=[
            pltpu.HBM((rows, inner), BF16),
            pltpu.HBM((rows, inner), BF16),
            full(F32),
            full(F32),
            jax.ShapeDtypeStruct((SUB, LANES), F32),
            pltpu.HBM((rows, states // 2, 2 * SUB, LANES), BF16),
            jax.ShapeDtypeStruct((states, SUB, LANES), F32),
        ],
        scratch_shapes=[pltpu.VMEM((rows * SUB, LANES), F32)] * 3
        + [
            pltpu.VMEM((2 * states * rows, LANES), F32),
            pltpu.VMEM((2, rows // 8, states // 2, 2 * SUB, LANES), BF16),
            pltpu.SemaphoreType.DMA((2,)),
        ],
        compiler_params=pltpu.CompilerParams(vmem_limit_bytes=26 * MIB),
        name="scan",
    )(*summed, in_hbm(mixed), in_hbm(w_up), in_hbm(beta_bias[None]), silu, dgate, in_hbm(skip_gain[None]))


def back_kernel(
    unroll, pins, place, one, two, mixed, wup, step_in, raw_in, gy, hist, last, peak, *rest, ):
    gmix, pay, ups, preb, step_t, mix_t, gs_t, kb, sum_d, sum_s, prods, zk, zq, slots, sems = rest[
        pins:
    ]
    rows, inner = mixed.shape
    states = last.shape[0]
    rank = wup.shape[0]
    span = zk.shape[0] // states
    chunk = slots.shape[1]
    chunks = rows // chunk

    def fetch(block):
        return pltpu.make_async_copy(
            hist.at[pl.ds(block * chunk, chunk)], slots.at[block % 2], sems.at[block % 2]
        )

    fetch(chunks - 1).start()
    fetch(chunks - 2).start()
    kq = key_query_of(one, two, rows, 2 * states)
    keys = kq[:, :states]
    norm = jnp.sum(keys * keys, axis=1, keepdims=True)
    spread(kb, kq)
    lay_tiles(step_t, step_in[...])
    lay_tiles(mix_t, mixed[...].astype(F32) * 0.5)
    gs_t[0:SUB, :] = jnp.zeros((SUB, LANES), F32)
    lay_tiles(gs_t, gy[...].astype(BF16).astype(F32), 1)

    def reduce_to(dest, row, terms, slot):
        base = slot * states * SUB
        for n in range(states):
            prods[pl.ds(base + n * SUB, SUB), :] = terms[n]
        for g in range(states // SUB):
            total = None
            for s in range(SUB):
                part = prods[pl.ds(base + g * SUB * SUB + s, SUB, stride=SUB), :]
                total = part if total is None else total + part
            dest[pl.ds(row + g * SUB * span, SUB, stride=span), :] = total

    tail = gs_t[pl.ds(rows * SUB, SUB), :]
    reduce_to(zq, rows, [last[n] * tail for n in range(states)], 0)

    def token(block, i, u, carried):
        t = block * chunk + i
        at = pl.ds(pl.multiple_of(t * SUB, SUB), SUB)
        size = step_t[at, :]
        half = mix_t[at, :]
        before = gs_t[at, :]
        grad = gs_t[pl.ds(pl.multiple_of(t * SUB + SUB, SUB), SUB), :]
        drive = size * half
        total_d, total_s = [None] * 2, [None] * 2
        following, for_key, for_query = [], [], []
        for n in range(states):
            key = pick(kb, rows, n, t)
            query = pick(kb, rows, states + n, t)
            if n % 2 == 0:
                pair = slots[block % 2, i, n // 2].astype(F32)
            state = pair[n % 2 * SUB : (n % 2 + 1) * SUB]
            full = query * grad + carried[n]
            by_key = full * key
            by_state = by_key * state
            term = key * by_state
            following.append(full - key * (size * by_key))
            for_key.append(full * drive - size * by_state)
            for_query.append(state * before)
            h = n % 2
            total_d[h] = by_key if total_d[h] is None else total_d[h] + by_key
            total_s[h] = term if total_s[h] is None else total_s[h] + term
        sum_d[at, :] = total_d[0] + total_d[1]
        sum_s[at, :] = total_s[0] + total_s[1]
        reduce_to(zk, t, for_key, 2 * u)
        reduce_to(zq, t, for_query, 2 * u + 1)
        return tuple(following)

    def some(block, i, carried):
        for u in range(unroll):
            carried = token(block, chunk - 1 - (i * unroll + u), u, carried)
        return carried

    zero = jnp.zeros((SUB, LANES), F32)
    carried = (zero,) * states
    for block in reversed(range(chunks)):
        fetch(block).wait()
        carried = lax.fori_loop(0, chunk // unroll, functools.partial(some, block), carried)
        if block >= 2:
            fetch(block - 2).start()

    total_norm = jnp.zeros((rows, LANES), F32)
    for j in range(SUB):
        at = slice(j * LANES, (j + 1) * LANES)
        drive_grad = lay_rows(sum_d, rows, j)
        size = step_in[:, at]
        grad_step = drive_grad * mixed[:, at].astype(F32) - lay_rows(sum_s, rows, j)
        gmix[:, at] = drive_grad * size
        total_norm = total_norm - grad_step * size * size
        raw = raw_in[:, at]
        plus = 1.0 + raw.astype(BF16).astype(F32) * norm
        pre = grad_step / (plus * plus) * raw * (1.0 - raw)
        ups[rank : rank + SUB, at] = jnp.broadcast_to(
            jnp.sum(pre, axis=0, keepdims=True), (SUB, LANES)
        )
        preb[:, at] = pre.astype(BF16)
    pay[:rows, :] = mm_nt(preb[...], wup[...])
    rank_b = (one[:rows, :] + two[:rows, :]).astype(BF16)
    ups[:rank, :] = mm_tn(rank_b, preb[...])

    blocks = [zk[pl.ds(n * span, rows), :].astype(BF16) for n in range(states)]
    blocks += [zq[pl.ds(n * span + 1, rows), :].astype(BF16) for n in range(states)]
    norm_high = total_norm.astype(BF16)
    blocks += [norm_high, (total_norm - norm_high.astype(F32)).astype(BF16)]
    shape = (LANES * len(blocks), LANES)
    block = lax.broadcasted_iota(jnp.int32, shape, 0) // LANES
    target = jnp.minimum(block, 2 * states)
    weight = jnp.where(block < states, 2.0, 1.0)
    chosen = jnp.where(target == lax.broadcasted_iota(jnp.int32, shape, 1), weight, 0.0)
    table = mm(jnp.concatenate(blocks, axis=1), chosen.astype(BF16))
    lane = lax.broadcasted_iota(jnp.int32, (rows, LANES), 1)
    row = lax.broadcasted_iota(jnp.int32, (rows, LANES), 0)
    mark = (lane == 2 * states + 1) & (row == place[1])
    table = jnp.where(mark, jnp.broadcast_to(peak[0:1, :], (rows, LANES)), table)
    flat = jnp.transpose(table)
    high = (pay.shape[0] - rows) * LANES // rows
    for c in range(rows // LANES):
        pay[rows + c * high : rows + (c + 1) * high, :] = flat[:high, c * LANES : (c + 1) * LANES]


def scan_backward(place, summed, mixed, w_up, step_in, raw, gy, hist, last, peak, pins):
    rows, inner = mixed.shape
    states = last.shape[0]
    unroll = 2
    span = rows + SUB
    high = 2 * states + SUB
    pay_rows = rows + high * rows // LANES
    return pl.pallas_call(
        functools.partial(back_kernel, unroll, len(pins)),
        in_specs=[pl.BlockSpec(memory_space=pltpu.SMEM)]
        + [WHOLE] * 7
        + [ANY]
        + [WHOLE] * 2
        + [ANY] * len(pins),
        out_specs=[WHOLE] * 3,
        out_shape=[
            pltpu.HBM((rows, inner), F32),
            jax.ShapeDtypeStruct((pay_rows, LANES), F32),
            pltpu.HBM((w_up.shape[0] + SUB, inner), F32),
        ],
        scratch_shapes=[
            pltpu.VMEM((rows, inner), BF16),
            pltpu.VMEM((rows * SUB, LANES), F32),
            pltpu.VMEM((rows * SUB, LANES), F32),
            pltpu.VMEM((rows * SUB + SUB, LANES), F32),
            pltpu.VMEM((2 * states * rows, LANES), F32),
            pltpu.VMEM((rows * SUB, LANES), F32),
            pltpu.VMEM((rows * SUB, LANES), F32),
            pltpu.VMEM((unroll * 2 * states * SUB, LANES), F32),
            pltpu.VMEM((states * span, LANES), F32),
            pltpu.VMEM((states * span, LANES), F32),
            pltpu.VMEM((2, rows // 8, states // 2, 2 * SUB, LANES), BF16),
            pltpu.SemaphoreType.DMA((2,)),
        ],
        compiler_params=pltpu.CompilerParams(vmem_limit_bytes=32 * MIB),
        name="back",
    )(
        place, *summed, in_hbm(mixed), in_hbm(w_up), step_in, raw, in_hbm(gy),
        in_hbm(hist), last, peak, *pins,
    )


def conv_kernel(
    pins, parts, place, one, two, grad_one, grad_two, mixed, gy, gmix, dsilu, prex, ups, cw, skip,
    wd, wk, *rest,
):
    prex_b, keep, send, table, keys, ranks, top = rest[pins:]
    step = pl.program_id(0)
    rows, blk = mixed.shape
    rank = wd.shape[1]
    count = wk.shape[0]

    @pl.when(step == 0)
    def _():
        high = (grad_one.shape[0] - rows) * LANES // rows
        kq = key_query_of(one, two, rows, count)
        gkq = key_query_of(grad_one, grad_two, rows, high)
        norm_grad = gkq[:, count : count + 1]
        lane = lax.broadcasted_iota(jnp.int32, (rows, count), 1)
        by_norm = jnp.where(lane < count // 2, 2.0 * kq * norm_grad, 0.0)
        keys[...] = (gkq[:, :count] + by_norm).astype(BF16)
        ranks[...] = (grad_one[:rows, :] + grad_two[:rows, :]).astype(BF16)
        peak = jnp.max(gkq[:, count + 1 : count + 2], axis=0, keepdims=True)
        top[...] = jnp.broadcast_to(peak, top.shape)

    kq_b = keys[...]
    rank_b = ranks[...]
    peak = top[0:1, 0:1]
    peak_high = peak.astype(BF16).astype(F32)
    taps = cw.shape[0]
    first = 2 * rank + count
    table[:rank, :] = ups[:rank, :]
    table[rank : 2 * rank, :] = mm_tn(rank_b, mixed[...])
    table[2 * rank : first, :] = mm_tn(kq_b, mixed[...])
    mix = mixed[...].astype(F32)
    grad_y = gy[...]
    total = grad_y * skip[...] + gmix[...]
    total = total + mm(kq_b, wk[...]) + mm_nt(rank_b, wd[...])
    grad = total * dsilu[...]
    pre = prex[...]
    row = lax.broadcasted_iota(jnp.int32, grad.shape, 0)
    out = None
    sums = []
    for j in range(taps):
        by = taps - 1 - j
        sums.append(jnp.sum(grad * shifted(pre, by, row), axis=0, keepdims=True))
        term = cw[j : j + 1, :] * shifted(grad, -by, row)
        out = term if out is None else out + term
    sums.append(jnp.sum(grad, axis=0, keepdims=True))
    sums.append(jnp.sum(grad_y * mix, axis=0, keepdims=True))
    sums.append(ups[rank : rank + 1, :])
    channel = lax.broadcasted_iota(jnp.int32, (1, blk), 1) + step * blk
    for value in (peak_high, peak - peak_high):
        sums.append(jnp.where(channel == place[0], jnp.broadcast_to(value, (1, blk)), 0.0))
    for i, line in enumerate(sums):
        table[first + i : first + i + 1, :] = line
    table[first + len(sums) :, :] = jnp.zeros((table.shape[0] - first - len(sums), blk), F32)
    prex_b[...] = out.astype(BF16)
    if parts != 8:
        keep[...] = table[...]
        return
    size = table.shape[0] // parts
    for dest, order in ((keep, (0, 4, 2, 6)), (send, (1, 5, 3, 7))):
        for i, p in enumerate(order):
            at = pl.ds(pl.multiple_of((place[0] ^ p) * size, SUB), size)
            dest[i] = table[at, :].astype(dest.dtype)


def conv_back(
    place, summed, grads, mixed, gy, gmix, dsilu, prex, ups, conv_weight, skip_gain, w_down,
    w_keyq, parts, pins,
):
    rows, inner = mixed.shape
    rank, count = w_down.shape[1], w_keyq.shape[0]
    blk = min(inner, 512)
    high = 8 * SMALL
    whole = lambda value: pl.BlockSpec(value.shape, lambda i: (0,) * value.ndim)
    cols = lambda height: pl.BlockSpec((height, blk), lambda i: (0, i))
    if parts == 8:
        half = (4, SMALL, inner)
        half_spec = pl.BlockSpec((4, SMALL, blk), lambda i: (0, 0, i))
    else:
        half = (high, inner)
        half_spec = cols(high)
    return pl.pallas_call(
        functools.partial(conv_kernel, len(pins), parts),
        grid=(inner // blk,),
        in_specs=[pl.BlockSpec(memory_space=pltpu.SMEM)]
        + [whole(value) for value in (*summed, *grads)]
        + [cols(rows)] * 5
        + [cols(ups.shape[0]), cols(conv_weight.shape[0]), cols(1)]
        + [pl.BlockSpec((blk, rank), lambda i: (i, 0)), cols(count)]
        + [ANY] * len(pins),
        out_specs=[cols(rows), half_spec, half_spec],
        out_shape=[
            pltpu.HBM((rows, inner), BF16),
            pltpu.HBM(half, F32),
            pltpu.HBM(half, BF16),
        ],
        scratch_shapes=[
            pltpu.VMEM((high, blk), F32),
            pltpu.VMEM((rows, count), BF16),
            pltpu.VMEM((rows, rank), BF16),
            pltpu.VMEM((SUB, LANES), F32),
        ],
        compiler_params=pltpu.CompilerParams(vmem_limit_bytes=26 * MIB),
        name="conv",
    )(
        place, *summed, *grads, in_hbm(mixed), in_hbm(gy), in_hbm(gmix), in_hbm(dsilu),
        in_hbm(prex), in_hbm(ups), in_hbm(conv_weight), in_hbm(skip_gain[None]), in_hbm(w_down),
        in_hbm(w_keyq), *pins,
    )


def branch_kernel(pins, place, gated, wo, tok, *rest):
    send, keep, keep_far = rest[pins:]
    i = pl.program_id(0)
    value = mm(gated[...], wo[...])

    @pl.when(i == 0)
    def _():
        keep[...] = value + tok[...].astype(F32)

    @pl.when(i == 2)
    def _():
        keep_far[...] = value

    @pl.when(i % 2 == 1)
    def _():
        send[0, 0] = value.astype(BF16)


def branch(place, gated, w_out, tokens, parts, pins):
    rows, inner = gated.shape
    width = w_out.shape[1]
    own = width // parts
    return pl.pallas_call(
        functools.partial(branch_kernel, len(pins)),
        grid_spec=pltpu.PrefetchScalarGridSpec(
            num_scalar_prefetch=1,
            grid=(parts,),
            in_specs=[
                pl.BlockSpec((rows, inner), lambda i, place: (0, 0)),
                pl.BlockSpec((inner, own), lambda i, place: (0, place[1] ^ i)),
                pl.BlockSpec((rows, own), lambda i, place: (0, place[1])),
            ]
            + [ANY] * len(pins),
            out_specs=[
                pl.BlockSpec((1, 1, rows, own), lambda i, place: (i // 2, 0, 0, 0)),
                pl.BlockSpec((rows, own), lambda i, place: (0, 0)),
                pl.BlockSpec((rows, own), lambda i, place: (0, 0)),
            ],
        ),
        out_shape=[
            pltpu.HBM((parts // 2, 2, rows, own), BF16),
            pltpu.HBM((rows, own), F32),
            pltpu.HBM((rows, own), F32),
        ],
        compiler_params=pltpu.CompilerParams(vmem_limit_bytes=16 * MIB),
        name="branch",
    )(place, in_hbm(gated), in_hbm(w_out), in_hbm(tokens), *pins)


def input_kernel(
    pins, extra, place, ids, weights, half_sent, prex, prez, wx, wz, tok, tok_own, cot, gain, *rest
):
    if extra:
        keep_z, come_z = rest[:2]
        grad_z = rest[pins + 2 + 7]
        grad_z[...] = keep_z[...] + come_z[...].astype(F32)
        rest = rest[2 : pins + 2 + 7] + rest[pins + 2 + 8 :]
    send, keep, keep_far, stats, slope, shift, base, inv, dots = rest[pins:]
    i = pl.program_id(0)
    rows, width = tok.shape

    @pl.when(i == 0)
    def _():
        value = tok[...].astype(F32)
        inv[...] = jnp.broadcast_to(
            lax.rsqrt(jnp.mean(value * value, axis=1, keepdims=True) + EPS), inv.shape
        )
        dots[...] = jnp.zeros_like(dots)

    value = mm_nt(prex[...], wx[...]) + mm_nt(prez[...], wz[...])
    rms = inv[:, 0:1]
    unit = tok_own[...].astype(F32) * rms
    by_unit = value * unit
    dots[...] += jnp.sum(by_unit * gain[...], axis=1, keepdims=True)
    line = jnp.sum(by_unit, axis=0, keepdims=True)
    own = line.shape[1] // LANES
    first = rows // LANES + (place[1] ^ i) * own
    for j in range(own):
        stats[pl.ds(first + j, 1), :] = line[:, j * LANES : (j + 1) * LANES]

    @pl.when(i == 0)
    def _():
        slope[...] = rms * gain[...]
        shift[...] = unit * rms * (1.0 / width)
        base[...] = cot[...].astype(F32) * weights[ids[0]]

    @pl.when(i == 0)
    def _():
        keep[...] = value

    @pl.when(i == 2)
    def _():
        keep_far[...] = value

    @pl.when(i % 2 == 1)
    def _():
        send[0, 0] = value.astype(BF16)

    @pl.when(i == pl.num_programs(0) - 1)
    def _():
        flat = jnp.transpose(dots[...])
        for c in range(rows // LANES):
            stats[c : c + 1, :] = flat[0:1, c * LANES : (c + 1) * LANES]


def input_grad(
    place, group_ids, group_weights, half_sent, prex, prez, w_x, w_z, tokens, cotangent, norm_gain,
    parts, extra, pins,
):
    rows, inner = prex.shape
    width = tokens.shape[1]
    own = width // parts
    whole = lambda shape: pl.BlockSpec(shape, lambda i, place: (0, 0))
    part = pl.BlockSpec((own, inner), lambda i, place: (place[1] ^ i, 0))
    mine = pl.BlockSpec((rows, own), lambda i, place: (0, 0))
    smem = pl.BlockSpec(memory_space=pltpu.SMEM)
    strip = lambda value: pl.BlockSpec(
        (value.shape[0] // parts, value.shape[1]), lambda i, place: (i, 0)
    )
    stat_rows = rows // LANES + width // LANES
    return pl.pallas_call(
        functools.partial(input_kernel, len(pins), len(extra)),
        grid_spec=pltpu.PrefetchScalarGridSpec(
            num_scalar_prefetch=1,
            grid=(parts,),
            in_specs=[
                smem,
                smem,
                ANY,
                whole((rows, inner)),
                whole((rows, inner)),
                part,
                part,
                whole((rows, width)),
                pl.BlockSpec((rows, own), lambda i, place: (0, place[1] ^ i)),
                pl.BlockSpec((rows, own), lambda i, place: (0, place[1])),
                pl.BlockSpec((1, own), lambda i, place: (0, place[1] ^ i)),
            ]
            + [strip(value) for value in extra]
            + [ANY] * len(pins),
            out_specs=[
                pl.BlockSpec((1, 1, rows, own), lambda i, place: (i // 2, 1, 0, 0)),
                mine,
                mine,
            ]
            + [whole((stat_rows, LANES)), mine, mine, mine]
            + [strip(value) for value in extra[:1]],
            scratch_shapes=[pltpu.VMEM((rows, LANES), F32)] * 2,
        ),
        out_shape=[
            pltpu.HBM((parts // 2, 2, rows, own), BF16),
            pltpu.HBM((rows, own), F32),
            pltpu.HBM((rows, own), F32),
            jax.ShapeDtypeStruct((stat_rows, LANES), F32),
        ]
        + [pltpu.HBM((rows, own), F32)] * 3
        + [jax.ShapeDtypeStruct(value.shape, F32) for value in extra[:1]],
        compiler_params=pltpu.CompilerParams(vmem_limit_bytes=24 * MIB),
        input_output_aliases={3: 0},
        name="inputs",
    )(
        place, group_ids, group_weights, in_hbm(half_sent), in_hbm(prex), in_hbm(prez), in_hbm(w_x), in_hbm(w_z), in_hbm(tokens),
        in_hbm(tokens), in_hbm(cotangent), in_hbm(norm_gain[None]),
        *[in_hbm(value) for value in extra[:1]], *extra[1:], *pins,
    )


def middle_kernel(
    place, gated, gated_far, up_own, up_a, up_b, every, wo, tok, small, small_come, *rest
):
    keep_out, later, send_out, send, keep, keep_far, small_keep, small_send = rest[len(rest) - 8 :]
    i = pl.program_id(0)

    @pl.when(i == 0)
    def _():
        for j in range(2):
            small_keep[j] = small[j] + small_come[j].astype(F32)
            small_send[j] = (small[2 + j] + small_come[2 + j].astype(F32)).astype(BF16)

    rows = gated.shape[0]
    half = rows // 2
    first = (place[1] & 1) * half
    own = keep_out.shape[1]
    total = mm_tn(gated[...], up_own[...])
    total = total + mm_tn(gated_far[pl.ds(pl.multiple_of(first, half), half), :], up_a[...])
    other = pl.ds(pl.multiple_of(half - first, half), half)
    total = total + mm_tn(gated_far[other, :], up_b[...])
    keep_out[...] = total[:, :own]
    later[...] = total[:, own : 2 * own]
    send_out[0] = total[:, 2 * own : 3 * own].astype(BF16)
    send_out[1] = total[:, 3 * own :].astype(BF16)

    value = mm(every[...], wo[...])

    @pl.when(i == 0)
    def _():
        keep[...] = value + tok[...].astype(F32)

    @pl.when(i == 2)
    def _():
        keep_far[...] = value

    @pl.when(i % 2 == 1)
    def _():
        send[0, 0] = value.astype(BF16)


def middle(place, gated, gated_far, ups, w_out, tokens, small, small_come, parts, pins):
    rows, inner = gated.shape
    width = w_out.shape[1]
    own = width // parts
    blk = inner // parts
    out = ups[0].shape[1] // 4
    whole = lambda value: pl.BlockSpec(value.shape, lambda i, place: (0,) * value.ndim)
    cols = pl.BlockSpec((rows, blk), lambda i, place: (0, i))
    down = lambda wide: pl.BlockSpec((blk, wide), lambda i, place: (i, 0))
    return pl.pallas_call(
        middle_kernel,
        grid_spec=pltpu.PrefetchScalarGridSpec(
            num_scalar_prefetch=1,
            grid=(parts,),
            in_specs=[cols, cols]
            + [whole(value) for value in (*ups, gated)]
            + [
                pl.BlockSpec((inner, own), lambda i, place: (0, place[1] ^ i)),
                pl.BlockSpec((rows, own), lambda i, place: (0, place[1])),
                whole(small),
                whole(small_come),
            ]
            + [ANY] * len(pins),
            out_specs=[
                down(out),
                down(out),
                pl.BlockSpec((2, blk, out), lambda i, place: (0, i, 0)),
                pl.BlockSpec((1, 1, rows, own), lambda i, place: (i // 2, 0, 0, 0)),
                pl.BlockSpec((rows, own), lambda i, place: (0, 0)),
                pl.BlockSpec((rows, own), lambda i, place: (0, 0)),
            ]
            + [pl.BlockSpec((2, SMALL, inner), lambda i, place: (0, 0, 0))] * 2,
        ),
        out_shape=[
            pltpu.HBM((inner, out), F32),
            pltpu.HBM((inner, out), F32),
            pltpu.HBM((2, inner, out), BF16),
            pltpu.HBM((parts // 2, 2, rows, own), BF16),
            pltpu.HBM((rows, own), F32),
            pltpu.HBM((rows, own), F32),
            pltpu.HBM((2, SMALL, inner), F32),
            pltpu.HBM((2, SMALL, inner), BF16),
        ],
        compiler_params=pltpu.CompilerParams(vmem_limit_bytes=36 * MIB),
        name="middle",
    )(
        place, in_hbm(gated), gated_far, *ups, in_hbm(gated), in_hbm(w_out), in_hbm(tokens),
        in_hbm(small), small_come, *pins,
    )


def finale_kernel(
    rank, count, place, keep_x, come_x, keep_out, come_out, far_out, keep_a, keep_b, come_a,
    come_b, far_a, far_b, stats, slope, shift, base, g0, g2, g3,
    grad_x, grad_out, block, grad_in, up, down, keyq, conv, *rest,
):
    lines = rest[:3]
    top, table, dots = rest[3:]
    i = pl.program_id(0)

    @pl.when(i == 0)
    def _():
        tall = jnp.transpose(jnp.concatenate([stats[...]] * (SUB // stats.shape[0]), axis=0))
        for c in range(stats.shape[0]):
            dots[c * LANES : (c + 1) * LANES, :] = jnp.broadcast_to(
                tall[:, c : c + 1], (LANES, LANES)
            )

    grad_x[...] = keep_x[...] + come_x[...].astype(F32)
    grad_out[...] = keep_out[...] + come_out[0].astype(F32) + far_out[...].astype(F32)
    value = keep_a[...] + come_a[0, 0].astype(F32) + far_a[0].astype(F32)
    block[...] = value.astype(BF16)
    value = keep_b[...] + come_b[0, 0].astype(F32) + far_b[0].astype(F32)
    some = value.shape[0]
    dot = dots[pl.ds(pl.multiple_of(i * some, some), some), :][:, 0:1]
    grad_in[...] = value * slope[...] - shift[...] * dot + base[...]

    @pl.when(i == pl.num_programs(0) - 1)
    def _():
        size = g0.shape[0] // 2
        pieces = [(0, g0, 0), (4, g0, 1), (1, g2, 0), (5, g2, 1)]
        pieces += [(p, g3, i) for i, p in enumerate((2, 6, 3, 7))]
        for p, source, i in pieces:
            at = pl.ds(pl.multiple_of((place[0] ^ p) * size, SUB), size)
            table[at, :] = source[i * size : (i + 1) * size, :].astype(F32)
        up[...] = table[:rank, :]
        down[...] = jnp.transpose(table[rank : 2 * rank, :])
        keyq[...] = table[2 * rank : 2 * rank + count, :]
        first = 2 * rank + count
        conv[...] = table[first : first + conv.shape[0], :]
        first += conv.shape[0]
        for i, line in enumerate(lines):
            line[...] = table[first + i : first + i + 1, :]
        tops = table[first + len(lines) : first + len(lines) + 1, :]
        tops = tops + table[first + len(lines) + 1 : first + len(lines) + 2, :]
        top[...] = jnp.broadcast_to(jnp.max(tops, axis=1, keepdims=True), top.shape)


def finale(
    place, keep_x, come_x, keep_out, come_out, far_out, out_keep, keep, come, far, stats, slope,
    shift, base, pieces, rank, count, taps,
):
    size, inner = keep_x.shape
    rows, own = slope.shape
    steps = 2
    whole = lambda shape: pl.BlockSpec(shape, lambda i: (0,) * len(shape))
    strip = lambda high, wide: pl.BlockSpec((high // steps, wide), lambda i: (i, 0))
    kept = strip(rows, own)
    came = lambda j: pl.BlockSpec((1, 1, rows // steps, own), lambda i: (0, j, i, 0))
    last = lambda j: pl.BlockSpec((1, rows // steps, own), lambda i: (j, i, 0))
    out = keep_out.shape[1]
    return pl.pallas_call(
        functools.partial(finale_kernel, rank, count),
        grid=(steps,),
        in_specs=[pl.BlockSpec(memory_space=pltpu.SMEM)]
        + [strip(size, inner)] * 2
        + [strip(inner, out)]
        + [pl.BlockSpec((1, inner // steps, out), lambda i: (0, i, 0)), strip(inner, out)]
        + [kept, kept, came(0), came(1), last(0), last(1)]
        + [whole(stats.shape)]
        + [strip(rows, own)] * 3
        + [whole(piece.shape) for piece in pieces],
        out_specs=[
            strip(size, inner),
            strip(inner, out),
            strip(rows, own),
            strip(rows, own),
            whole((rank, inner)),
            whole((inner, rank)),
            whole((count, inner)),
            whole((taps, inner)),
            *[whole((1, inner))] * 3,
            whole((SUB, LANES)),
        ],
        out_shape=[
            jax.ShapeDtypeStruct((size, inner), F32),
            jax.ShapeDtypeStruct((inner, out), F32),
            jax.ShapeDtypeStruct((rows, own), BF16),
            jax.ShapeDtypeStruct((rows, own), F32),
            jax.ShapeDtypeStruct((rank, inner), F32),
            jax.ShapeDtypeStruct((inner, rank), F32),
            jax.ShapeDtypeStruct((count, inner), F32),
            jax.ShapeDtypeStruct((taps, inner), F32),
            *[jax.ShapeDtypeStruct((1, inner), F32)] * 3,
            jax.ShapeDtypeStruct((SUB, LANES), F32),
        ],
        scratch_shapes=[pltpu.VMEM((8 * SMALL, inner), F32), pltpu.VMEM((rows, LANES), F32)],
        compiler_params=pltpu.CompilerParams(vmem_limit_bytes=32 * MIB),
        name="finale",
    )(
        place, in_hbm(keep_x), in_hbm(come_x), in_hbm(keep_out), in_hbm(come_out), in_hbm(far_out),
        in_hbm(out_keep), in_hbm(keep), in_hbm(come), in_hbm(come), in_hbm(far), in_hbm(far), stats, in_hbm(slope), in_hbm(shift), in_hbm(base),
        *pieces,
    )


def in_weight_kernel(pins, l0, l1, l2, l3, r0, r1, r2, r3, *rest):
    keep, send = rest[pins:]
    i = pl.program_id(0)
    total = None
    for left, right in ((l0[...], r0), (l1[...], r1), (l2[0], r2), (l3[...], r3)):
        term = mm_tn(left, right[...])
        total = term if total is None else total + term

    @pl.when(i == 0)
    def _():
        send[...] = total.astype(BF16)

    @pl.when(i == 1)
    def _():
        keep[...] = total


def in_weight(lefts, rights, pins):
    rows, inner = rights[0].shape
    own = lefts[0].shape[1] // 2
    whole = lambda value: pl.BlockSpec(value.shape, lambda i: (0,) * value.ndim)
    side = pl.BlockSpec((rows, own), lambda i: (0, 1 - i))
    return pl.pallas_call(
        functools.partial(in_weight_kernel, len(pins)),
        grid=(2,),
        in_specs=[side, side, pl.BlockSpec((1, rows, own), lambda i: (0, 0, 1 - i)), side]
        + [whole(r) for r in rights]
        + [ANY] * len(pins),
        out_specs=[pl.BlockSpec((own, inner), lambda i: (0, 0))] * 2,
        out_shape=[
            pltpu.HBM((own, inner), F32),
            pltpu.HBM((own, inner), BF16),
        ],
        compiler_params=pltpu.CompilerParams(vmem_limit_bytes=20 * MIB),
        name="inw",
    )(in_hbm(lefts[0]), *lefts[1:], in_hbm(rights[0]), *rights[1:], *pins)


def split_bits(axis):
    bits = bits_of(axis)
    return [bit for bit in (2, 1) if bit in bits], [bit for bit in reversed(bits) if bit > 2]


def gather_tokens(value, axis):
    pieces = [value]
    for bit in split_bits(axis)[0]:
        pieces = pieces + [swap(piece, axis, bit) for piece in pieces]
    return pieces


def exchange_cols(value, axis):
    size = lax.axis_size(axis)
    me = lax.axis_index(axis)
    gather, scatter = split_bits(axis)
    rows, cols = value.shape
    outer = 2 ** len(scatter)
    pieces = [value.reshape((rows, outer) + (2,) * len(gather) + (cols // size,))]
    for bit in gather:
        kept, sent = zip(*(halves(piece, 2, (me // bit) % 2) for piece in pieces))
        pieces = list(kept) + [swap(piece, axis, bit) for piece in sent]
    return [piece.reshape(rows, -1) for piece in pieces]


def scatter_sum(value, axis, dim):
    me = lax.axis_index(axis)
    scatter = split_bits(axis)[1]
    for bit in scatter:
        shape = value.shape
        split = shape[:dim] + (2, shape[dim] // 2) + shape[dim + 1 :]
        kept, sent = halves(value.reshape(split), dim, (me // bit) % 2)
        value = kept + swap(sent.astype(BF16), axis, bit).astype(F32)
    return value


def per_device(
    tokens,
    norm_gain,
    w_x,
    w_z,
    conv_weight,
    conv_bias,
    w_down,
    w_up,
    beta_bias,
    w_keyq,
    skip_gain,
    w_out,
    cotangent,
    group_ids,
    group_weights,
):
    rows, width = tokens.shape
    states = w_keyq.shape[1] // 2
    taps = conv_weight.shape[0]
    assert group_ids.shape[0] == 1
    parts = lax.axis_size("state")
    assert parts == 4
    dp_size = lax.axis_size("dp")
    own_width = width // parts
    state_index = lax.axis_index("state")
    place = jnp.stack([lax.axis_index("dp"), state_index]).astype(jnp.int32)
    blocked = dp_size if dp_size == 8 and width % (8 * LANES) == 0 else 0
    keyq_t = w_keyq.T

    normed, upstream_b, pre_x, mixed_b, dsilu, part, *blocks = front(
        place, group_ids, group_weights, tokens, cotangent, norm_gain, w_x,
        conv_weight, conv_bias, w_down, keyq_t, blocked,
    )
    summed = all_but_last(part, "state")
    pins_back = pins_conv = pins_inputs = extra = ()
    if blocked:
        far, near, own, up_far, up_own = blocks
        far = swap(far, "dp", 2)
        near = swap(near, "dp", 1)
        up_far = swap(up_far, "dp", 4)
        pins_back = (far, near, up_far)
    else:
        norm_parts = exchange_cols(normed, "dp")
        up_parts = exchange_cols(upstream_b, "dp")
    silu_z, dgate, grad_y = gate(normed, upstream_b, w_z, w_out)

    gated_b, prez_b, step_size, raw, peak, hist, last = scan_forward(
        summed, mixed_b, w_up, beta_bias, silu_z, dgate, skip_gain, states
    )
    if blocked:
        gated_far = swap(gated_b, "dp", 4)
        prez_far = swap(prez_b, "dp", 2)
        prez_near = swap(prez_b, "dp", 1)

    gmix, pay, ups = scan_backward(
        place, summed, mixed_b, w_up, step_size, raw, grad_y, hist, last, peak, pins_back
    )
    grads = all_but_last(pay, "state")
    if blocked:
        up_parts = (up_own, up_far, swap(up_far, "state", 1))
        (prez_far,) = after((prez_far,), (pay,))
        prez_last = swap(prez_far, "dp", 1)
        sides = (own, far, near, swap(near[1], "dp", 2))
        pins_conv = (gated_far, up_parts[2], prez_near, sides[3])

    prex_b, small, small_send = conv_back(
        place, summed, grads, mixed_b, grad_y, gmix, dsilu, pre_x, ups, conv_weight, skip_gain,
        w_down, keyq_t, dp_size, pins_conv,
    )

    if blocked:
        prex_far = swap(prex_b, "dp", 2)
        prex_near = swap(prex_b, "dp", 1)
        keep_z, send_z = in_weight(
            sides, (prez_b, prez_far, prez_near, prez_last), (in_hbm(prex_b),)
        )
        come_z = swap(send_z, "dp", 4)
        keep_out, later, send_out, half_sent, out_keep, out_far, small, small_send = middle(
            place, gated_b, gated_far, up_parts, w_out, tokens, small,
            swap(small_send, "dp", 1), parts,
            (in_hbm(send_z), prex_far, prex_near),
        )
        prex_last = swap(prex_far, "dp", 1)
        keep_x, send_x = in_weight(
            sides, (prex_b, prex_far, prex_near, prex_last), (in_hbm(send_out), come_z)
        )
        come_x = swap(send_x, "dp", 4)
        come_out = swap(send_out, "dp", 1)
        (small_send,) = after((small_send,), (in_hbm(send_x),))
        small = small + swap(small_send, "dp", 2).astype(F32)
        pins_inputs = (in_hbm(send_x),)
        extra = (keep_z, come_z)
    else:
        half_sent, out_keep, out_far = branch(place, gated_b, w_out, tokens, parts, ())
    send, keep, keep_far, stats, slope, shift, base, *grad_wz = input_grad(
        place, group_ids, group_weights, half_sent, prex_b, prez_b, w_x, w_z, tokens, cotangent,
        norm_gain, parts, extra, pins_inputs,
    )
    if blocked:
        (grad_wz,) = grad_wz
        far_send = (later + come_out[1].astype(F32)).astype(BF16)
        far_out = swap(far_send, "dp", 2)
        stats, small = after((stats, small), (in_hbm(come_x), in_hbm(come_out)))
    else:

        def weight_grad(value, left):
            pieces = gather_tokens(value, "dp")
            pairs = zip(pieces, up_parts) if left else zip(norm_parts, pieces)
            return scatter_sum(sum(mm_tn(a, b) for a, b in pairs), "dp", 1 if left else 0)

        grad_wout = weight_grad(gated_b, True)
        grad_wz = weight_grad(prez_b, False)
        grad_wx = weight_grad(prex_b, False)

    come = swap(send, "state", 1)
    pair = [(a + b.astype(F32)).astype(BF16) for a, b in zip((out_far, keep_far), come[1])]
    come_far = swap(jnp.stack(pair), "state", 2)
    stats = all_sum(stats, "state")
    if not blocked:
        block_out = out_keep + come[0, 0].astype(F32) + come_far[0].astype(F32)
        block_out = block_out.astype(BF16)
        norm_grad = keep + come[0, 1].astype(F32) + come_far[1].astype(F32)
        row_stat = stats[: rows // LANES].reshape(rows, 1)
        grad_in = norm_grad * slope - shift * row_stat + base
    gain_rows = own_width // LANES
    gain = lax.dynamic_slice_in_dim(
        stats, rows // LANES + state_index * gain_rows, gain_rows, 0
    )

    count = 2 * states
    rank = w_up.shape[0]
    if blocked:
        small = lax.reduce_precision(small.reshape(-1, small.shape[-1]), 8, 7)
        flipped = jnp.concatenate([small[SMALL:], small[:SMALL]], axis=0).astype(BF16)
        gathered = (small + swap(flipped, "dp", 4).astype(F32)).astype(BF16)
        for bit in (4, 1, 2):
            gain = gain + swap(gain, "dp", bit)
        pieces = [gathered]
        for bit, pins in ((1, ()), (2, ())):
            if pins:
                (gathered,) = after((gathered,), pins)
            got = swap(gathered, "dp", bit)
            pieces.append(got)
            gathered = jnp.concatenate([gathered, got], axis=0)
        grad_gain = gain.reshape(-1)
        grad_wx, grad_wout, block_out, grad_in, grad_up, down, keyq, *lines = finale(
            place, keep_x, come_x, keep_out, come_out, far_out, out_keep, keep, come, come_far,
            stats[: rows // LANES], slope, shift, base, pieces, rank, count, taps,
        )
    else:
        small = all_sum(small, "dp")
        grad_up = small[:rank]
        down = small[rank : 2 * rank].T
        keyq = small[2 * rank : 2 * rank + count]
        lines = small[2 * rank + count :]
        top = jnp.max(lines[taps + 3] + lines[taps + 4]).reshape(1, 1)
        lines = (lines[:taps], *[lines[taps + i : taps + i + 1] for i in range(3)], top)
        grad_gain = all_sum(gain, "dp").reshape(-1)
    grad_taps, grad_bias, grad_skip, grad_beta, top = lines
    return (
        block_out,
        grad_in,
        grad_gain,
        grad_wx,
        grad_wz,
        grad_taps,
        grad_bias[0],
        down,
        grad_up,
        grad_beta[0],
        keyq.T,
        grad_skip[0],
        grad_wout,
        top[0, 0],
    )


def solution(mesh):
    placed = (
        P("dp", None),
        P(),
        P(None, "state"),
        P(None, "state"),
        P(None, "state"),
        P("state"),
        P("state", None),
        P(None, "state"),
        P("state"),
        P("state", None),
        P("state"),
        P("state", None),
        P("dp", None),
        P("dp"),
        P(),
    )
    return jax.shard_map(
        per_device,
        mesh=mesh,
        in_specs=placed,
        out_specs=(
            P("dp", "state"),
            P("dp", "state"),
            P("state"),
            P("dp", "state"),
            P("dp", "state"),
            P(None, "state"),
            P("state"),
            P("state", None),
            P(None, "state"),
            P("state"),
            P("state", None),
            P("state"),
            P("state", "dp"),
            P(),
        ),
        check_vma=False,
    )
```

```python
import functools

import jax
import jax.numpy as jnp
from jax import lax
from jax.experimental import pallas as pl
from jax.experimental.pallas import tpu as pltpu
from jax.sharding import PartitionSpec as P

EPS = 1e-05
LANES = 128
SUB = 8
F32 = jnp.float32
BF16 = jnp.bfloat16
MIB = 2**20
WHOLE = pl.BlockSpec(memory_space=pltpu.VMEM)
ANY = pl.BlockSpec(memory_space=pl.ANY)
SMALL = 40


def mm(left, right):
    return jnp.dot(left, right, preferred_element_type=F32)


def mm_nt(left, right):
    return lax.dot_general(left, right, (((1,), (1,)), ((), ())), preferred_element_type=F32)


def mm_tn(left, right):
    return lax.dot_general(left, right, (((0,), (0,)), ((), ())), preferred_element_type=F32)


def swap(value, axis, bit):
    size = lax.axis_size(axis)
    return lax.ppermute(value, axis, [(i, i ^ bit) for i in range(size)])


def bits_of(axis):
    size = lax.axis_size(axis)
    bits, bit = [], 1
    while bit < size:
        bits.append(bit)
        bit *= 2
    return bits


def all_sum(value, axis):
    for bit in bits_of(axis):
        value = value + swap(value, axis, bit)
    return value


def all_max(value, axis):
    for bit in bits_of(axis):
        value = jnp.maximum(value, swap(value, axis, bit))
    return value


def halves(value, dim, bit_set):
    kept = lax.dynamic_index_in_dim(value, bit_set, dim, keepdims=False)
    sent = lax.dynamic_index_in_dim(value, 1 - bit_set, dim, keepdims=False)
    return kept, sent


def all_but_last(value, axis):
    bits = bits_of(axis)
    for bit in bits[:-1]:
        value = value + swap(value, axis, bit)
    return value, swap(value, axis, bits[-1])


def after(values, pins):
    def nothing(*refs):
        pass

    return pl.pallas_call(
        nothing,
        in_specs=[ANY] * (len(values) + len(pins)),
        out_specs=[ANY] * len(values),
        out_shape=[jax.ShapeDtypeStruct(value.shape, value.dtype) for value in values],
        input_output_aliases={i: i for i in range(len(values))},
        name="after",
    )(*values, *pins)


def in_hbm(value):
    return pltpu.with_memory_space_constraint(value, pltpu.HBM)


def shifted(value, by, rows):
    if by == 0:
        return value
    count = value.shape[0]
    moved = pltpu.roll(value, by % count, 0)
    keep = rows >= by if by > 0 else rows < count + by
    return jnp.where(keep, moved, 0.0)


def front_kernel(
    blocked, place, ids, weights, tok, cot, gain, wx, cw, cb, wd, wk,
    normed, up, prex, mixed, dsilu, part, *rest,
):
    step = pl.program_id(0)
    rows, width = tok.shape
    acc = rest[-1]

    @pl.when(step == 0)
    def _():
        value = tok[...].astype(F32)
        inv = lax.rsqrt(jnp.mean(value * value, axis=1, keepdims=True) + EPS)
        normed[...] = (value * inv * gain[...]).astype(BF16)
        part[...] = jnp.zeros_like(part)
        acc[...] = jnp.zeros_like(acc)

    pre = mm(normed[...], wx[...])
    prex[...] = pre
    row = lax.broadcasted_iota(jnp.int32, pre.shape, 0)
    taps = cw.shape[0]
    conv = cb[...] + sum(cw[j : j + 1, :] * shifted(pre, taps - 1 - j, row) for j in range(taps))
    sig = jax.nn.sigmoid(conv)
    mix = (conv * sig).astype(BF16)
    mixed[...] = mix
    dsilu[...] = sig * (1.0 + conv * (1.0 - sig))
    part[:rows, :] += mm(mix, wd[...])
    acc[...] += mm_nt(wk[...], mix)

    @pl.when(step == pl.num_programs(0) - 1)
    def _():
        wide = acc.shape[0]
        for c in range(rows // LANES):
            part[rows + c * wide : rows + (c + 1) * wide, :] = acc[:, c * LANES : (c + 1) * LANES]
        up[...] = (cot[...].astype(F32) * weights[ids[0]]).astype(BF16)
        if blocked:
            far, near, own, up_far, up_own = rest[:5]
            size = width // blocked
            for p in range(blocked):
                cols = pl.ds(pl.multiple_of((place[0] ^ p) * size, size), size)
                dest = near.at[p >> 1 & 1] if p & 1 else (far if p & 2 else own)
                dest[:, (p // 4) * size : (p // 4 + 1) * size] = normed[:, cols]
                at = (p & 1) * 2 + (p >> 1 & 1)
                at = slice(at * size, (at + 1) * size)
                if p & 4:
                    half = rows // 2
                    some = pl.ds(pl.multiple_of((place[1] & 1) * half, half), half)
                    up_far[:, at] = up[some, cols]
                else:
                    up_own[:, at] = up[:, cols]


def front(
    place, group_ids, group_weights, tokens, cotangent, norm_gain, w_x,
    conv_weight, conv_bias, w_down, w_keyq, blocked,
):
    rows, width = tokens.shape
    inner = w_x.shape[1]
    rank, kq = w_down.shape[1], w_keyq.shape[0]
    blk = min(inner, 512)
    whole = lambda shape: pl.BlockSpec(shape, lambda i: (0,) * len(shape))
    cols = lambda height: pl.BlockSpec((height, blk), lambda i: (0, i))
    smem = pl.BlockSpec(memory_space=pltpu.SMEM)
    part_rows = rows + kq * rows // LANES
    shapes = []
    if blocked:
        quarter, half = width // 4, width // 2
        shapes = [(rows, quarter), (2, rows, quarter), (rows, quarter), (rows // 2, half)]
        shapes += [(rows, half)]
    return pl.pallas_call(
        functools.partial(front_kernel, blocked),
        grid=(inner // blk,),
        in_specs=[
            smem,
            smem,
            smem,
            whole((rows, width)),
            whole((rows, width)),
            whole((1, width)),
            cols(width),
            cols(conv_weight.shape[0]),
            cols(1),
            pl.BlockSpec((blk, rank), lambda i: (i, 0)),
            cols(kq),
        ],
        out_specs=[
            whole((rows, width)),
            whole((rows, width)),
            cols(rows),
            cols(rows),
            cols(rows),
            whole((part_rows, LANES)),
        ]
        + [whole(shape) for shape in shapes],
        out_shape=[
            jax.ShapeDtypeStruct((rows, width), BF16),
            jax.ShapeDtypeStruct((rows, width), BF16),
            pltpu.HBM((rows, inner), F32),
            pltpu.HBM((rows, inner), BF16),
            pltpu.HBM((rows, inner), F32),
            jax.ShapeDtypeStruct((part_rows, LANES), F32),
        ]
        + [pltpu.HBM(shape, BF16) for shape in shapes],
        scratch_shapes=[pltpu.VMEM((kq, rows), F32)],
        compiler_params=pltpu.CompilerParams(vmem_limit_bytes=36 * MIB),
        name="front",
    )(
        place, group_ids, group_weights, in_hbm(tokens), in_hbm(cotangent),
        in_hbm(norm_gain[None]), in_hbm(w_x), in_hbm(conv_weight), in_hbm(conv_bias[None]),
        in_hbm(w_down), in_hbm(w_keyq),
    )


def gate_kernel(normed, up, wz, wo, silu, dgate, gy):
    pre = mm(normed[...], wz[...])
    back = mm_nt(up[...], wo[...])
    sig = jax.nn.sigmoid(pre)
    act = pre * sig
    silu[...] = act
    gy[...] = back * act
    dgate[...] = back * sig * (1.0 + pre * (1.0 - sig))


def gate(normed, upstream_b, w_z, w_out):
    rows, width = normed.shape
    inner = w_z.shape[1]
    blk = min(inner, 512)
    whole = lambda shape: pl.BlockSpec(shape, lambda i: (0, 0))
    cols = lambda height: pl.BlockSpec((height, blk), lambda i: (0, i))
    return pl.pallas_call(
        gate_kernel,
        grid=(inner // blk,),
        in_specs=[
            whole((rows, width)),
            whole((rows, width)),
            cols(width),
            pl.BlockSpec((blk, width), lambda i: (i, 0)),
        ],
        out_specs=[cols(rows)] * 3,
        out_shape=[jax.ShapeDtypeStruct((rows, inner), F32)] * 2 + [pltpu.HBM((rows, inner), F32)],
        compiler_params=pltpu.CompilerParams(vmem_limit_bytes=24 * MIB),
        name="gate",
    )(normed, upstream_b, in_hbm(w_z), in_hbm(w_out))


def key_query_of(one, two, rows, count):
    parts = []
    for c in range(rows // LANES):
        at = slice(rows + c * count, rows + (c + 1) * count)
        parts.append(one[at, :] + two[at, :])
    return jnp.transpose(jnp.concatenate(parts, axis=1))


def lay_tiles(dest, value, base=0):
    for j in range(SUB):
        dest[pl.ds(base * SUB + j, value.shape[0], stride=SUB), :] = value[
            :, j * LANES : (j + 1) * LANES
        ]


def lay_rows(source, count, j):
    return source[pl.ds(j, count, stride=SUB), :]


def spread(dest, key_query):
    rows, count = key_query.shape
    for n in range(count):
        dest[n * rows : (n + 1) * rows, :] = jnp.broadcast_to(
            key_query[:, n : n + 1], (rows, LANES)
        )


def pick(source, rows, n, t):
    return source[pl.ds(n * rows + t, SUB, stride=0), :]


def scan_kernel(
    unroll, one, two, mixed, wup, bias, silu, dgate, skip,
    gated, prez, step_out, raw_out, peak, hist, last, step_t, mix_t, out_t, kb, slots, sems,
):
    rows, inner = mixed.shape
    span = slots.shape[1]
    states = kb.shape[0] // rows // 2
    kq = key_query_of(one, two, rows, 2 * states)
    keys = kq[:, :states]
    norm = jnp.sum(keys * keys, axis=1, keepdims=True)
    spread(kb, kq)
    rank_b = (one[:rows, :] + two[:rows, :]).astype(BF16)
    raw = jax.nn.sigmoid(mm(rank_b, wup[...]) + bias[...])
    raw_out[...] = raw
    highest = jnp.max(jnp.max(raw, axis=0, keepdims=True), axis=1, keepdims=True)
    peak[...] = jnp.broadcast_to(highest, peak.shape)
    beta = raw.astype(BF16).astype(F32)
    size = beta / (1.0 + beta * norm)
    step_out[...] = size
    lay_tiles(step_t, size)
    lay_tiles(mix_t, mixed[...].astype(F32))

    def token(block, i, carried):
        t = block * span + i
        at = pl.ds(pl.multiple_of(t * SUB, SUB), SUB)
        size = step_t[at, :]
        mix = mix_t[at, :]
        sums = [None] * 4
        following = []
        for n in range(states):
            key = pick(kb, rows, n, t)
            query = pick(kb, rows, states + n, t)
            state = carried[n]
            if n % 2:
                pair = jnp.concatenate([carried[n - 1], state], axis=0)
                slots[block % 2, i, n // 2] = pair.astype(BF16)
            state = state + (size * key) * (mix - key * state)
            term = query * state
            sums[n % 4] = term if sums[n % 4] is None else sums[n % 4] + term
            following.append(state)
        out_t[at, :] = (sums[0] + sums[1]) + (sums[2] + sums[3])
        return tuple(following)

    zero = jnp.zeros((SUB, LANES), F32)
    final = (zero,) * states
    copies = []
    for block in range(rows // span):
        if block >= 2:
            copies[block - 2].wait()
        final = lax.fori_loop(0, span, functools.partial(token, block), final, unroll=unroll)
        copies.append(
            pltpu.make_async_copy(
                slots.at[block % 2], hist.at[pl.ds(block * span, span)], sems.at[block % 2]
            )
        )
        copies[-1].start()
    for n in range(states):
        last[n] = final[n]
    for j in range(SUB):
        at = slice(j * LANES, (j + 1) * LANES)
        y = lay_rows(out_t, rows, j) + skip[:, at] * mixed[:, at].astype(F32)
        gated[:, at] = (y * silu[:, at]).astype(BF16)
        prez[:, at] = (y * dgate[:, at]).astype(BF16)
    for copy in copies[-2:]:
        copy.wait()


def scan_forward(summed, mixed, w_up, beta_bias, silu, dgate, skip_gain, states):
    rows, inner = mixed.shape
    full = lambda dtype: jax.ShapeDtypeStruct((rows, inner), dtype)
    return pl.pallas_call(
        functools.partial(scan_kernel, 8),
        in_specs=[WHOLE] * 8,
        out_specs=[WHOLE] * 5 + [pl.BlockSpec(memory_space=pl.ANY), WHOLE],
        out_shape=[
            pltpu.HBM((rows, inner), BF16),
            pltpu.HBM((rows, inner), BF16),
            full(F32),
            full(F32),
            jax.ShapeDtypeStruct((SUB, LANES), F32),
            pltpu.HBM((rows, states // 2, 2 * SUB, LANES), BF16),
            jax.ShapeDtypeStruct((states, SUB, LANES), F32),
        ],
        scratch_shapes=[pltpu.VMEM((rows * SUB, LANES), F32)] * 3
        + [
            pltpu.VMEM((2 * states * rows + SUB, LANES), F32),
            pltpu.VMEM((2, rows // 8, states // 2, 2 * SUB, LANES), BF16),
            pltpu.SemaphoreType.DMA((2,)),
        ],
        compiler_params=pltpu.CompilerParams(vmem_limit_bytes=26 * MIB),
        name="scan",
    )(*summed, in_hbm(mixed), in_hbm(w_up), in_hbm(beta_bias[None]), silu, dgate, in_hbm(skip_gain[None]))


def back_kernel(
    unroll, pins, place, one, two, mixed, wup, step_in, raw_in, gy, hist, last, peak, *rest, ):
    gmix, pay, ups, preb, step_t, mix_t, gs_t, kb, sum_d, sum_s, prods, zk, zq, slots, sems = rest[
        pins:
    ]
    rows, inner = mixed.shape
    states = last.shape[0]
    rank = wup.shape[0]
    span = rows + SUB
    chunk = slots.shape[1]
    chunks = rows // chunk

    def fetch(block):
        return pltpu.make_async_copy(
            hist.at[pl.ds(block * chunk, chunk)], slots.at[block % 2], sems.at[block % 2]
        )

    fetch(chunks - 1).start()
    fetch(chunks - 2).start()
    kq = key_query_of(one, two, rows, 2 * states)
    keys = kq[:, :states]
    norm = jnp.sum(keys * keys, axis=1, keepdims=True)
    spread(kb, kq)
    lay_tiles(step_t, step_in[...])
    lay_tiles(mix_t, mixed[...].astype(F32) * 0.5)
    gs_t[0:SUB, :] = jnp.zeros((SUB, LANES), F32)
    lay_tiles(gs_t, gy[...].astype(BF16).astype(F32), 1)

    def reduce_to(dest, row, terms, slot):
        base = slot * states * SUB
        for n in range(states):
            prods[pl.ds(base + n * SUB, SUB), :] = terms[n]
        for g in range(states // SUB):
            total = None
            for s in range(SUB):
                part = prods[pl.ds(base + g * SUB * SUB + s, SUB, stride=SUB), :]
                total = part if total is None else total + part
            dest[pl.ds(row + g * SUB * span, SUB, stride=span), :] = total

    tail = gs_t[pl.ds(rows * SUB, SUB), :]
    reduce_to(zq, rows, [last[n] * tail for n in range(states)], 0)

    def token(block, i, u, carried):
        t = block * chunk + i
        at = pl.ds(pl.multiple_of(t * SUB, SUB), SUB)
        size = step_t[at, :]
        half = mix_t[at, :]
        before = gs_t[at, :]
        grad = gs_t[pl.ds(pl.multiple_of(t * SUB + SUB, SUB), SUB), :]
        drive = size * half
        total_d, total_s = [None] * 2, [None] * 2
        following, for_key, for_query = [], [], []
        for n in range(states):
            key = pick(kb, rows, n, t)
            query = pick(kb, rows, states + n, t)
            if n % 2 == 0:
                pair = slots[block % 2, i, n // 2].astype(F32)
            state = pair[n % 2 * SUB : (n % 2 + 1) * SUB]
            full = query * grad + carried[n]
            by_key = full * key
            by_state = by_key * state
            term = key * by_state
            following.append(full - key * (size * by_key))
            for_key.append(full * drive - size * by_state)
            for_query.append(state * before)
            h = n % 2
            total_d[h] = by_key if total_d[h] is None else total_d[h] + by_key
            total_s[h] = term if total_s[h] is None else total_s[h] + term
        sum_d[at, :] = total_d[0] + total_d[1]
        sum_s[at, :] = total_s[0] + total_s[1]
        reduce_to(zk, t, for_key, 2 * u)
        reduce_to(zq, t, for_query, 2 * u + 1)
        return tuple(following)

    def some(block, i, carried):
        for u in range(unroll):
            carried = token(block, chunk - 1 - (i * unroll + u), u, carried)
        return carried

    zero = jnp.zeros((SUB, LANES), F32)
    carried = (zero,) * states
    for block in reversed(range(chunks)):
        fetch(block).wait()
        carried = lax.fori_loop(0, chunk // unroll, functools.partial(some, block), carried)
        if block >= 2:
            fetch(block - 2).start()

    total_norm = jnp.zeros((rows, LANES), F32)
    for j in range(SUB):
        at = slice(j * LANES, (j + 1) * LANES)
        drive_grad = lay_rows(sum_d, rows, j)
        size = step_in[:, at]
        grad_step = drive_grad * mixed[:, at].astype(F32) - lay_rows(sum_s, rows, j)
        gmix[:, at] = drive_grad * size
        total_norm = total_norm - grad_step * size * size
        raw = raw_in[:, at]
        plus = 1.0 + raw.astype(BF16).astype(F32) * norm
        pre = grad_step / (plus * plus) * raw * (1.0 - raw)
        ups[rank : rank + SUB, at] = jnp.broadcast_to(
            jnp.sum(pre, axis=0, keepdims=True), (SUB, LANES)
        )
        preb[:, at] = pre.astype(BF16)
    pay[:rows, :] = mm_nt(preb[...], wup[...])
    rank_b = (one[:rows, :] + two[:rows, :]).astype(BF16)
    ups[:rank, :] = mm_tn(rank_b, preb[...])

    blocks = [zk[pl.ds(n * span, rows), :].astype(BF16) for n in range(states)]
    blocks += [zq[pl.ds(n * span + 1, rows), :].astype(BF16) for n in range(states)]
    norm_high = total_norm.astype(BF16)
    blocks += [norm_high, (total_norm - norm_high.astype(F32)).astype(BF16)]
    shape = (LANES * len(blocks), LANES)
    block = lax.broadcasted_iota(jnp.int32, shape, 0) // LANES
    target = jnp.minimum(block, 2 * states)
    weight = jnp.where(block < states, 2.0, 1.0)
    chosen = jnp.where(target == lax.broadcasted_iota(jnp.int32, shape, 1), weight, 0.0)
    table = mm(jnp.concatenate(blocks, axis=1), chosen.astype(BF16))
    lane = lax.broadcasted_iota(jnp.int32, (rows, LANES), 1)
    row = lax.broadcasted_iota(jnp.int32, (rows, LANES), 0)
    mark = (lane == 2 * states + 1) & (row == place[1])
    table = jnp.where(mark, jnp.broadcast_to(peak[0:1, :], (rows, LANES)), table)
    flat = jnp.transpose(table)
    high = (pay.shape[0] - rows) * LANES // rows
    for c in range(rows // LANES):
        pay[rows + c * high : rows + (c + 1) * high, :] = flat[:high, c * LANES : (c + 1) * LANES]


def scan_backward(place, summed, mixed, w_up, step_in, raw, gy, hist, last, peak, pins):
    rows, inner = mixed.shape
    states = last.shape[0]
    unroll = 2
    span = rows + SUB
    high = 2 * states + SUB
    pay_rows = rows + high * rows // LANES
    return pl.pallas_call(
        functools.partial(back_kernel, unroll, len(pins)),
        in_specs=[pl.BlockSpec(memory_space=pltpu.SMEM)]
        + [WHOLE] * 7
        + [ANY]
        + [WHOLE] * 2
        + [ANY] * len(pins),
        out_specs=[WHOLE] * 3,
        out_shape=[
            pltpu.HBM((rows, inner), F32),
            jax.ShapeDtypeStruct((pay_rows, LANES), F32),
            pltpu.HBM((w_up.shape[0] + SUB, inner), F32),
        ],
        scratch_shapes=[
            pltpu.VMEM((rows, inner), BF16),
            pltpu.VMEM((rows * SUB, LANES), F32),
            pltpu.VMEM((rows * SUB, LANES), F32),
            pltpu.VMEM((rows * SUB + SUB, LANES), F32),
            pltpu.VMEM((2 * states * rows + SUB, LANES), F32),
            pltpu.VMEM((rows * SUB, LANES), F32),
            pltpu.VMEM((rows * SUB, LANES), F32),
            pltpu.VMEM((unroll * 2 * states * SUB + SUB * SUB, LANES), F32),
            pltpu.VMEM((states * span + span, LANES), F32),
            pltpu.VMEM((states * span + span, LANES), F32),
            pltpu.VMEM((2, rows // 8, states // 2, 2 * SUB, LANES), BF16),
            pltpu.SemaphoreType.DMA((2,)),
        ],
        compiler_params=pltpu.CompilerParams(vmem_limit_bytes=32 * MIB),
        name="back",
    )(
        place, *summed, in_hbm(mixed), in_hbm(w_up), step_in, raw, in_hbm(gy),
        in_hbm(hist), last, peak, *pins,
    )


def conv_kernel(
    pins, parts, place, one, two, grad_one, grad_two, mixed, gy, gmix, dsilu, prex, ups, cw, skip,
    wd, wk, *rest,
):
    prex_b, keep, send, table, keys, ranks, top = rest[pins:]
    step = pl.program_id(0)
    rows, blk = mixed.shape
    rank = wd.shape[1]
    count = wk.shape[0]

    @pl.when(step == 0)
    def _():
        high = (grad_one.shape[0] - rows) * LANES // rows
        kq = key_query_of(one, two, rows, count)
        gkq = key_query_of(grad_one, grad_two, rows, high)
        norm_grad = gkq[:, count : count + 1]
        lane = lax.broadcasted_iota(jnp.int32, (rows, count), 1)
        by_norm = jnp.where(lane < count // 2, 2.0 * kq * norm_grad, 0.0)
        keys[...] = (gkq[:, :count] + by_norm).astype(BF16)
        ranks[...] = (grad_one[:rows, :] + grad_two[:rows, :]).astype(BF16)
        peak = jnp.max(gkq[:, count + 1 : count + 2], axis=0, keepdims=True)
        top[...] = jnp.broadcast_to(peak, top.shape)

    kq_b = keys[...]
    rank_b = ranks[...]
    peak = top[0:1, 0:1]
    peak_high = peak.astype(BF16).astype(F32)
    taps = cw.shape[0]
    first = 2 * rank + count
    table[:rank, :] = ups[:rank, :]
    table[rank : 2 * rank, :] = mm_tn(rank_b, mixed[...])
    table[2 * rank : first, :] = mm_tn(kq_b, mixed[...])
    mix = mixed[...].astype(F32)
    grad_y = gy[...]
    total = grad_y * skip[...] + gmix[...]
    total = total + mm(kq_b, wk[...]) + mm_nt(rank_b, wd[...])
    grad = total * dsilu[...]
    pre = prex[...]
    row = lax.broadcasted_iota(jnp.int32, grad.shape, 0)
    out = None
    sums = []
    for j in range(taps):
        by = taps - 1 - j
        sums.append(jnp.sum(grad * shifted(pre, by, row), axis=0, keepdims=True))
        term = cw[j : j + 1, :] * shifted(grad, -by, row)
        out = term if out is None else out + term
    sums.append(jnp.sum(grad, axis=0, keepdims=True))
    sums.append(jnp.sum(grad_y * mix, axis=0, keepdims=True))
    sums.append(ups[rank : rank + 1, :])
    channel = lax.broadcasted_iota(jnp.int32, (1, blk), 1) + step * blk
    for value in (peak_high, peak - peak_high):
        sums.append(jnp.where(channel == place[0], jnp.broadcast_to(value, (1, blk)), 0.0))
    for i, line in enumerate(sums):
        table[first + i : first + i + 1, :] = line
    table[first + len(sums) :, :] = jnp.zeros((table.shape[0] - first - len(sums), blk), F32)
    prex_b[...] = out.astype(BF16)
    if parts != 8:
        keep[...] = table[...]
        return
    size = table.shape[0] // parts
    for dest, order in ((keep, (0, 4, 2, 6)), (send, (1, 5, 3, 7))):
        for i, p in enumerate(order):
            at = pl.ds(pl.multiple_of((place[0] ^ p) * size, SUB), size)
            dest[i] = table[at, :].astype(dest.dtype)


def conv_back(
    place, summed, grads, mixed, gy, gmix, dsilu, prex, ups, conv_weight, skip_gain, w_down,
    w_keyq, parts, pins,
):
    rows, inner = mixed.shape
    rank, count = w_down.shape[1], w_keyq.shape[0]
    blk = min(inner, 512)
    high = 8 * SMALL
    whole = lambda value: pl.BlockSpec(value.shape, lambda i: (0,) * value.ndim)
    cols = lambda height: pl.BlockSpec((height, blk), lambda i: (0, i))
    if parts == 8:
        half = (4, SMALL, inner)
        half_spec = pl.BlockSpec((4, SMALL, blk), lambda i: (0, 0, i))
    else:
        half = (high, inner)
        half_spec = cols(high)
    return pl.pallas_call(
        functools.partial(conv_kernel, len(pins), parts),
        grid=(inner // blk,),
        in_specs=[pl.BlockSpec(memory_space=pltpu.SMEM)]
        + [whole(value) for value in (*summed, *grads)]
        + [cols(rows)] * 5
        + [cols(ups.shape[0]), cols(conv_weight.shape[0]), cols(1)]
        + [pl.BlockSpec((blk, rank), lambda i: (i, 0)), cols(count)]
        + [ANY] * len(pins),
        out_specs=[cols(rows), half_spec, half_spec],
        out_shape=[
            pltpu.HBM((rows, inner), BF16),
            pltpu.HBM(half, F32),
            pltpu.HBM(half, BF16),
        ],
        scratch_shapes=[
            pltpu.VMEM((high, blk), F32),
            pltpu.VMEM((rows, count), BF16),
            pltpu.VMEM((rows, rank), BF16),
            pltpu.VMEM((SUB, LANES), F32),
        ],
        compiler_params=pltpu.CompilerParams(vmem_limit_bytes=26 * MIB),
        name="conv",
    )(
        place, *summed, *grads, in_hbm(mixed), in_hbm(gy), in_hbm(gmix), in_hbm(dsilu),
        in_hbm(prex), in_hbm(ups), in_hbm(conv_weight), in_hbm(skip_gain[None]), in_hbm(w_down),
        in_hbm(w_keyq), *pins,
    )


def branch_kernel(pins, place, gated, wo, tok, *rest):
    send, keep, keep_far = rest[pins:]
    i = pl.program_id(0)
    value = mm(gated[...], wo[...])

    @pl.when(i == 0)
    def _():
        keep[...] = value + tok[...].astype(F32)

    @pl.when(i == 2)
    def _():
        keep_far[...] = value

    @pl.when(i % 2 == 1)
    def _():
        send[0, 0] = value.astype(BF16)


def branch(place, gated, w_out, tokens, parts, pins):
    rows, inner = gated.shape
    width = w_out.shape[1]
    own = width // parts
    return pl.pallas_call(
        functools.partial(branch_kernel, len(pins)),
        grid_spec=pltpu.PrefetchScalarGridSpec(
            num_scalar_prefetch=1,
            grid=(parts,),
            in_specs=[
                pl.BlockSpec((rows, inner), lambda i, place: (0, 0)),
                pl.BlockSpec((inner, own), lambda i, place: (0, place[1] ^ i)),
                pl.BlockSpec((rows, own), lambda i, place: (0, place[1])),
            ]
            + [ANY] * len(pins),
            out_specs=[
                pl.BlockSpec((1, 1, rows, own), lambda i, place: (i // 2, 0, 0, 0)),
                pl.BlockSpec((rows, own), lambda i, place: (0, 0)),
                pl.BlockSpec((rows, own), lambda i, place: (0, 0)),
            ],
        ),
        out_shape=[
            pltpu.HBM((parts // 2, 2, rows, own), BF16),
            pltpu.HBM((rows, own), F32),
            pltpu.HBM((rows, own), F32),
        ],
        compiler_params=pltpu.CompilerParams(vmem_limit_bytes=16 * MIB),
        name="branch",
    )(place, in_hbm(gated), in_hbm(w_out), in_hbm(tokens), *pins)


def input_kernel(
    pins, extra, place, ids, weights, half_sent, prex, prez, wx, wz, tok, tok_own, cot, gain, *rest
):
    if extra:
        keep_z, come_z = rest[:2]
        grad_z = rest[pins + 2 + 7]
        grad_z[...] = keep_z[...] + come_z[...].astype(F32)
        rest = rest[2 : pins + 2 + 7] + rest[pins + 2 + 8 :]
    send, keep, keep_far, stats, slope, shift, base, inv, dots = rest[pins:]
    i = pl.program_id(0)
    rows, width = tok.shape

    @pl.when(i == 0)
    def _():
        value = tok[...].astype(F32)
        inv[...] = jnp.broadcast_to(
            lax.rsqrt(jnp.mean(value * value, axis=1, keepdims=True) + EPS), inv.shape
        )
        dots[...] = jnp.zeros_like(dots)

    value = mm_nt(prex[...], wx[...]) + mm_nt(prez[...], wz[...])
    rms = inv[:, 0:1]
    unit = tok_own[...].astype(F32) * rms
    by_unit = value * unit
    dots[...] += jnp.sum(by_unit * gain[...], axis=1, keepdims=True)
    line = jnp.sum(by_unit, axis=0, keepdims=True)
    own = line.shape[1] // LANES
    first = rows // LANES + (place[1] ^ i) * own
    for j in range(own):
        stats[pl.ds(first + j, 1), :] = line[:, j * LANES : (j + 1) * LANES]

    @pl.when(i == 0)
    def _():
        slope[...] = rms * gain[...]
        shift[...] = unit * rms * (1.0 / width)
        base[...] = cot[...].astype(F32) * weights[ids[0]]

    @pl.when(i == 0)
    def _():
        keep[...] = value

    @pl.when(i == 2)
    def _():
        keep_far[...] = value

    @pl.when(i % 2 == 1)
    def _():
        send[0, 0] = value.astype(BF16)

    @pl.when(i == pl.num_programs(0) - 1)
    def _():
        flat = jnp.transpose(dots[...])
        for c in range(rows // LANES):
            stats[c : c + 1, :] = flat[0:1, c * LANES : (c + 1) * LANES]


def input_grad(
    place, group_ids, group_weights, half_sent, prex, prez, w_x, w_z, tokens, cotangent, norm_gain,
    parts, extra, pins,
):
    rows, inner = prex.shape
    width = tokens.shape[1]
    own = width // parts
    whole = lambda shape: pl.BlockSpec(shape, lambda i, place: (0, 0))
    part = pl.BlockSpec((own, inner), lambda i, place: (place[1] ^ i, 0))
    mine = pl.BlockSpec((rows, own), lambda i, place: (0, 0))
    smem = pl.BlockSpec(memory_space=pltpu.SMEM)
    strip = lambda value: pl.BlockSpec(
        (value.shape[0] // parts, value.shape[1]), lambda i, place: (i, 0)
    )
    stat_rows = rows // LANES + width // LANES
    return pl.pallas_call(
        functools.partial(input_kernel, len(pins), len(extra)),
        grid_spec=pltpu.PrefetchScalarGridSpec(
            num_scalar_prefetch=1,
            grid=(parts,),
            in_specs=[
                smem,
                smem,
                ANY,
                whole((rows, inner)),
                whole((rows, inner)),
                part,
                part,
                whole((rows, width)),
                pl.BlockSpec((rows, own), lambda i, place: (0, place[1] ^ i)),
                pl.BlockSpec((rows, own), lambda i, place: (0, place[1])),
                pl.BlockSpec((1, own), lambda i, place: (0, place[1] ^ i)),
            ]
            + [strip(value) for value in extra]
            + [ANY] * len(pins),
            out_specs=[
                pl.BlockSpec((1, 1, rows, own), lambda i, place: (i // 2, 1, 0, 0)),
                mine,
                mine,
            ]
            + [whole((stat_rows, LANES)), mine, mine, mine]
            + [strip(value) for value in extra[:1]],
            scratch_shapes=[pltpu.VMEM((rows, LANES), F32)] * 2,
        ),
        out_shape=[
            pltpu.HBM((parts // 2, 2, rows, own), BF16),
            pltpu.HBM((rows, own), F32),
            pltpu.HBM((rows, own), F32),
            jax.ShapeDtypeStruct((stat_rows, LANES), F32),
        ]
        + [pltpu.HBM((rows, own), F32)] * 3
        + [jax.ShapeDtypeStruct(value.shape, F32) for value in extra[:1]],
        compiler_params=pltpu.CompilerParams(vmem_limit_bytes=24 * MIB),
        input_output_aliases={3: 0},
        name="inputs",
    )(
        place, group_ids, group_weights, in_hbm(half_sent), in_hbm(prex), in_hbm(prez), in_hbm(w_x), in_hbm(w_z), in_hbm(tokens),
        in_hbm(tokens), in_hbm(cotangent), in_hbm(norm_gain[None]),
        *[in_hbm(value) for value in extra[:1]], *extra[1:], *pins,
    )


def middle_kernel(
    place, gated, gated_far, up_own, up_a, up_b, every, wo, tok, small, small_come, *rest
):
    keep_out, later, send_out, send, keep, keep_far, small_keep, small_send = rest[len(rest) - 8 :]
    i = pl.program_id(0)

    @pl.when(i == 0)
    def _():
        for j in range(2):
            small_keep[j] = small[j] + small_come[j].astype(F32)
            small_send[j] = (small[2 + j] + small_come[2 + j].astype(F32)).astype(BF16)

    rows = gated.shape[0]
    half = rows // 2
    first = (place[1] & 1) * half
    own = keep_out.shape[1]
    total = mm_tn(gated[...], up_own[...])
    total = total + mm_tn(gated_far[pl.ds(pl.multiple_of(first, half), half), :], up_a[...])
    other = pl.ds(pl.multiple_of(half - first, half), half)
    total = total + mm_tn(gated_far[other, :], up_b[...])
    keep_out[...] = total[:, :own]
    later[...] = total[:, own : 2 * own]
    send_out[0] = total[:, 2 * own : 3 * own].astype(BF16)
    send_out[1] = total[:, 3 * own :].astype(BF16)

    value = mm(every[...], wo[...])

    @pl.when(i == 0)
    def _():
        keep[...] = value + tok[...].astype(F32)

    @pl.when(i == 2)
    def _():
        keep_far[...] = value

    @pl.when(i % 2 == 1)
    def _():
        send[0, 0] = value.astype(BF16)


def middle(place, gated, gated_far, ups, w_out, tokens, small, small_come, parts, pins):
    rows, inner = gated.shape
    width = w_out.shape[1]
    own = width // parts
    blk = inner // parts
    out = ups[0].shape[1] // 4
    whole = lambda value: pl.BlockSpec(value.shape, lambda i, place: (0,) * value.ndim)
    cols = pl.BlockSpec((rows, blk), lambda i, place: (0, i))
    down = lambda wide: pl.BlockSpec((blk, wide), lambda i, place: (i, 0))
    return pl.pallas_call(
        middle_kernel,
        grid_spec=pltpu.PrefetchScalarGridSpec(
            num_scalar_prefetch=1,
            grid=(parts,),
            in_specs=[cols, cols]
            + [whole(value) for value in (*ups, gated)]
            + [
                pl.BlockSpec((inner, own), lambda i, place: (0, place[1] ^ i)),
                pl.BlockSpec((rows, own), lambda i, place: (0, place[1])),
                whole(small),
                whole(small_come),
            ]
            + [ANY] * len(pins),
            out_specs=[
                down(out),
                down(out),
                pl.BlockSpec((2, blk, out), lambda i, place: (0, i, 0)),
                pl.BlockSpec((1, 1, rows, own), lambda i, place: (i // 2, 0, 0, 0)),
                pl.BlockSpec((rows, own), lambda i, place: (0, 0)),
                pl.BlockSpec((rows, own), lambda i, place: (0, 0)),
            ]
            + [pl.BlockSpec((2, SMALL, inner), lambda i, place: (0, 0, 0))] * 2,
        ),
        out_shape=[
            pltpu.HBM((inner, out), F32),
            pltpu.HBM((inner, out), F32),
            pltpu.HBM((2, inner, out), BF16),
            pltpu.HBM((parts // 2, 2, rows, own), BF16),
            pltpu.HBM((rows, own), F32),
            pltpu.HBM((rows, own), F32),
            pltpu.HBM((2, SMALL, inner), F32),
            pltpu.HBM((2, SMALL, inner), BF16),
        ],
        compiler_params=pltpu.CompilerParams(vmem_limit_bytes=36 * MIB),
        name="middle",
    )(
        place, in_hbm(gated), gated_far, *ups, in_hbm(gated), in_hbm(w_out), in_hbm(tokens),
        in_hbm(small), small_come, *pins,
    )


def finale_kernel(
    rank, count, place, keep_x, come_x, keep_out, come_out, far_out, keep_a, keep_b, come_a,
    come_b, far_a, far_b, stats, slope, shift, base, g0, g2, g3,
    grad_x, grad_out, block, grad_in, up, down, keyq, conv, *rest,
):
    lines = rest[:3]
    top, table, dots = rest[3:]
    i = pl.program_id(0)

    @pl.when(i == 0)
    def _():
        tall = jnp.transpose(jnp.concatenate([stats[...]] * (SUB // stats.shape[0]), axis=0))
        for c in range(stats.shape[0]):
            dots[c * LANES : (c + 1) * LANES, :] = jnp.broadcast_to(
                tall[:, c : c + 1], (LANES, LANES)
            )

    grad_x[...] = keep_x[...] + come_x[...].astype(F32)
    grad_out[...] = keep_out[...] + come_out[0].astype(F32) + far_out[...].astype(F32)
    value = keep_a[...] + come_a[0, 0].astype(F32) + far_a[0].astype(F32)
    block[...] = value.astype(BF16)
    value = keep_b[...] + come_b[0, 0].astype(F32) + far_b[0].astype(F32)
    some = value.shape[0]
    dot = dots[pl.ds(pl.multiple_of(i * some, some), some), :][:, 0:1]
    grad_in[...] = value * slope[...] - shift[...] * dot + base[...]

    @pl.when(i == pl.num_programs(0) - 1)
    def _():
        size = g0.shape[0] // 2
        pieces = [(0, g0, 0), (4, g0, 1), (1, g2, 0), (5, g2, 1)]
        pieces += [(p, g3, i) for i, p in enumerate((2, 6, 3, 7))]
        for p, source, i in pieces:
            at = pl.ds(pl.multiple_of((place[0] ^ p) * size, SUB), size)
            table[at, :] = source[i * size : (i + 1) * size, :].astype(F32)
        up[...] = table[:rank, :]
        down[...] = jnp.transpose(table[rank : 2 * rank, :])
        keyq[...] = table[2 * rank : 2 * rank + count, :]
        first = 2 * rank + count
        conv[...] = table[first : first + conv.shape[0], :]
        first += conv.shape[0]
        for i, line in enumerate(lines):
            line[...] = table[first + i : first + i + 1, :]
        tops = table[first + len(lines) : first + len(lines) + 1, :]
        tops = tops + table[first + len(lines) + 1 : first + len(lines) + 2, :]
        top[...] = jnp.broadcast_to(jnp.max(tops, axis=1, keepdims=True), top.shape)


def finale(
    place, keep_x, come_x, keep_out, come_out, far_out, out_keep, keep, come, far, stats, slope,
    shift, base, pieces, rank, count, taps,
):
    size, inner = keep_x.shape
    rows, own = slope.shape
    steps = 2
    whole = lambda shape: pl.BlockSpec(shape, lambda i: (0,) * len(shape))
    strip = lambda high, wide: pl.BlockSpec((high // steps, wide), lambda i: (i, 0))
    kept = strip(rows, own)
    came = lambda j: pl.BlockSpec((1, 1, rows // steps, own), lambda i: (0, j, i, 0))
    last = lambda j: pl.BlockSpec((1, rows // steps, own), lambda i: (j, i, 0))
    out = keep_out.shape[1]
    return pl.pallas_call(
        functools.partial(finale_kernel, rank, count),
        grid=(steps,),
        in_specs=[pl.BlockSpec(memory_space=pltpu.SMEM)]
        + [strip(size, inner)] * 2
        + [strip(inner, out)]
        + [pl.BlockSpec((1, inner // steps, out), lambda i: (0, i, 0)), strip(inner, out)]
        + [kept, kept, came(0), came(1), last(0), last(1)]
        + [whole(stats.shape)]
        + [strip(rows, own)] * 3
        + [whole(piece.shape) for piece in pieces],
        out_specs=[
            strip(size, inner),
            strip(inner, out),
            strip(rows, own),
            strip(rows, own),
            whole((rank, inner)),
            whole((inner, rank)),
            whole((count, inner)),
            whole((taps, inner)),
            *[whole((1, inner))] * 3,
            whole((SUB, LANES)),
        ],
        out_shape=[
            jax.ShapeDtypeStruct((size, inner), F32),
            jax.ShapeDtypeStruct((inner, out), F32),
            jax.ShapeDtypeStruct((rows, own), BF16),
            jax.ShapeDtypeStruct((rows, own), F32),
            jax.ShapeDtypeStruct((rank, inner), F32),
            jax.ShapeDtypeStruct((inner, rank), F32),
            jax.ShapeDtypeStruct((count, inner), F32),
            jax.ShapeDtypeStruct((taps, inner), F32),
            *[jax.ShapeDtypeStruct((1, inner), F32)] * 3,
            jax.ShapeDtypeStruct((SUB, LANES), F32),
        ],
        scratch_shapes=[pltpu.VMEM((8 * SMALL, inner), F32), pltpu.VMEM((rows, LANES), F32)],
        compiler_params=pltpu.CompilerParams(vmem_limit_bytes=32 * MIB),
        name="finale",
    )(
        place, in_hbm(keep_x), in_hbm(come_x), in_hbm(keep_out), in_hbm(come_out), in_hbm(far_out),
        in_hbm(out_keep), in_hbm(keep), in_hbm(come), in_hbm(come), in_hbm(far), in_hbm(far), stats, in_hbm(slope), in_hbm(shift), in_hbm(base),
        *pieces,
    )


def in_weight_kernel(pins, l0, l1, l2, l3, r0, r1, r2, r3, *rest):
    keep, send = rest[pins:]
    i = pl.program_id(0)
    total = None
    for left, right in ((l0[...], r0), (l1[...], r1), (l2[0], r2), (l3[...], r3)):
        term = mm_tn(left, right[...])
        total = term if total is None else total + term

    @pl.when(i == 0)
    def _():
        send[...] = total.astype(BF16)

    @pl.when(i == 1)
    def _():
        keep[...] = total


def in_weight(lefts, rights, pins):
    rows, inner = rights[0].shape
    own = lefts[0].shape[1] // 2
    whole = lambda value: pl.BlockSpec(value.shape, lambda i: (0,) * value.ndim)
    side = pl.BlockSpec((rows, own), lambda i: (0, 1 - i))
    return pl.pallas_call(
        functools.partial(in_weight_kernel, len(pins)),
        grid=(2,),
        in_specs=[side, side, pl.BlockSpec((1, rows, own), lambda i: (0, 0, 1 - i)), side]
        + [whole(r) for r in rights]
        + [ANY] * len(pins),
        out_specs=[pl.BlockSpec((own, inner), lambda i: (0, 0))] * 2,
        out_shape=[
            pltpu.HBM((own, inner), F32),
            pltpu.HBM((own, inner), BF16),
        ],
        compiler_params=pltpu.CompilerParams(vmem_limit_bytes=20 * MIB),
        name="inw",
    )(in_hbm(lefts[0]), *lefts[1:], in_hbm(rights[0]), *rights[1:], *pins)


def split_bits(axis):
    bits = bits_of(axis)
    return [bit for bit in (2, 1) if bit in bits], [bit for bit in reversed(bits) if bit > 2]


def gather_tokens(value, axis):
    pieces = [value]
    for bit in split_bits(axis)[0]:
        pieces = pieces + [swap(piece, axis, bit) for piece in pieces]
    return pieces


def exchange_cols(value, axis):
    size = lax.axis_size(axis)
    me = lax.axis_index(axis)
    gather, scatter = split_bits(axis)
    rows, cols = value.shape
    outer = 2 ** len(scatter)
    pieces = [value.reshape((rows, outer) + (2,) * len(gather) + (cols // size,))]
    for bit in gather:
        kept, sent = zip(*(halves(piece, 2, (me // bit) % 2) for piece in pieces))
        pieces = list(kept) + [swap(piece, axis, bit) for piece in sent]
    return [piece.reshape(rows, -1) for piece in pieces]


def scatter_sum(value, axis, dim):
    me = lax.axis_index(axis)
    scatter = split_bits(axis)[1]
    for bit in scatter:
        shape = value.shape
        split = shape[:dim] + (2, shape[dim] // 2) + shape[dim + 1 :]
        kept, sent = halves(value.reshape(split), dim, (me // bit) % 2)
        value = kept + swap(sent.astype(BF16), axis, bit).astype(F32)
    return value


def per_device(
    tokens,
    norm_gain,
    w_x,
    w_z,
    conv_weight,
    conv_bias,
    w_down,
    w_up,
    beta_bias,
    w_keyq,
    skip_gain,
    w_out,
    cotangent,
    group_ids,
    group_weights,
):
    rows, width = tokens.shape
    states = w_keyq.shape[1] // 2
    taps = conv_weight.shape[0]
    assert group_ids.shape[0] == 1
    parts = lax.axis_size("state")
    assert parts == 4
    dp_size = lax.axis_size("dp")
    own_width = width // parts
    state_index = lax.axis_index("state")
    place = jnp.stack([lax.axis_index("dp"), state_index]).astype(jnp.int32)
    blocked = dp_size if dp_size == 8 and width % (8 * LANES) == 0 else 0
    keyq_t = w_keyq.T

    normed, upstream_b, pre_x, mixed_b, dsilu, part, *blocks = front(
        place, group_ids, group_weights, tokens, cotangent, norm_gain, w_x,
        conv_weight, conv_bias, w_down, keyq_t, blocked,
    )
    summed = all_but_last(part, "state")
    pins_back = pins_conv = pins_inputs = extra = ()
    if blocked:
        far, near, own, up_far, up_own = blocks
        far = swap(far, "dp", 2)
        near = swap(near, "dp", 1)
        up_far = swap(up_far, "dp", 4)
        pins_back = (far, near, up_far)
    else:
        norm_parts = exchange_cols(normed, "dp")
        up_parts = exchange_cols(upstream_b, "dp")
    silu_z, dgate, grad_y = gate(normed, upstream_b, w_z, w_out)

    gated_b, prez_b, step_size, raw, peak, hist, last = scan_forward(
        summed, mixed_b, w_up, beta_bias, silu_z, dgate, skip_gain, states
    )
    if blocked:
        gated_far = swap(gated_b, "dp", 4)
        prez_far = swap(prez_b, "dp", 2)
        prez_near = swap(prez_b, "dp", 1)

    gmix, pay, ups = scan_backward(
        place, summed, mixed_b, w_up, step_size, raw, grad_y, hist, last, peak, pins_back
    )
    grads = all_but_last(pay, "state")
    if blocked:
        up_parts = (up_own, up_far, swap(up_far, "state", 1))
        (prez_far,) = after((prez_far,), (pay,))
        prez_last = swap(prez_far, "dp", 1)
        sides = (own, far, near, swap(near[1], "dp", 2))
        pins_conv = (gated_far, up_parts[2], prez_near, sides[3])

    prex_b, small, small_send = conv_back(
        place, summed, grads, mixed_b, grad_y, gmix, dsilu, pre_x, ups, conv_weight, skip_gain,
        w_down, keyq_t, dp_size, pins_conv,
    )

    if blocked:
        prex_far = swap(prex_b, "dp", 2)
        prex_near = swap(prex_b, "dp", 1)
        keep_z, send_z = in_weight(
            sides, (prez_b, prez_far, prez_near, prez_last), (in_hbm(prex_b),)
        )
        come_z = swap(send_z, "dp", 4)
        keep_out, later, send_out, half_sent, out_keep, out_far, small, small_send = middle(
            place, gated_b, gated_far, up_parts, w_out, tokens, small,
            swap(small_send, "dp", 1), parts,
            (in_hbm(send_z), prex_far, prex_near),
        )
        prex_last = swap(prex_far, "dp", 1)
        keep_x, send_x = in_weight(
            sides, (prex_b, prex_far, prex_near, prex_last), (in_hbm(send_out), come_z)
        )
        come_x = swap(send_x, "dp", 4)
        come_out = swap(send_out, "dp", 1)
        (small_send,) = after((small_send,), (in_hbm(send_x),))
        small = small + swap(small_send, "dp", 2).astype(F32)
        pins_inputs = (in_hbm(send_x),)
        extra = (keep_z, come_z)
    else:
        half_sent, out_keep, out_far = branch(place, gated_b, w_out, tokens, parts, ())
    send, keep, keep_far, stats, slope, shift, base, *grad_wz = input_grad(
        place, group_ids, group_weights, half_sent, prex_b, prez_b, w_x, w_z, tokens, cotangent,
        norm_gain, parts, extra, pins_inputs,
    )
    if blocked:
        (grad_wz,) = grad_wz
        far_send = (later + come_out[1].astype(F32)).astype(BF16)
        far_out = swap(far_send, "dp", 2)
        small = lax.reduce_precision(small.reshape(-1, small.shape[-1]), 8, 7)
        flipped = jnp.concatenate([small[SMALL:], small[:SMALL]], axis=0).astype(BF16)
        stats, flipped = after((stats, flipped), (in_hbm(come_x), in_hbm(come_out)))
    else:

        def weight_grad(value, left):
            pieces = gather_tokens(value, "dp")
            pairs = zip(pieces, up_parts) if left else zip(norm_parts, pieces)
            return scatter_sum(sum(mm_tn(a, b) for a, b in pairs), "dp", 1 if left else 0)

        grad_wout = weight_grad(gated_b, True)
        grad_wz = weight_grad(prez_b, False)
        grad_wx = weight_grad(prex_b, False)

    come = swap(send, "state", 1)
    pair = [(a + b.astype(F32)).astype(BF16) for a, b in zip((out_far, keep_far), come[1])]
    come_far = swap(jnp.stack(pair), "state", 2)
    stats = all_sum(stats, "state")
    if not blocked:
        block_out = out_keep + come[0, 0].astype(F32) + come_far[0].astype(F32)
        block_out = block_out.astype(BF16)
        norm_grad = keep + come[0, 1].astype(F32) + come_far[1].astype(F32)
        row_stat = stats[: rows // LANES].reshape(rows, 1)
        grad_in = norm_grad * slope - shift * row_stat + base
    gain_rows = own_width // LANES
    gain = lax.dynamic_slice_in_dim(
        stats, rows // LANES + state_index * gain_rows, gain_rows, 0
    )

    count = 2 * states
    rank = w_up.shape[0]
    if blocked:
        gathered = (small + swap(flipped, "dp", 4).astype(F32)).astype(BF16)
        for bit in (4, 1, 2):
            gain = gain + swap(gain, "dp", bit)
        pieces = [gathered]
        for bit, pins in ((1, ()), (2, ())):
            if pins:
                (gathered,) = after((gathered,), pins)
            got = swap(gathered, "dp", bit)
            pieces.append(got)
            gathered = jnp.concatenate([gathered, got], axis=0)
        grad_gain = gain.reshape(-1)
        grad_wx, grad_wout, block_out, grad_in, grad_up, down, keyq, *lines = finale(
            place, keep_x, come_x, keep_out, come_out, far_out, out_keep, keep, come, come_far,
            stats[: rows // LANES], slope, shift, base, pieces, rank, count, taps,
        )
    else:
        small = all_sum(small, "dp")
        grad_up = small[:rank]
        down = small[rank : 2 * rank].T
        keyq = small[2 * rank : 2 * rank + count]
        lines = small[2 * rank + count :]
        top = jnp.max(lines[taps + 3] + lines[taps + 4]).reshape(1, 1)
        lines = (lines[:taps], *[lines[taps + i : taps + i + 1] for i in range(3)], top)
        grad_gain = all_sum(gain, "dp").reshape(-1)
    grad_taps, grad_bias, grad_skip, grad_beta, top = lines
    return (
        block_out,
        grad_in,
        grad_gain,
        grad_wx,
        grad_wz,
        grad_taps,
        grad_bias[0],
        down,
        grad_up,
        grad_beta[0],
        keyq.T,
        grad_skip[0],
        grad_wout,
        top[0, 0],
    )


def solution(mesh):
    placed = (
        P("dp", None),
        P(),
        P(None, "state"),
        P(None, "state"),
        P(None, "state"),
        P("state"),
        P("state", None),
        P(None, "state"),
        P("state"),
        P("state", None),
        P("state"),
        P("state", None),
        P("dp", None),
        P("dp"),
        P(),
    )
    return jax.shard_map(
        per_device,
        mesh=mesh,
        in_specs=placed,
        out_specs=(
            P("dp", "state"),
            P("dp", "state"),
            P("state"),
            P("dp", "state"),
            P("dp", "state"),
            P(None, "state"),
            P("state"),
            P("state", None),
            P(None, "state"),
            P("state"),
            P("state", None),
            P("state"),
            P("state", "dp"),
            P(),
        ),
        check_vma=False,
    )
```
